32 devices in a mesh: groups: 2 (over y), region: 16 (over z, x, core).
Axes of the slice: x: 2, y: 2, z: 4, core: 2. Of those that a mesh axis runs over, the one named last changes fastest.
Arguments:
- point_feats: bfloat16 [32768, 128], P(('groups', 'region')), parts along dimension 0, may hold values from -6 to 6
- point_owner: int32 [32768, 1], P(('groups', 'region')), parts along dimension 0, may hold values from 0 to 15; in each aligned block of 1024 rows (0 to 1023, 1024 to 2047, ...) at most 160 rows name the same one
- point_slot: int32 [32768], P(('groups', 'region')), parts along dimension 0, may hold values from 0 to 2047
- adjacency: int32 [512, 27], P(('groups', 'region')), parts along dimension 0, may hold values from -1 to 255, as said below
- kernel: bfloat16 [27, 128, 128], replicated, may hold values from -0.109375 to 0.109375
- cotangent: bfloat16 [512, 128, 128], P(('groups', 'region')), parts along dimension 0, may hold values from -6 to 6
Outputs:
- out_tiles: bfloat16 [512, 128, 128], P(('groups', 'region')), parts along dimension 0
- grad_points: bfloat16 [32768, 128], P(('groups', 'region')), parts along dimension 0
- grad_weight: float32 [54, 128, 128], P('groups'), parts along dimension 0
The draws below stay inside these ranges and needn't reach their ends.
There are 2 independent parts, one for each index of `groups`. The reference program is written for one: setup_inputs(seed, part) draws one part's arguments, and reference() takes and returns one part's arrays. A program takes and returns all parts, laid end to end along the dimension named above; an argument that names none is the same for every part. Nothing has to cross between parts.
Inputs may be any that keep to these rules, and one draw needn't show every extreme that they name: `point_owner`: no device's points name one owner more than 160 times. `adjacency`: bricks occupy a grid of 32 x 4 x 2 brick positions; the 16 bricks stored on device r (ids r * 16 on) fill the x positions r * 2 to (r + 1) * 2 - 1 in an arbitrary storage order; entry k = 9 (a + 1) + 3 (b + 1) + (c + 1) of brick t is the brick at t's position plus (a, b, c), or -1 where that lies outside the grid.
All inputs are finite; a program needn't handle non-finite values.
Results may differ from the reference program's by a relative error of at most 0.0039.
Values may be sent and summed in bfloat16 or wider, within the bound.
No kernel may reach another device: no remote copies, remote signals or barrier semaphores. Data moves between devices by JAX's collectives and lax.ppermute only.
A program may use at most 128 MiB of HBM per device.

```python
import math
import jax
import jax.numpy as jnp
import numpy as np

C = 128
VX = 4
VY = 4
VZ = 8
VOX = 128
KOFF = 27
GY = 4
GZ = 2
SX = 2
P_DEV = 1024
TILES_DEV = 16
GX = 32
CAP = 160
TILES = 256
POINTS = 16384
N_REGION = 16


def draw_adjacency(key, part):
    key = jax.random.fold_in(key, 11)
    slots = jnp.arange(TILES_DEV, dtype=jnp.int32)
    scores = jax.random.randint(key, (N_REGION, TILES_DEV), 0, 1 << 20) * TILES_DEV + slots[None, :]
    placed = jnp.argsort(scores, axis=1).astype(jnp.int32)
    where_is = jnp.argsort(placed, axis=1).astype(jnp.int32)
    brick = jnp.arange(TILES, dtype=jnp.int32)
    region = brick // TILES_DEV
    position = where_is[region, brick % TILES_DEV]
    layer = position // (GY * GZ)
    across = position // GZ % GY
    height = position % GZ
    column = jnp.arange(KOFF, dtype=jnp.int32)[None, :]
    next_x = (region * SX + layer)[:, None] + column // 9 - 1
    next_y = across[:, None] + column // 3 % 3 - 1
    next_z = height[:, None] + column % 3 - 1
    inside = (next_x >= 0) & (next_x < GX) & (next_y >= 0) & (next_y < GY) & (next_z >= 0) & (next_z < GZ)
    clip_x = jnp.clip(next_x, 0, GX - 1)
    clip_y = jnp.clip(next_y, 0, GY - 1)
    clip_z = jnp.clip(next_z, 0, GZ - 1)
    holder = clip_x // SX
    spot = (clip_x % SX * GY + clip_y) * GZ + clip_z
    neighbour = holder * TILES_DEV + placed[holder, spot]
    return jnp.where(inside, neighbour, -1).astype(jnp.int32)


def with_ends(drawn, key, least, high):
    index_at = [jax.random.randint(jax.random.fold_in(key, axis), (), 0, length) for axis, length in enumerate(drawn.shape)]
    main_axis = drawn.shape.index(max(drawn.shape))
    beside = index_at[:main_axis] + [(index_at[main_axis] + 1) % drawn.shape[main_axis]] + index_at[main_axis + 1:]
    return drawn.at[tuple(index_at)].set(least).at[tuple(beside)].set(high)


def block_scale(own_key, dims, cuts, low, top_value):
    level, own = 1.0, jax.random.fold_in(own_key, 6)
    for axis_at, blocks in cuts:
        steps = jnp.exp(jax.random.uniform(jax.random.fold_in(own, axis_at), (blocks,), jnp.float32, low / len(cuts), top_value / len(cuts)))
        level = level * jnp.repeat(steps, dims[axis_at] // blocks).reshape([-1 if axis == axis_at else 1 for axis in range(len(dims))])
    return level


def assign_block(rng, own, number, rows, count, top, limit, slope):
    order = jax.random.permutation(rng, count)
    heavy_load, usual = load_shares(count, rows * top, limit, slope, True), load_shares(count, rows * top, limit, slope, False)
    places = jnp.arange(count)

    def named(sizes, rotation):
        used = int((sizes > 0).sum())
        fixed = max(1, used // 4)
        moved = fixed + (places - fixed + rotation * (used - fixed)) % max(1, count - fixed)
        return jnp.zeros((count,), jnp.int32).at[order[jnp.where(places < fixed, places, moved)]].set(jnp.asarray(sizes, jnp.int32))

    sizes = jnp.where(number % 4 == 0, named(heavy_load, number // 4), named(usual, number - number // 4 - 1))
    mixed = jax.random.permutation(jax.random.fold_in(own, 3), count)
    source_of, taker = mixed[0:count // 2 * 2:2], mixed[1:count // 2 * 2:2]
    margin = jnp.minimum(sizes[source_of] - 1, limit - sizes[taker]) // 2
    margin = jnp.where((source_of == order[0]) | (taker == order[0]) | (sizes[taker] == 0), 0, jnp.maximum(margin, 0))
    moved = jax.random.randint(jax.random.fold_in(own, 4), (count // 2,), 0, 1 << 20) % (margin + 1)
    sizes = sizes.at[source_of].add(-moved).at[taker].add(moved)
    labels = jnp.searchsorted(jnp.cumsum(sizes), jnp.arange(rows * top), side="right").astype(jnp.int32)
    listing = labels.reshape(top, rows).T
    listing = listing[jax.random.permutation(jax.random.fold_in(own, 1), rows)]
    rotation = jax.random.randint(jax.random.fold_in(own, 2), (rows, 1), 0, top)
    return jnp.take_along_axis(listing, (jnp.arange(top)[None, :] + rotation) % top, axis=1)


def load_shares(amount, total, bound, skew, full):
    loads = [(1 << 20) // math.isqrt(standing ** skew) + 1 for standing in range(1, amount + 1)]
    largest = bound if full else min(bound, max(-(-total // amount), total * loads[0] // sum(loads)))
    least = 1 if total - largest >= amount - 1 else 0
    given, surplus = [largest] + [least] * (amount - 1), total - largest - least * (amount - 1)
    while surplus > 0:
        free = [i for i in range(1, amount) if given[i] < largest] or [i for i in range(1, amount) if given[i] < bound]
        mass, left = sum([loads[i] for i in free]), surplus
        for i in free:
            extra = min(bound - given[i], max(1, left * loads[i] // mass), surplus)
            given[i] = given[i] + extra
            surplus = surplus - extra
    return np.array(given)


def gaussian(rng, dims, spread, limit, cuts=(), kind=jnp.bfloat16):
    level = block_scale(rng, dims, cuts, -0.22, 0.18) if cuts else 1.0
    array = jax.random.normal(rng, dims, jnp.float32) * spread * level
    return jnp.minimum(jnp.maximum(array, -limit), limit).astype(kind)


def setup_inputs(seed: int = 0, part: int = 0) -> dict:
    key_list = jax.random.split(jax.random.key(seed), 7)
    own_keys = jax.random.split(jax.random.fold_in(key_list[6], part), 7)
    point_feats = gaussian(own_keys[0], (POINTS, C), 1.0, 6.0, ((0, 16),))
    point_owner_keys = jax.random.split(jax.random.fold_in(own_keys[1], 1), POINTS // P_DEV)
    point_owner_turns = jax.random.permutation(jax.random.fold_in(own_keys[1], 3), POINTS // P_DEV)
    point_owner = jax.vmap(lambda own, number: assign_block(jax.random.fold_in(own_keys[1], 2), own, number, P_DEV, N_REGION, 1, CAP, 2))(point_owner_keys, point_owner_turns).reshape((POINTS, 1))
    point_slot = with_ends(jax.random.randint(own_keys[2], (POINTS,), 0, TILES_DEV * VOX), jax.random.fold_in(own_keys[2], 1), 0, (TILES_DEV * VOX) - 1).astype(jnp.int32)
    adjacency = draw_adjacency(jax.random.fold_in(jax.random.fold_in(key_list[6], part), 71), part)
    kernel = gaussian(key_list[4], (KOFF, C, C), (KOFF * C) ** -0.5, 0.109375)
    cotangent = gaussian(own_keys[5], (TILES, VOX, C), 1.0, 6.0, ((0, 16),))
    return {"point_feats": point_feats, "point_owner": point_owner, "point_slot": point_slot, "adjacency": adjacency, "kernel": kernel, "cotangent": cotangent}


def ranges(offset, length):
    if offset == 0:
        return slice(length - 1, length)
    if offset == 2:
        return slice(0, 1)
    return slice(0, length)

def assemble(storage, indices):
    size_x, size_y, size_z = (storage.shape[1], storage.shape[2], storage.shape[3])
    layers = []
    for offset_x in range(3):
        strips = []
        for offset_y in range(3):
            pieces = []
            for offset_z in range(3):
                column = (offset_x * 3 + offset_y) * 3 + offset_z
                source = storage[:, ranges(offset_x, size_x), ranges(offset_y, size_y), ranges(offset_z, size_z)]
                pieces.append(jnp.take(source, indices[:, column], axis=0))
            strips.append(jnp.concatenate(pieces, axis=3))
        layers.append(jnp.concatenate(strips, axis=2))
    return jnp.concatenate(layers, axis=1)

def window(padded, offset):
    size_x, size_y, size_z = (padded.shape[1] - 2, padded.shape[2] - 2, padded.shape[3] - 2)
    start_x, start_y, start_z = (offset // 9, offset // 3 % 3, offset % 3)
    piece = padded[:, start_x:start_x + size_x, start_y:start_y + size_y, start_z:start_z + size_z]
    return piece.reshape(-1, padded.shape[4])

def reference(point_feats, point_owner, point_slot, adjacency, kernel, cotangent):
    vox_dev = TILES_DEV * VOX
    total = TILES * VOX
    voxel_id = (point_owner[:, 0] * vox_dev + point_slot).astype(jnp.int32)
    sums = jax.ops.segment_sum(point_feats.astype(jnp.float32), voxel_id, num_segments=total)
    count = jax.ops.segment_sum(jnp.ones((POINTS,), jnp.float32), voxel_id, num_segments=total)
    denom = jnp.maximum(count, 1.0)
    voxel_feats = (sums / denom[:, None]).astype(jnp.bfloat16)
    indices = jnp.where(adjacency >= 0, adjacency, TILES).astype(jnp.int32)
    blank = jnp.zeros((1, VX, VY, VZ, C), jnp.bfloat16)
    padded = assemble(jnp.concatenate([voxel_feats.reshape(TILES, VX, VY, VZ, C), blank], axis=0), indices)
    padded_cot = assemble(jnp.concatenate([cotangent.reshape(TILES, VX, VY, VZ, C), blank], axis=0), indices)
    flat_cot = cotangent.reshape(total, C)
    output = jnp.zeros((total, C), jnp.float32)
    grad_x = jnp.zeros((total, C), jnp.float32)
    weight_terms = []
    for offset in range(KOFF):
        gathered = window(padded, offset)
        output = output + jnp.dot(gathered, kernel[offset], preferred_element_type=jnp.float32)
        weight_terms.append(jnp.dot(gathered.T, flat_cot, preferred_element_type=jnp.float32))
        mirrored = window(padded_cot, KOFF - 1 - offset)
        grad_x = grad_x + jnp.dot(mirrored, kernel[offset].T, preferred_element_type=jnp.float32)
    grad_weight = jnp.stack(weight_terms) * (1.0 / math.sqrt(TILES * VOX))
    voxel_grad = (grad_x / denom[:, None]).astype(jnp.bfloat16)
    grad_points = voxel_grad[voxel_id]
    return (output.astype(jnp.bfloat16).reshape(TILES, VOX, C), grad_points, grad_weight)
```

```python
import functools
import math

import jax
import jax.numpy as jnp
from jax import lax
from jax.experimental import pallas as pl
from jax.experimental.pallas import tpu as pltpu
from jax.sharding import PartitionSpec as P

VX = 4
VY = 4
VZ = 8
GY = 4
GZ = 2
SX = 2
KOFF = 27
NY = GY * VY
NZ = GZ * VZ
NX = SX * VX
SLAB = NY * NZ
DENSE = NX * SLAB
LANES = 128
BF = jnp.bfloat16
F32 = jnp.float32
VMEM = pl.BlockSpec(memory_space=pltpu.VMEM)
SMEM = pl.BlockSpec(memory_space=pltpu.SMEM)
PARAMS = pltpu.CompilerParams(vmem_limit_bytes=48 * 1024 * 1024)


def up_to(value, unit):
    return (value + unit - 1) // unit * unit


def iota(shape, dim, dtype=jnp.int32):
    return lax.broadcasted_iota(jnp.int32, shape, dim).astype(dtype)


def call(body, outs, args, smem=(), scratch=(), flops=0):
    moved = sum(math.prod(o.shape) * o.dtype.itemsize for o in outs)
    moved += sum(math.prod(a.shape) * a.dtype.itemsize for a in args)
    return pl.pallas_call(
        body,
        out_shape=outs,
        in_specs=[SMEM if i in smem else VMEM for i in range(len(args))],
        out_specs=[VMEM] * len(outs),
        scratch_shapes=list(scratch),
        compiler_params=PARAMS,
        cost_estimate=pl.CostEstimate(flops=flops, bytes_accessed=moved, transcendentals=0),
    )(*args)


def corner(adj_ref, t, lowest):
    tiles = adj_ref.shape[0]
    left = adj_ref[t, 4]
    layer = jnp.where((left >= lowest) & (left < lowest + tiles), 1, 0)
    before = adj_ref[t, 10]
    second = adj_ref[jnp.clip(before - lowest, 0, tiles - 1), 10] < 0
    inner = jnp.where(second, 1, 2)
    across = jnp.where(before < 0, 0, jnp.where(adj_ref[t, 16] < 0, GY - 1, inner))
    height = jnp.where(adj_ref[t, 12] >= 0, 1, 0)
    return layer * VX, across * VY, height * VZ


def pack_body(cap_rows, owner_ref, slot_ref, feats_ref, msg_ref, place_ref, table_ref):
    regions = msg_ref.shape[0]
    points = feats_ref.shape[0]
    segs = up_to(cap_rows, LANES) // LANES
    owner = owner_ref[...]
    slot = slot_ref[...]
    mine = iota((regions, points), 0) == owner
    marks = jnp.where(mine, 1.0, 0.0)
    marks_bf = marks.astype(BF)
    earlier = jnp.where(iota((LANES, LANES), 0) < iota((LANES, LANES), 1), 1.0, 0.0).astype(BF)
    carry = jnp.zeros((regions, 1), F32)
    ranks = []
    for start in range(0, points, LANES):
        seg = marks[:, start : start + LANES]
        pre = jnp.dot(marks_bf[:, start : start + LANES], earlier, preferred_element_type=F32)
        ranks.append(jnp.sum((pre + carry) * seg, axis=0, keepdims=True))
        carry = carry + jnp.sum(seg, axis=1, keepdims=True)
    rank = jnp.concatenate(ranks, axis=1).astype(jnp.int32)
    place = owner * cap_rows + rank
    place_ref[...] = jnp.broadcast_to(place, (8, points)).astype(F32)
    block = jnp.broadcast_to((place >> 7).astype(F32), (LANES, points)).astype(BF)
    within = jnp.broadcast_to((place & (LANES - 1)).astype(F32), (LANES, points)).astype(BF)
    row = iota((LANES, points), 0, F32).astype(BF)
    one = jnp.where(row == within, jnp.ones_like(row), jnp.zeros_like(row))
    feats = feats_ref[...]
    chunk = math.lcm(cap_rows, LANES)
    for start in range(0, regions * cap_rows, chunk):
        picks = [
            jnp.where(block == jnp.asarray(q, BF), one, jnp.zeros_like(one))
            for q in range(start // LANES, (start + chunk) // LANES)
        ]
        picker = jnp.concatenate(picks, axis=0)
        rows = jnp.dot(picker, feats, preferred_element_type=F32).astype(BF)
        for i in range(chunk // cap_rows):
            msg_ref[start // cap_rows + i, 0:cap_rows, :] = rows[i * cap_rows : (i + 1) * cap_rows]
    high = jnp.where(mine, (slot >> 7) + 1, 0).astype(F32)
    low = jnp.where(mine, slot & (LANES - 1), 0).astype(F32)
    values = jnp.concatenate([high, low], axis=0).astype(BF)
    by_rank = jnp.where(iota((segs * LANES, points), 0) == rank, 1.0, 0.0).astype(BF)
    table_ref[...] = lax.dot_general(
        values, by_rank, (((1,), (1,)), ((), ())), preferred_element_type=F32
    )
    line = iota((16, LANES), 0)
    for o in range(regions):
        tile = jnp.zeros((16, LANES), F32)
        for s in range(segs):
            lanes = slice(s * LANES, (s + 1) * LANES)
            tile = jnp.where(line == s, table_ref[o : o + 1, lanes], tile)
            tile = jnp.where(line == segs + s, table_ref[regions + o : regions + o + 1, lanes], tile)
        msg_ref[o, cap_rows : cap_rows + 16, :] = tile.astype(BF)


def pack(owner, slot, feats, regions, cap_rows):
    points, channels = feats.shape
    segs = up_to(cap_rows, LANES) // LANES
    return call(
        functools.partial(pack_body, cap_rows),
        [
            jax.ShapeDtypeStruct((regions, cap_rows + 16, channels), BF),
            jax.ShapeDtypeStruct((8, points), F32),
        ],
        [owner, slot, feats],
        scratch=[pltpu.VMEM((2 * regions, segs * LANES), F32)],
        flops=2 * regions * cap_rows * points * channels,
    )


def dense_body(adj_ref, bricks_ref, dense_ref, low_ref, high_ref, grid_ref):
    tiles, vox, channels = bricks_ref.shape
    lowest = lax.axis_index("region") * tiles
    for t in range(tiles):
        x, y, z = corner(adj_ref, t, lowest)
        brick = bricks_ref[t].astype(F32).reshape(VX, VY, VZ, channels)
        grid_ref[pl.ds(x, VX), pl.ds(y, VY), pl.ds(pl.multiple_of(z, VZ), VZ), :] = brick
    for x in range(NX):
        slab = grid_ref[x].reshape(SLAB, channels).astype(BF)
        dense_ref[x] = slab
        if x == 0:
            low_ref[...] = slab
        if x == NX - 1:
            high_ref[...] = slab


def to_dense(adjacency, bricks):
    channels = bricks.shape[2]
    face = jax.ShapeDtypeStruct((SLAB, channels), BF)
    return call(
        dense_body,
        [jax.ShapeDtypeStruct((NX, SLAB, channels), BF), face, face],
        [adjacency, bricks],
        smem=(0,),
        scratch=[pltpu.VMEM((NX, NY, NZ, channels), F32)],
    )


def fill_shifts(shift_ref, dense_ref, low_ref, high_ref):
    channels = dense_ref.shape[2]
    border = jnp.zeros((NZ, channels), BF)
    height = iota((SLAB, channels), 0) % NZ
    for x in range(NX + 2):
        if x == 0:
            slab = low_ref[...]
        elif x == NX + 1:
            slab = high_ref[...]
        else:
            slab = dense_ref[x - 1]
        wide = slab.astype(F32)
        lower = jnp.where(height == 0, 0.0, pltpu.roll(wide, 1, 0))
        upper = jnp.where(height == NZ - 1, 0.0, pltpu.roll(wide, SLAB - 1, 0))
        for c, copy in enumerate((lower.astype(BF), slab, upper.astype(BF))):
            shift_ref[c, x, 0:NZ, :] = border
            shift_ref[c, x, NZ : NZ + SLAB, :] = copy
            shift_ref[c, x, NZ + SLAB : NZ + SLAB + NZ, :] = border


def conv_slab(shift_ref, weights_ref, x):
    pieces = []
    for k in range(KOFF):
        a, b, c = k // 9, k // 3 % 3, k % 3
        pieces.append(shift_ref[c, x + a, b * NZ : b * NZ + SLAB, :])
    return jnp.dot(
        jnp.concatenate(pieces, axis=1), weights_ref[...], preferred_element_type=F32
    )


SHIFTS = (3, NX + 2, SLAB + 2 * NZ)


def gradient_body(dense_ref, low_ref, high_ref, weights_ref, grad_ref, shift_ref):
    fill_shifts(shift_ref, dense_ref, low_ref, high_ref)

    def step(x, carry):
        grad_ref[x] = conv_slab(shift_ref, weights_ref, x)
        return carry

    lax.fori_loop(0, NX, step, 0)


def gradient(dense, low, high, weights):
    channels = dense.shape[2]
    return call(
        gradient_body,
        [
            jax.ShapeDtypeStruct((NX, SLAB, channels), F32),
            jax.ShapeDtypeStruct(SHIFTS + (channels,), BF),
        ],
        [dense, low, high, weights],
        flops=2 * DENSE * KOFF * channels * channels,
    )


def forward_body(adj_ref, dense_ref, low_ref, high_ref, weights_ref, out_ref, shift_ref, grid_ref):
    tiles, vox, channels = out_ref.shape
    lowest = lax.axis_index("region") * tiles
    fill_shifts(shift_ref, dense_ref, low_ref, high_ref)

    def step(x, carry):
        grid_ref[x] = conv_slab(shift_ref, weights_ref, x).reshape(NY, NZ, channels)
        return carry

    lax.fori_loop(0, NX, step, 0)
    for t in range(tiles):
        x, y, z = corner(adj_ref, t, lowest)
        brick = grid_ref[pl.ds(x, VX), pl.ds(y, VY), pl.ds(pl.multiple_of(z, VZ), VZ), :]
        out_ref[t] = brick.reshape(vox, channels).astype(BF)


def forward(adjacency, dense, low, high, weights, tiles):
    channels = dense.shape[2]
    return call(
        forward_body,
        [jax.ShapeDtypeStruct((tiles, VX * VY * VZ, channels), BF)],
        [adjacency, dense, low, high, weights],
        smem=(0,),
        scratch=[
            pltpu.VMEM(SHIFTS + (channels,), BF),
            pltpu.VMEM((NX, NY, NZ, channels), F32),
        ],
        flops=2 * DENSE * KOFF * channels * channels,
    )[0]


def voxel_body(
    cap_rows, adj_ref, msg_ref, grad_ref, turned_ref, dense_ref, low_ref, high_ref, back_ref,
    table_ref, feats_ref, pick_ref,
):
    regions, rows, channels = msg_ref.shape
    tiles = adj_ref.shape[0]
    segs = up_to(cap_rows, LANES) // LANES
    lowest = lax.axis_index("region") * tiles
    for r in range(regions):
        feats_ref[r * cap_rows : (r + 1) * cap_rows, :] = msg_ref[r, 0:cap_rows, :]
        tile = msg_ref[r, cap_rows : cap_rows + 16, :].astype(F32)
        for s in range(segs):
            lanes = slice(s * LANES, (s + 1) * LANES)
            table_ref[r : r + 1, lanes] = tile[s : s + 1]
            table_ref[regions + r : regions + r + 1, lanes] = tile[segs + s : segs + s + 1]
    high = table_ref[0:regions, :].astype(jnp.int32)
    low = table_ref[regions : 2 * regions, :].astype(jnp.int32)
    start = jnp.full(high.shape, -DENSE, jnp.int32)
    for t in range(tiles):
        x, y, z = corner(adj_ref, t, lowest)
        start = jnp.where(high == t + 1, (x * NY + y) * NZ + z, start)
    inside = ((low >> 5) * NY + ((low >> 3) & 3)) * NZ + (low & 7)
    spot = jnp.where(start < 0, -LANES, start + inside)
    blocks = (spot >> 7).astype(F32)
    withins = (spot & (LANES - 1)).astype(F32)
    turned = jnp.transpose(jnp.concatenate([blocks, withins], axis=0))
    lane = iota((cap_rows, LANES), 1, F32).astype(BF)
    for r in range(regions):
        block = jnp.broadcast_to(turned[0:cap_rows, r : r + 1], (cap_rows, LANES)).astype(BF)
        within = jnp.broadcast_to(
            turned[0:cap_rows, regions + r : regions + r + 1], (cap_rows, LANES)
        ).astype(BF)
        one = jnp.where(lane == within, jnp.ones_like(lane), jnp.zeros_like(lane))
        for q in range(DENSE // LANES):
            pick_ref[r * cap_rows : (r + 1) * cap_rows, q * LANES : (q + 1) * LANES] = jnp.where(
                block == jnp.asarray(q, BF), one, jnp.zeros_like(one)
            )
    total = regions * cap_rows
    flipped = jnp.transpose(feats_ref[...].astype(F32)).astype(BF)
    left = jnp.concatenate([flipped, jnp.ones((16, total), BF)], axis=0)
    width = 2 * LANES
    for q in range(0, DENSE, width):
        part = jnp.dot(left, pick_ref[:, q : q + width], preferred_element_type=F32)
        denom = jnp.maximum(part[channels : channels + 8], 1.0)
        mean = part[0:channels] / denom[0:1]
        turned_ref[:, q : q + width] = mean.astype(BF)
        upright = jnp.transpose(mean).astype(BF)
        dense_ref[q // SLAB, q % SLAB : q % SLAB + width, :] = upright
        if q == 0:
            low_ref[...] = upright
        if q == DENSE - width:
            high_ref[...] = upright
        column = jnp.transpose(denom)[:, 0:1]
        grad_ref[q // SLAB, q % SLAB : q % SLAB + width, :] = (
            grad_ref[q // SLAB, q % SLAB : q % SLAB + width, :] / column
        )
    voxel_grad = grad_ref[...].reshape(DENSE, channels).astype(BF)
    chunk = total // 4
    for start in range(0, total, chunk):
        picked = jnp.dot(
            pick_ref[start : start + chunk, :], voxel_grad, preferred_element_type=F32
        )
        for r in range(start // cap_rows, (start + chunk) // cap_rows):
            back_ref[r] = picked[r * cap_rows - start : (r + 1) * cap_rows - start].astype(BF)


def voxels(adjacency, msg, grad, cap_rows):
    regions, rows, channels = msg.shape
    segs = up_to(cap_rows, LANES) // LANES
    face = jax.ShapeDtypeStruct((SLAB, channels), BF)
    total = regions * cap_rows
    return call(
        functools.partial(voxel_body, cap_rows),
        [
            jax.ShapeDtypeStruct((channels, DENSE), BF),
            jax.ShapeDtypeStruct((NX, SLAB, channels), BF),
            face,
            face,
            jax.ShapeDtypeStruct((regions, cap_rows, channels), BF),
        ],
        [adjacency, msg, grad],
        smem=(0,),
        scratch=[
            pltpu.VMEM((2 * regions, segs * LANES), F32),
            pltpu.VMEM((total, channels), BF),
            pltpu.VMEM((total, DENSE), BF),
        ],
        flops=4 * total * DENSE * channels,
    )


def weight_body(scaling, turned_ref, shift_ref, keep_ref, send_ref, all_ref):
    channels = turned_ref.shape[0]
    half = keep_ref.shape[0]
    core = lax.rem(lax.axis_index("region"), 2)
    left = turned_ref[...]
    for k in range(0, KOFF, 2):
        pieces = []
        for j in range(k, min(k + 2, KOFF)):
            a, b, c = j // 9, j // 3 % 3, j % 3
            window = shift_ref[c, a : a + NX, b * NZ : b * NZ + SLAB, :]
            pieces.append(window.reshape(DENSE, channels))
        right = jnp.concatenate(pieces, axis=1)
        term = jnp.dot(left, right, preferred_element_type=F32) * scaling
        for i in range(len(pieces)):
            at = (KOFF - 1 - k - i) * channels
            all_ref[at : at + channels, :] = term[:, i * channels : (i + 1) * channels]
    keep_ref[...] = all_ref[pl.ds(pl.multiple_of(core * half, 8), half), :]
    send_ref[...] = all_ref[pl.ds(pl.multiple_of((1 - core) * half, 8), half), :]


def weight_terms(turned, shifts, scaling):
    channels = turned.shape[0]
    half = jax.ShapeDtypeStruct((KOFF * channels // 2, channels), F32)
    return call(
        functools.partial(weight_body, scaling),
        [half, half],
        [turned, shifts],
        scratch=[pltpu.VMEM((KOFF * channels, channels), F32)],
        flops=2 * DENSE * KOFF * channels * channels,
    )


def unpack_body(place_ref, rows_ref, out_ref):
    regions, cap_rows, channels = rows_ref.shape
    points = out_ref.shape[0]
    total = regions * cap_rows
    place = jnp.transpose(place_ref[...])[:, 0:1].astype(jnp.int32)
    block = jnp.broadcast_to((place >> 7).astype(F32), (points, LANES)).astype(BF)
    within = jnp.broadcast_to((place & (LANES - 1)).astype(F32), (points, LANES)).astype(BF)
    lane = iota((points, LANES), 1, F32).astype(BF)
    one = jnp.where(lane == within, jnp.ones_like(lane), jnp.zeros_like(lane))
    rows = rows_ref[...].reshape(total, channels)
    chunk = 256
    for start in range(0, points, chunk):
        keep = slice(start, start + chunk)
        picks = [
            jnp.where(block[keep] == jnp.asarray(q, BF), one[keep], jnp.zeros_like(one[keep]))
            for q in range(total // LANES)
        ]
        picker = jnp.concatenate(picks, axis=1)
        out_ref[keep, :] = jnp.dot(picker, rows, preferred_element_type=F32).astype(BF)


def unpack(place, rows, points):
    regions, cap_rows, channels = rows.shape
    return call(
        unpack_body,
        [jax.ShapeDtypeStruct((points, channels), BF)],
        [place, rows],
        flops=2 * regions * cap_rows * points * channels,
    )[0]


def from_sides(low, high):
    count = lax.axis_size("region")
    up = [(i, i + 1) for i in range(count - 1)]
    down = [(j, i) for i, j in up]
    return lax.ppermute(high, "region", up), lax.ppermute(low, "region", down)


def swapped(array, bit):
    count = lax.axis_size("region")
    return lax.ppermute(array, "region", [(i, i ^ bit) for i in range(count)])


def total_over_region(keep, send):
    count = lax.axis_size("region")
    me = lax.axis_index("region")
    term = keep + swapped(send, 1)
    bit = 2
    while bit < count:
        half = term.shape[0] // 2
        side = (me // bit) % 2
        sent = lax.dynamic_slice_in_dim(term, (1 - side) * half, half).astype(BF)
        kept = lax.dynamic_slice_in_dim(term, side * half, half)
        term = kept + swapped(sent, bit).astype(F32)
        bit *= 2
    term = term.astype(BF)
    while bit > 1:
        bit //= 2
        other = swapped(term, bit)
        side = (me // bit) % 2
        term = jnp.where(
            side == 0,
            jnp.concatenate([term, other], axis=0),
            jnp.concatenate([other, term], axis=0),
        )
    return term.astype(F32)


def exchange(array):
    return lax.all_to_all(array, "region", split_axis=0, concat_axis=0, tiled=True)


def local(point_feats, point_owner, point_slot, adjacency, kernel, cotangent):
    regions = lax.axis_size("region")
    points, channels = point_feats.shape
    tiles, vox = cotangent.shape[0], cotangent.shape[1]
    capacity = (5 * points + 2 * regions - 1) // (2 * regions)
    cap_rows = up_to(capacity, 16)
    msg, place = pack(
        point_owner.reshape(1, points), point_slot.reshape(1, points), point_feats, regions, cap_rows
    )
    received = exchange(msg)
    cot, cot_low, cot_high = to_dense(adjacency, cotangent)
    below, above = from_sides(cot_low, cot_high)
    mirrored = jnp.transpose(kernel[::-1], (0, 2, 1)).reshape(KOFF * channels, channels)
    grad, shifts = gradient(cot, below, above, mirrored)
    turned, feats, low, high, back = voxels(adjacency, received, grad, cap_rows)
    scaling = 1.0 / math.sqrt(tiles * regions * vox)
    keep, send = weight_terms(turned, shifts, scaling)
    grad_weight = total_over_region(keep, send).reshape(KOFF, channels, channels)
    feats_below, feats_above = from_sides(low, high)
    weights = kernel.reshape(KOFF * channels, channels)
    out_tiles = forward(adjacency, feats, feats_below, feats_above, weights, tiles)
    grad_points = unpack(place, exchange(back), points)
    return out_tiles, grad_points, grad_weight


def solution(mesh):
    placed = (
        P(("groups", "region"), None),
        P(("groups", "region"), None),
        P(("groups", "region")),
        P(("groups", "region"), None),
        P(),
        P(("groups", "region"), None, None),
    )
    return jax.shard_map(
        local,
        mesh=mesh,
        in_specs=placed,
        out_specs=(
            P(("groups", "region"), None, None),
            P(("groups", "region"), None),
            P("groups", None, None),
        ),
        check_vma=False,
    )
```

```python
import functools
import math

import jax
import jax.numpy as jnp
from jax import lax
from jax.experimental import pallas as pl
from jax.experimental.pallas import tpu as pltpu
from jax.sharding import PartitionSpec as P

VX = 4
VY = 4
VZ = 8
GY = 4
GZ = 2
SX = 2
KOFF = 27
NY = GY * VY
NZ = GZ * VZ
NX = SX * VX
SLAB = NY * NZ
DENSE = NX * SLAB
LANES = 128
BF = jnp.bfloat16
F32 = jnp.float32
VMEM = pl.BlockSpec(memory_space=pltpu.VMEM)
SMEM = pl.BlockSpec(memory_space=pltpu.SMEM)
FAR = pl.BlockSpec(memory_space=pltpu.HBM)
MIB = 1024 * 1024


def up_to(value, unit):
    return (value + unit - 1) // unit * unit


def iota(shape, dim, dtype=jnp.int32):
    return lax.broadcasted_iota(jnp.int32, shape, dim).astype(dtype)


def call(body, outs, args, smem=(), far=(), far_outs=(), scratch=(), flops=0, limit=16):
    moved = sum(math.prod(o.shape) * o.dtype.itemsize for o in outs)
    moved += sum(math.prod(a.shape) * a.dtype.itemsize for a in args)
    return pl.pallas_call(
        body,
        out_shape=outs,
        in_specs=[SMEM if i in smem else FAR if i in far else VMEM for i in range(len(args))],
        out_specs=[FAR if i in far_outs else VMEM for i in range(len(outs))],
        scratch_shapes=list(scratch),
        compiler_params=pltpu.CompilerParams(vmem_limit_bytes=limit * MIB),
        cost_estimate=pl.CostEstimate(flops=flops, bytes_accessed=moved, transcendentals=0),
    )(*args)


def corner(adj_ref, t, lowest):
    tiles = adj_ref.shape[0]
    left = adj_ref[t, 4]
    layer = jnp.where((left >= lowest) & (left < lowest + tiles), 1, 0)
    before = adj_ref[t, 10]
    second = adj_ref[jnp.clip(before - lowest, 0, tiles - 1), 10] < 0
    inner = jnp.where(second, 1, 2)
    across = jnp.where(before < 0, 0, jnp.where(adj_ref[t, 16] < 0, GY - 1, inner))
    height = jnp.where(adj_ref[t, 12] >= 0, 1, 0)
    return layer * VX, across * VY, height * VZ


def pack_body(
    cap_rows, owner_far, slot_far, feats_far, msg_ref, place_ref, table_ref, owner_ref, slot_ref, feats_ref, sems
):
    regions = msg_ref.shape[0]
    points = feats_ref.shape[0]
    pairs = ((owner_far, owner_ref), (slot_far, slot_ref), (feats_far, feats_ref))
    copies = [pltpu.make_async_copy(a, b, sems.at[i]) for i, (a, b) in enumerate(pairs)]
    for copy in copies:
        copy.start()
    copies[0].wait()
    copies[1].wait()
    segs = up_to(cap_rows, LANES) // LANES
    owner = owner_ref[...]
    slot = slot_ref[...]
    mine = iota((regions, points), 0) == owner
    marks = jnp.where(mine, 1.0, 0.0)
    marks_bf = marks.astype(BF)
    earlier = jnp.where(iota((LANES, LANES), 0) < iota((LANES, LANES), 1), 1.0, 0.0).astype(BF)
    carry = jnp.zeros((regions, 1), F32)
    ranks = []
    for start in range(0, points, LANES):
        seg = marks[:, start : start + LANES]
        pre = jnp.dot(marks_bf[:, start : start + LANES], earlier, preferred_element_type=F32)
        ranks.append(jnp.sum((pre + carry) * seg, axis=0, keepdims=True))
        carry = carry + jnp.sum(seg, axis=1, keepdims=True)
    rank = jnp.concatenate(ranks, axis=1).astype(jnp.int32)
    place = owner * cap_rows + rank
    place_ref[...] = jnp.broadcast_to(place, (8, points)).astype(F32)
    block = jnp.broadcast_to((place >> 7).astype(F32), (LANES, points)).astype(BF)
    within = jnp.broadcast_to((place & (LANES - 1)).astype(F32), (LANES, points)).astype(BF)
    row = iota((LANES, points), 0, F32).astype(BF)
    one = jnp.where(row == within, jnp.ones_like(row), jnp.zeros_like(row))
    copies[2].wait()
    feats = feats_ref[...]
    chunk = math.lcm(cap_rows, LANES)
    for start in range(0, regions * cap_rows, chunk):
        picks = [
            jnp.where(block == jnp.asarray(q, BF), one, jnp.zeros_like(one))
            for q in range(start // LANES, (start + chunk) // LANES)
        ]
        picker = jnp.concatenate(picks, axis=0)
        rows = jnp.dot(picker, feats, preferred_element_type=F32).astype(BF)
        for i in range(chunk // cap_rows):
            msg_ref[start // cap_rows + i, 0:cap_rows, :] = rows[i * cap_rows : (i + 1) * cap_rows]
    high = jnp.where(mine, (slot >> 7) + 1, 0).astype(F32)
    low = jnp.where(mine, slot & (LANES - 1), 0).astype(F32)
    values = jnp.concatenate([high, low], axis=0).astype(BF)
    by_rank = jnp.where(iota((segs * LANES, points), 0) == rank, 1.0, 0.0).astype(BF)
    table_ref[...] = lax.dot_general(
        values, by_rank, (((1,), (1,)), ((), ())), preferred_element_type=F32
    )
    line = iota((16, LANES), 0)
    for o in range(regions):
        tile = jnp.zeros((16, LANES), F32)
        for s in range(segs):
            lanes = slice(s * LANES, (s + 1) * LANES)
            tile = jnp.where(line == s, table_ref[o : o + 1, lanes], tile)
            tile = jnp.where(line == segs + s, table_ref[regions + o : regions + o + 1, lanes], tile)
        msg_ref[o, cap_rows : cap_rows + 16, :] = tile.astype(BF)


def pack(owner, slot, feats, regions, cap_rows):
    points, channels = feats.shape
    segs = up_to(cap_rows, LANES) // LANES
    return call(
        functools.partial(pack_body, cap_rows),
        [
            jax.ShapeDtypeStruct((regions, cap_rows + 16, channels), BF),
            jax.ShapeDtypeStruct((8, points), F32),
        ],
        [owner, slot, feats],
        far=(0, 1, 2),
        scratch=[
            pltpu.VMEM((2 * regions, segs * LANES), F32),
            pltpu.VMEM((1, points), jnp.int32),
            pltpu.VMEM((1, points), jnp.int32),
            pltpu.VMEM((points, channels), BF),
            pltpu.SemaphoreType.DMA((3,)),
        ],
        limit=60,
        flops=2 * regions * cap_rows * points * channels,
    )


def dense_body(adj_ref, bricks_ref, dense_ref, low_ref, high_ref, grid_ref):
    tiles, vox, channels = bricks_ref.shape
    lowest = lax.axis_index("region") * tiles
    for t in range(tiles):
        x, y, z = corner(adj_ref, t, lowest)
        brick = bricks_ref[t].astype(F32).reshape(VX, VY, VZ, channels)
        grid_ref[pl.ds(x, VX), pl.ds(y, VY), pl.ds(pl.multiple_of(z, VZ), VZ), :] = brick
    for x in range(NX):
        slab = grid_ref[x].reshape(SLAB, channels).astype(BF)
        dense_ref[x] = slab
        if x == 0:
            low_ref[...] = slab
        if x == NX - 1:
            high_ref[...] = slab


def to_dense(adjacency, bricks):
    channels = bricks.shape[2]
    face = jax.ShapeDtypeStruct((SLAB, channels), BF)
    return call(
        dense_body,
        [jax.ShapeDtypeStruct((NX, SLAB, channels), BF), face, face],
        [adjacency, bricks],
        smem=(0,),
        scratch=[pltpu.VMEM((NX, NY, NZ, channels), F32)],
    )


SHIFTED = SLAB + 2 * NZ
INNER = NX - 2


def put_shifts(shift_ref, x, slab):
    border = jnp.zeros((NZ, slab.shape[1]), BF)
    height = iota(slab.shape, 0) % NZ
    wide = slab.astype(F32)
    lower = jnp.where(height == 0, 0.0, pltpu.roll(wide, 1, 0))
    upper = jnp.where(height == NZ - 1, 0.0, pltpu.roll(wide, SLAB - 1, 0))
    for c, copy in enumerate((lower.astype(BF), slab, upper.astype(BF))):
        shift_ref[c, x, 0:NZ, :] = border
        shift_ref[c, x, NZ : NZ + SLAB, :] = copy
        shift_ref[c, x, NZ + SLAB : SHIFTED, :] = border


def conv_slab(shift_ref, weights_ref, x):
    pieces = []
    for k in range(KOFF):
        a, b, c = k // 9, k // 3 % 3, k % 3
        pieces.append(shift_ref[c, x + a, b * NZ : b * NZ + SLAB, :])
    return jnp.dot(
        jnp.concatenate(pieces, axis=1), weights_ref[...], preferred_element_type=F32
    )


def conv_inner(shift_ref, weights_ref, store):
    def step(x, carry):
        store(x, conv_slab(shift_ref, weights_ref, x))
        return carry

    lax.fori_loop(0, INNER, step, 0)


def conv_edges(shift_ref, weights_ref, slabs):
    for i, slab in enumerate(slabs):
        put_shifts(shift_ref, i, slab)
    return conv_slab(shift_ref, weights_ref, 0), conv_slab(shift_ref, weights_ref, 3)


def inner_gradient_body(dense_ref, weights_ref, grad_far, shift_far, grad_ref, shift_ref, sems):
    for x in range(NX):
        put_shifts(shift_ref, x, dense_ref[x])
    shift_out = pltpu.make_async_copy(shift_ref, shift_far, sems.at[0])
    shift_out.start()

    def store(x, value):
        grad_ref[x] = value

    conv_inner(shift_ref, weights_ref, store)
    grad_out = pltpu.make_async_copy(grad_ref, grad_far, sems.at[1])
    grad_out.start()
    shift_out.wait()
    grad_out.wait()


def inner_gradient(dense, weights):
    channels = dense.shape[2]
    grads, shifts = (INNER, SLAB, channels), (3, NX, SHIFTED, channels)
    return call(
        inner_gradient_body,
        [jax.ShapeDtypeStruct(grads, F32), jax.ShapeDtypeStruct(shifts, BF)],
        [dense, weights],
        far_outs=(0, 1),
        scratch=[
            pltpu.VMEM(grads, F32),
            pltpu.VMEM(shifts, BF),
            pltpu.SemaphoreType.DMA((2,)),
        ],
        flops=2 * INNER * SLAB * KOFF * channels * channels,
        limit=60,
    )


def edge_gradient_body(dense_ref, low_ref, high_ref, weights_ref, grad_ref, edge_ref, shift_ref):
    slabs = [low_ref[...]] + [dense_ref[x] for x in (0, 1, NX - 2, NX - 1)] + [high_ref[...]]
    first, last = conv_edges(shift_ref, weights_ref, slabs)
    grad_ref[0] = first
    grad_ref[1] = last
    edge_ref[0] = shift_ref[:, 0]
    edge_ref[1] = shift_ref[:, 5]


def edge_gradient(dense, low, high, weights):
    channels = dense.shape[2]
    return call(
        edge_gradient_body,
        [
            jax.ShapeDtypeStruct((2, SLAB, channels), F32),
            jax.ShapeDtypeStruct((2, 3, SHIFTED, channels), BF),
        ],
        [dense, low, high, weights],
        scratch=[pltpu.VMEM((3, 6, SHIFTED, channels), BF)],
        flops=4 * SLAB * KOFF * channels * channels,
    )


def upright(turned):
    return jnp.transpose(turned.astype(F32)).astype(BF)


def inner_forward_body(turned_far, weights_far, out_ref, shift_ref, turned_ref, weights_ref, sems):
    turned_in = pltpu.make_async_copy(turned_far, turned_ref, sems.at[0])
    weights_in = pltpu.make_async_copy(weights_far, weights_ref, sems.at[1])
    turned_in.start()
    weights_in.start()
    turned_in.wait()
    for x in range(NX):
        put_shifts(shift_ref, x, upright(turned_ref[:, x * SLAB : (x + 1) * SLAB]))
    weights_in.wait()

    def store(x, value):
        out_ref[x] = value.astype(BF)

    conv_inner(shift_ref, weights_ref, store)


def inner_forward(turned, weights):
    channels = turned.shape[0]
    return call(
        inner_forward_body,
        [jax.ShapeDtypeStruct((INNER, SLAB, channels), BF)],
        [turned, weights],
        far=(0, 1),
        scratch=[
            pltpu.VMEM((3, NX, SHIFTED, channels), BF),
            pltpu.VMEM(turned.shape, BF),
            pltpu.VMEM(weights.shape, BF),
            pltpu.SemaphoreType.DMA((2,)),
        ],
        flops=2 * INNER * SLAB * KOFF * channels * channels,
        limit=58,
    )[0]


def edge_forward_body(
    adj_ref, turned_far, low_ref, high_ref, weights_far, inner_far, out_ref,
    shift_ref, grid_ref, turned_ref, weights_ref, inner_ref, sems,
):
    ends = ((0, 2 * SLAB), (DENSE - 2 * SLAB, DENSE))
    copies = [
        pltpu.make_async_copy(turned_far.at[:, a:b], turned_ref.at[i], sems.at[i])
        for i, (a, b) in enumerate(ends)
    ]
    copies.append(pltpu.make_async_copy(weights_far, weights_ref, sems.at[2]))
    copies.append(pltpu.make_async_copy(inner_far, inner_ref, sems.at[3]))
    for copy in copies:
        copy.start()
    tiles, vox, channels = out_ref.shape
    lowest = lax.axis_index("region") * tiles
    before, after = upright(low_ref[...]), upright(high_ref[...])
    for copy in copies:
        copy.wait()
    own = [upright(turned_ref[i, :, j * SLAB : (j + 1) * SLAB]) for i in range(2) for j in range(2)]
    first, last = conv_edges(shift_ref, weights_ref, [before] + own + [after])
    grid_ref[0] = first.reshape(NY, NZ, channels)
    grid_ref[NX - 1] = last.reshape(NY, NZ, channels)
    for x in range(INNER):
        grid_ref[x + 1] = inner_ref[x].astype(F32).reshape(NY, NZ, channels)
    for t in range(tiles):
        x, y, z = corner(adj_ref, t, lowest)
        brick = grid_ref[pl.ds(x, VX), pl.ds(y, VY), pl.ds(pl.multiple_of(z, VZ), VZ), :]
        out_ref[t] = brick.reshape(vox, channels).astype(BF)


def edge_forward(adjacency, turned, low, high, weights, inner, tiles):
    channels = turned.shape[0]
    return call(
        edge_forward_body,
        [jax.ShapeDtypeStruct((tiles, VX * VY * VZ, channels), BF)],
        [adjacency, turned, low, high, weights, inner],
        smem=(0,),
        far=(1, 4, 5),
        scratch=[
            pltpu.VMEM((3, 6, SHIFTED, channels), BF),
            pltpu.VMEM((NX, NY, NZ, channels), F32),
            pltpu.VMEM((2, channels, 2 * SLAB), BF),
            pltpu.VMEM(weights.shape, BF),
            pltpu.VMEM(inner.shape, BF),
            pltpu.SemaphoreType.DMA((4,)),
        ],
        flops=4 * SLAB * KOFF * channels * channels,
        limit=58,
    )[0]


def read_slots(cap_rows, adj_ref, msg_ref, table_ref):
    regions = msg_ref.shape[0]
    tiles = adj_ref.shape[0]
    segs = up_to(cap_rows, LANES) // LANES
    lowest = lax.axis_index("region") * tiles
    for r in range(regions):
        tile = msg_ref[r, cap_rows : cap_rows + 16, :].astype(F32)
        for s in range(segs):
            lanes = slice(s * LANES, (s + 1) * LANES)
            table_ref[r : r + 1, lanes] = tile[s : s + 1]
            table_ref[regions + r : regions + r + 1, lanes] = tile[segs + s : segs + s + 1]
    high = table_ref[0:regions, :].astype(jnp.int32)
    low = table_ref[regions : 2 * regions, :].astype(jnp.int32)
    start = jnp.full(high.shape, -DENSE, jnp.int32)
    for t in range(tiles):
        x, y, z = corner(adj_ref, t, lowest)
        start = jnp.where(high == t + 1, (x * NY + y) * NZ + z, start)
    inside = ((low >> 5) * NY + ((low >> 3) & 3)) * NZ + (low & 7)
    spot = jnp.where(start < 0, -LANES, start + inside)
    blocks = (spot >> 7).astype(F32)
    withins = (spot & (LANES - 1)).astype(F32)
    return jnp.transpose(jnp.concatenate([blocks, withins], axis=0))


def fill_picks(pick_ref, columns, r, regions, cap_rows, row):
    shape = (cap_rows, LANES)
    lane = iota(shape, 1, F32).astype(BF)
    block = jnp.broadcast_to(columns[0:cap_rows, r : r + 1], shape).astype(BF)
    place = regions + r
    within = jnp.broadcast_to(columns[0:cap_rows, place : place + 1], shape).astype(BF)
    one = jnp.where(lane == within, jnp.ones_like(lane), jnp.zeros_like(lane))
    for q in range(DENSE // LANES):
        pick_ref[row : row + cap_rows, q * LANES : (q + 1) * LANES] = jnp.where(
            block == jnp.asarray(q, BF), one, jnp.zeros_like(one)
        )


def voxel_body(
    cap_rows, scaling, adj_ref, msg_ref, shift_far, grad_far, edge_shift_far, edge_grad_far,
    turned_far, low_ref, high_ref, back_far, keep_ref, send_ref,
    table_ref, feats_ref, pick_ref, all_ref, shift_ref, grad_ref, turned_ref, back_ref, sems,
):
    grad_pairs = (
        (grad_far, grad_ref.at[1 : NX - 1]),
        (edge_grad_far.at[0], grad_ref.at[0]),
        (edge_grad_far.at[1], grad_ref.at[NX - 1]),
    )
    shift_pairs = (
        (shift_far, shift_ref.at[:, 1 : NX + 1]),
        (edge_shift_far.at[0], shift_ref.at[:, 0]),
        (edge_shift_far.at[1], shift_ref.at[:, NX + 1]),
    )
    copies = [
        pltpu.make_async_copy(a, b, sems.at[2 + i]) for i, (a, b) in enumerate(grad_pairs + shift_pairs)
    ]
    for copy in copies:
        copy.start()
    regions, rows, channels = msg_ref.shape
    total = regions * cap_rows
    columns = read_slots(cap_rows, adj_ref, msg_ref, table_ref)
    for r in range(regions):
        feats_ref[r * cap_rows : (r + 1) * cap_rows, :] = msg_ref[r, 0:cap_rows, :]
        fill_picks(pick_ref, columns, r, regions, cap_rows, r * cap_rows)
    flipped = jnp.transpose(feats_ref[...].astype(F32)).astype(BF)
    left = jnp.concatenate([flipped, jnp.ones((16, total), BF)], axis=0)
    width = 2 * LANES
    for copy in copies[:3]:
        copy.wait()
    for q in range(0, DENSE, width):
        part = jnp.dot(left, pick_ref[:, q : q + width], preferred_element_type=F32)
        denom = jnp.maximum(part[channels : channels + 8], 1.0)
        turned_ref[:, q : q + width] = (part[0:channels] / denom[0:1]).astype(BF)
        x = q // SLAB
        grad_ref[x] = grad_ref[x] / jnp.transpose(denom)[:, 0:1]
    turned_out = pltpu.make_async_copy(turned_ref, turned_far, sems.at[0])
    turned_out.start()
    low_ref[...] = turned_ref[:, 0:SLAB]
    high_ref[...] = turned_ref[:, DENSE - SLAB : DENSE]
    voxel_grad = grad_ref[...].reshape(DENSE, channels).astype(BF)
    group = regions // 4
    for r in range(0, regions, group):
        picked = jnp.dot(
            pick_ref[r * cap_rows : (r + group) * cap_rows, :], voxel_grad, preferred_element_type=F32
        ).astype(BF)
        for i in range(group):
            back_ref[r + i] = picked[i * cap_rows : (i + 1) * cap_rows]
    back_out = pltpu.make_async_copy(back_ref, back_far, sems.at[1])
    back_out.start()
    left = turned_ref[...]
    for copy in copies[3:]:
        copy.wait()
    for k in range(0, KOFF, 2):
        pieces = []
        for j in range(k, min(k + 2, KOFF)):
            a, b, c = j // 9, j // 3 % 3, j % 3
            window = shift_ref[c, a : a + NX, b * NZ : b * NZ + SLAB, :]
            pieces.append(window.reshape(DENSE, channels))
        right = jnp.concatenate(pieces, axis=1)
        term = jnp.dot(left, right, preferred_element_type=F32) * scaling
        for i in range(len(pieces)):
            at = (KOFF - 1 - k - i) * channels
            all_ref[at : at + channels, :] = term[:, i * channels : (i + 1) * channels]
    core = lax.rem(lax.axis_index("region"), 2)
    half = keep_ref.shape[0]
    keep_ref[...] = all_ref[pl.ds(pl.multiple_of(core * half, 16), half), :]
    send_ref[...] = all_ref[pl.ds(pl.multiple_of((1 - core) * half, 16), half), :].astype(BF)
    turned_out.wait()
    back_out.wait()


def voxels(adjacency, msg, shifts, grad, edge_shifts, edge_grad, cap_rows, scaling):
    regions, rows, channels = msg.shape
    segs = up_to(cap_rows, LANES) // LANES
    total = regions * cap_rows
    face = jax.ShapeDtypeStruct((channels, SLAB), BF)
    half = (KOFF * channels // 2, channels)
    return call(
        functools.partial(voxel_body, cap_rows, scaling),
        [
            jax.ShapeDtypeStruct((channels, DENSE), BF),
            face,
            face,
            jax.ShapeDtypeStruct((regions, cap_rows, channels), BF),
            jax.ShapeDtypeStruct(half, F32),
            jax.ShapeDtypeStruct(half, BF),
        ],
        [adjacency, msg, shifts, grad, edge_shifts, edge_grad],
        smem=(0,),
        far=(2, 3, 4, 5),
        far_outs=(0, 3),
        scratch=[
            pltpu.VMEM((2 * regions, segs * LANES), F32),
            pltpu.VMEM((total, channels), BF),
            pltpu.VMEM((total, DENSE), BF),
            pltpu.VMEM((KOFF * channels, channels), F32),
            pltpu.VMEM((3, NX + 2, SHIFTED, channels), BF),
            pltpu.VMEM((NX, SLAB, channels), F32),
            pltpu.VMEM((channels, DENSE), BF),
            pltpu.VMEM((regions, cap_rows, channels), BF),
            pltpu.SemaphoreType.DMA((8,)),
        ],
        flops=2 * DENSE * (KOFF * channels + 2 * total) * channels,
        limit=60,
    )


def split_body(keep_ref, got_ref, own_ref, *sent_refs):
    rows = own_ref.shape[0]
    size = 1 + len(sent_refs)
    side = lax.rem(lax.axis_index("region") // 2, size)
    for i in range(size):
        part = pl.ds(pl.multiple_of((side ^ i) * rows, 16), rows)
        total = keep_ref[part, :] + got_ref[part, :].astype(F32)
        if i == 0:
            own_ref[...] = total
        else:
            sent_refs[i - 1][...] = total.astype(BF)


def split(keep, got, size):
    rows, channels = keep.shape[0] // size, keep.shape[1]
    return call(
        split_body,
        [jax.ShapeDtypeStruct((rows, channels), F32)]
        + [jax.ShapeDtypeStruct((rows, channels), BF)] * (size - 1),
        [keep, got],
    )


def unpack_body(place_ref, rows_ref, out_ref):
    regions, cap_rows, channels = rows_ref.shape
    points = out_ref.shape[0]
    total = regions * cap_rows
    place = jnp.transpose(place_ref[...])[:, 0:1].astype(jnp.int32)
    block = jnp.broadcast_to((place >> 7).astype(F32), (points, LANES)).astype(BF)
    within = jnp.broadcast_to((place & (LANES - 1)).astype(F32), (points, LANES)).astype(BF)
    lane = iota((points, LANES), 1, F32).astype(BF)
    one = jnp.where(lane == within, jnp.ones_like(lane), jnp.zeros_like(lane))
    rows = rows_ref[...].reshape(total, channels)
    chunk = 256
    for start in range(0, points, chunk):
        keep = slice(start, start + chunk)
        picks = [
            jnp.where(block[keep] == jnp.asarray(q, BF), one[keep], jnp.zeros_like(one[keep]))
            for q in range(total // LANES)
        ]
        picker = jnp.concatenate(picks, axis=1)
        out_ref[keep, :] = jnp.dot(picker, rows, preferred_element_type=F32).astype(BF)


def unpack(place, rows, points):
    regions, cap_rows, channels = rows.shape
    return call(
        unpack_body,
        [jax.ShapeDtypeStruct((points, channels), BF)],
        [place, rows],
        flops=2 * regions * cap_rows * points * channels,
    )[0]


def from_sides(low, high):
    count = lax.axis_size("region")
    up = [(i, i + 1) for i in range(count - 1)]
    down = [(j, i) for i, j in up]
    return lax.ppermute(high, "region", up), lax.ppermute(low, "region", down)


def swapped(array, bit):
    count = lax.axis_size("region")
    return lax.ppermute(array, "region", [(i, i ^ bit) for i in range(count)])


def in_order(pieces, side):
    return jnp.concatenate(
        [lax.select_n(side ^ q, *pieces) for q in range(len(pieces))], axis=0
    )


def reduce_group(term, bit, size):
    side = (lax.axis_index("region") // bit) % size
    rows = term.shape[0] // size
    parts = [lax.dynamic_slice_in_dim(term, (side ^ i) * rows, rows) for i in range(size)]
    return sum_group(parts[0], [part.astype(BF) for part in parts[1:]], bit)


def sum_group(total, sent, bit):
    for i, part in enumerate(sent):
        total = total + swapped(part, bit * (i + 1)).astype(F32)
    return total


def gather_group(term, bit, size):
    return [term] + [swapped(term, bit * i) for i in range(1, size)]


def groups_of(count):
    found, bit = [], 2
    while bit < count:
        size = min(4, count // bit)
        found.append((bit, size))
        bit *= size
    return found


def last_body(own_ref, other_ref, out_ref):
    size, rows, channels = own_ref.shape
    me = lax.axis_index("region")
    core = lax.rem(me, 2)
    side = lax.rem(me // 2, size)
    for half, ref in ((core, own_ref), (1 - core, other_ref)):
        for i in range(size):
            at = pl.multiple_of((half * size + (side ^ i)) * rows, 16)
            out_ref[pl.ds(at, rows), :] = ref[i].astype(F32)


def last_step(own, other):
    size, rows, channels = own.shape
    return call(
        last_body,
        [jax.ShapeDtypeStruct((2 * size * rows, channels), F32)],
        [own, other],
    )[0]


def exchange(array):
    return lax.all_to_all(array, "region", split_axis=0, concat_axis=0, tiled=True)


def local(point_feats, point_owner, point_slot, adjacency, kernel, cotangent):
    regions = lax.axis_size("region")
    points, channels = point_feats.shape
    tiles, vox = cotangent.shape[0], cotangent.shape[1]
    capacity = (5 * points + 2 * regions - 1) // (2 * regions)
    cap_rows = up_to(capacity, 16)
    msg, place = pack(
        point_owner.reshape(1, points), point_slot.reshape(1, points), point_feats, regions, cap_rows
    )
    received = exchange(msg)
    cot, cot_low, cot_high = to_dense(adjacency, cotangent)
    below, above = from_sides(cot_low, cot_high)
    mirrored = jnp.transpose(kernel[::-1], (0, 2, 1)).reshape(KOFF * channels, channels)
    grad, shifts = inner_gradient(cot, mirrored)
    edge_grad, edge_shifts = edge_gradient(cot, below, above, mirrored)
    scaling = 1.0 / math.sqrt(tiles * regions * vox)
    turned, low, high, back, keep, send = voxels(
        adjacency, received, shifts, grad, edge_shifts, edge_grad, cap_rows, scaling
    )
    returned = exchange(back)
    groups = groups_of(regions)
    bit, size = groups[0]
    term, *sent = split(keep, swapped(send, 1), size)
    weights = kernel.reshape(KOFF * channels, channels)
    turned, *sent = lax.optimization_barrier((turned, *sent))
    inner = inner_forward(turned, weights)
    term = sum_group(term, sent, bit)
    term, returned, inner = lax.optimization_barrier((term, returned, inner))
    for bit, size in groups[1:]:
        term = reduce_group(term, bit, size)
    term, low, high = lax.optimization_barrier((term.astype(BF), low, high))
    feats_below, feats_above = from_sides(low, high)
    grad_points = unpack(place, returned, points)
    out_tiles = edge_forward(adjacency, turned, feats_below, feats_above, weights, inner, tiles)
    for bit, size in groups[:0:-1]:
        side = (lax.axis_index("region") // bit) % size
        term = in_order(gather_group(term, bit, size), side)
    own = jnp.stack(gather_group(term, *groups[0]))
    own, out_tiles, grad_points = lax.optimization_barrier((own, out_tiles, grad_points))
    grad_weight = last_step(own, swapped(own, 1)).reshape(KOFF, channels, channels)
    return out_tiles, grad_points, grad_weight


def solution(mesh):
    placed = (
        P(("groups", "region"), None),
        P(("groups", "region"), None),
        P(("groups", "region")),
        P(("groups", "region"), None),
        P(),
        P(("groups", "region"), None, None),
    )
    return jax.shard_map(
        local,
        mesh=mesh,
        in_specs=placed,
        out_specs=(
            P(("groups", "region"), None, None),
            P(("groups", "region"), None),
            P("groups", None, None),
        ),
        check_vma=False,
    )
```

```python
import functools
import math

import jax
import jax.numpy as jnp
from jax import lax
from jax.experimental import pallas as pl
from jax.experimental.pallas import tpu as pltpu
from jax.sharding import PartitionSpec as P

VX = 4
VY = 4
VZ = 8
GY = 4
GZ = 2
SX = 2
KOFF = 27
NY = GY * VY
NZ = GZ * VZ
NX = SX * VX
SLAB = NY * NZ
DENSE = NX * SLAB
LANES = 128
BF = jnp.bfloat16
F32 = jnp.float32
VMEM = pl.BlockSpec(memory_space=pltpu.VMEM)
SMEM = pl.BlockSpec(memory_space=pltpu.SMEM)
FAR = pl.BlockSpec(memory_space=pltpu.HBM)
MIB = 1024 * 1024
VOXEL_LIMIT = 60


def up_to(value, unit):
    return (value + unit - 1) // unit * unit


def iota(shape, dim, dtype=jnp.int32):
    return lax.broadcasted_iota(jnp.int32, shape, dim).astype(dtype)


def call(body, outs, args, smem=(), far=(), far_outs=(), scratch=(), flops=0, limit=16):
    moved = sum(math.prod(o.shape) * o.dtype.itemsize for o in outs)
    moved += sum(math.prod(a.shape) * a.dtype.itemsize for a in args)
    return pl.pallas_call(
        body,
        out_shape=outs,
        in_specs=[SMEM if i in smem else FAR if i in far else VMEM for i in range(len(args))],
        out_specs=[FAR if i in far_outs else VMEM for i in range(len(outs))],
        scratch_shapes=list(scratch),
        compiler_params=pltpu.CompilerParams(vmem_limit_bytes=limit * MIB),
        cost_estimate=pl.CostEstimate(flops=flops, bytes_accessed=moved, transcendentals=0),
    )(*args)


def corner(adj_ref, t, lowest):
    tiles = adj_ref.shape[0]
    left = adj_ref[t, 4]
    layer = jnp.where((left >= lowest) & (left < lowest + tiles), 1, 0)
    before = adj_ref[t, 10]
    second = adj_ref[jnp.clip(before - lowest, 0, tiles - 1), 10] < 0
    inner = jnp.where(second, 1, 2)
    across = jnp.where(before < 0, 0, jnp.where(adj_ref[t, 16] < 0, GY - 1, inner))
    height = jnp.where(adj_ref[t, 12] >= 0, 1, 0)
    return layer * VX, across * VY, height * VZ


def pack_body(
    cap_rows, owner_far, slot_far, feats_far, msg_ref, place_ref, table_ref, owner_ref, slot_ref, feats_ref, sems
):
    regions = msg_ref.shape[0]
    points = feats_ref.shape[0]
    pairs = ((owner_far, owner_ref), (slot_far, slot_ref), (feats_far, feats_ref))
    copies = [pltpu.make_async_copy(a, b, sems.at[i]) for i, (a, b) in enumerate(pairs)]
    for copy in copies:
        copy.start()
    copies[0].wait()
    copies[1].wait()
    segs = up_to(cap_rows, LANES) // LANES
    owner = owner_ref[...]
    slot = slot_ref[...]
    mine = iota((regions, points), 0) == owner
    marks = jnp.where(mine, 1.0, 0.0)
    marks_bf = marks.astype(BF)
    earlier = jnp.where(iota((LANES, LANES), 0) < iota((LANES, LANES), 1), 1.0, 0.0).astype(BF)
    carry = jnp.zeros((regions, 1), F32)
    ranks = []
    for start in range(0, points, LANES):
        seg = marks[:, start : start + LANES]
        pre = jnp.dot(marks_bf[:, start : start + LANES], earlier, preferred_element_type=F32)
        ranks.append(jnp.sum((pre + carry) * seg, axis=0, keepdims=True))
        carry = carry + jnp.sum(seg, axis=1, keepdims=True)
    rank = jnp.concatenate(ranks, axis=1).astype(jnp.int32)
    place = owner * cap_rows + rank
    place_ref[...] = jnp.broadcast_to(place, (8, points)).astype(F32)
    block = jnp.broadcast_to((place >> 7).astype(F32), (LANES, points)).astype(BF)
    within = jnp.broadcast_to((place & (LANES - 1)).astype(F32), (LANES, points)).astype(BF)
    row = iota((LANES, points), 0, F32).astype(BF)
    one = jnp.where(row == within, jnp.ones_like(row), jnp.zeros_like(row))
    copies[2].wait()
    feats = feats_ref[...]
    chunk = math.lcm(cap_rows, LANES)
    for start in range(0, regions * cap_rows, chunk):
        picks = [
            jnp.where(block == jnp.asarray(q, BF), one, jnp.zeros_like(one))
            for q in range(start // LANES, (start + chunk) // LANES)
        ]
        picker = jnp.concatenate(picks, axis=0)
        rows = jnp.dot(picker, feats, preferred_element_type=F32).astype(BF)
        for i in range(chunk // cap_rows):
            msg_ref[start // cap_rows + i, 0:cap_rows, :] = rows[i * cap_rows : (i + 1) * cap_rows]
    high = jnp.where(mine, (slot >> 7) + 1, 0).astype(F32)
    low = jnp.where(mine, slot & (LANES - 1), 0).astype(F32)
    values = jnp.concatenate([high, low], axis=0).astype(BF)
    by_rank = jnp.where(iota((segs * LANES, points), 0) == rank, 1.0, 0.0).astype(BF)
    table_ref[...] = lax.dot_general(
        values, by_rank, (((1,), (1,)), ((), ())), preferred_element_type=F32
    )
    line = iota((16, LANES), 0)
    for o in range(regions):
        tile = jnp.zeros((16, LANES), F32)
        for s in range(segs):
            lanes = slice(s * LANES, (s + 1) * LANES)
            tile = jnp.where(line == s, table_ref[o : o + 1, lanes], tile)
            tile = jnp.where(line == segs + s, table_ref[regions + o : regions + o + 1, lanes], tile)
        msg_ref[o, cap_rows : cap_rows + 16, :] = tile.astype(BF)


def pack(owner, slot, feats, regions, cap_rows):
    points, channels = feats.shape
    segs = up_to(cap_rows, LANES) // LANES
    return call(
        functools.partial(pack_body, cap_rows),
        [
            jax.ShapeDtypeStruct((regions, cap_rows + 16, channels), BF),
            jax.ShapeDtypeStruct((8, points), F32),
        ],
        [owner, slot, feats],
        far=(0, 1, 2),
        scratch=[
            pltpu.VMEM((2 * regions, segs * LANES), F32),
            pltpu.VMEM((1, points), jnp.int32),
            pltpu.VMEM((1, points), jnp.int32),
            pltpu.VMEM((points, channels), BF),
            pltpu.SemaphoreType.DMA((3,)),
        ],
        limit=60,
        flops=2 * regions * cap_rows * points * channels,
    )


def dense_body(adj_ref, bricks_ref, dense_ref, low_ref, high_ref, grid_ref):
    tiles, vox, channels = bricks_ref.shape
    lowest = lax.axis_index("region") * tiles
    for t in range(tiles):
        x, y, z = corner(adj_ref, t, lowest)
        brick = bricks_ref[t].astype(F32).reshape(VX, VY, VZ, channels)
        grid_ref[pl.ds(x, VX), pl.ds(y, VY), pl.ds(pl.multiple_of(z, VZ), VZ), :] = brick
    for x in range(NX):
        slab = grid_ref[x].reshape(SLAB, channels).astype(BF)
        dense_ref[x] = slab
        if x == 0:
            low_ref[...] = slab
        if x == NX - 1:
            high_ref[...] = slab


def to_dense(adjacency, bricks):
    channels = bricks.shape[2]
    face = jax.ShapeDtypeStruct((SLAB, channels), BF)
    return call(
        dense_body,
        [jax.ShapeDtypeStruct((NX, SLAB, channels), BF), face, face],
        [adjacency, bricks],
        smem=(0,),
        scratch=[pltpu.VMEM((NX, NY, NZ, channels), F32)],
    )


SHIFTED = SLAB + 2 * NZ
INNER = NX - 2


def put_shifts(shift_ref, x, slab):
    border = jnp.zeros((NZ, slab.shape[1]), BF)
    height = iota(slab.shape, 0) % NZ
    wide = slab.astype(F32)
    lower = jnp.where(height == 0, 0.0, pltpu.roll(wide, 1, 0))
    upper = jnp.where(height == NZ - 1, 0.0, pltpu.roll(wide, SLAB - 1, 0))
    for c, copy in enumerate((lower.astype(BF), slab, upper.astype(BF))):
        shift_ref[c, x, 0:NZ, :] = border
        shift_ref[c, x, NZ : NZ + SLAB, :] = copy
        shift_ref[c, x, NZ + SLAB : SHIFTED, :] = border


def conv_slab(shift_ref, weights_ref, x):
    pieces = []
    for k in range(KOFF):
        a, b, c = k // 9, k // 3 % 3, k % 3
        pieces.append(shift_ref[c, x + a, b * NZ : b * NZ + SLAB, :])
    return jnp.dot(
        jnp.concatenate(pieces, axis=1), weights_ref[...], preferred_element_type=F32
    )


def conv_inner(shift_ref, weights_ref, store):
    def step(x, carry):
        store(x, conv_slab(shift_ref, weights_ref, x))
        return carry

    lax.fori_loop(0, INNER, step, 0)


def conv_edges(shift_ref, weights_ref, slabs):
    for i, slab in enumerate(slabs):
        put_shifts(shift_ref, i, slab)
    return conv_slab(shift_ref, weights_ref, 0), conv_slab(shift_ref, weights_ref, 3)


def inner_gradient_body(dense_ref, weights_ref, grad_ref, shift_ref):
    for x in range(NX):
        put_shifts(shift_ref, x, dense_ref[x])

    def store(x, value):
        grad_ref[x] = value

    conv_inner(shift_ref, weights_ref, store)


def inner_gradient(dense, weights):
    channels = dense.shape[2]
    return call(
        inner_gradient_body,
        [jax.ShapeDtypeStruct((INNER, SLAB, channels), F32)],
        [dense, weights],
        scratch=[pltpu.VMEM((3, NX, SHIFTED, channels), BF)],
        flops=2 * INNER * SLAB * KOFF * channels * channels,
    )[0]


def upright(turned):
    return jnp.transpose(turned.astype(F32)).astype(BF)


def inner_forward_body(turned_far, weights_far, out_ref, shift_ref, turned_ref, weights_ref, sems):
    turned_in = pltpu.make_async_copy(turned_far, turned_ref, sems.at[0])
    weights_in = pltpu.make_async_copy(weights_far, weights_ref, sems.at[1])
    turned_in.start()
    weights_in.start()
    turned_in.wait()
    for x in range(NX):
        put_shifts(shift_ref, x, upright(turned_ref[:, x * SLAB : (x + 1) * SLAB]))
    weights_in.wait()

    def store(x, value):
        out_ref[x] = value.astype(BF)

    conv_inner(shift_ref, weights_ref, store)


def inner_forward(turned, weights):
    channels = turned.shape[0]
    return call(
        inner_forward_body,
        [jax.ShapeDtypeStruct((INNER, SLAB, channels), BF)],
        [turned, weights],
        far=(0, 1),
        scratch=[
            pltpu.VMEM((3, NX, SHIFTED, channels), BF),
            pltpu.VMEM(turned.shape, BF),
            pltpu.VMEM(weights.shape, BF),
            pltpu.SemaphoreType.DMA((2,)),
        ],
        flops=2 * INNER * SLAB * KOFF * channels * channels,
        limit=20,
    )[0]


def edge_forward_body(
    adj_ref, turned_far, low_ref, high_ref, weights_far, inner_far, out_ref,
    shift_ref, grid_ref, turned_ref, weights_ref, inner_ref, sems,
):
    ends = ((0, 2 * SLAB), (DENSE - 2 * SLAB, DENSE))
    copies = [
        pltpu.make_async_copy(turned_far.at[:, a:b], turned_ref.at[i], sems.at[i])
        for i, (a, b) in enumerate(ends)
    ]
    copies.append(pltpu.make_async_copy(weights_far, weights_ref, sems.at[2]))
    copies.append(pltpu.make_async_copy(inner_far, inner_ref, sems.at[3]))
    for copy in copies:
        copy.start()
    tiles, vox, channels = out_ref.shape
    lowest = lax.axis_index("region") * tiles
    before, after = upright(low_ref[...]), upright(high_ref[...])
    for copy in copies:
        copy.wait()
    own = [upright(turned_ref[i, :, j * SLAB : (j + 1) * SLAB]) for i in range(2) for j in range(2)]
    first, last = conv_edges(shift_ref, weights_ref, [before] + own + [after])
    grid_ref[0] = first.reshape(NY, NZ, channels)
    grid_ref[NX - 1] = last.reshape(NY, NZ, channels)
    for x in range(INNER):
        grid_ref[x + 1] = inner_ref[x].astype(F32).reshape(NY, NZ, channels)
    for t in range(tiles):
        x, y, z = corner(adj_ref, t, lowest)
        brick = grid_ref[pl.ds(x, VX), pl.ds(y, VY), pl.ds(pl.multiple_of(z, VZ), VZ), :]
        out_ref[t] = brick.reshape(vox, channels).astype(BF)


def edge_forward(adjacency, turned, low, high, weights, inner, tiles):
    channels = turned.shape[0]
    return call(
        edge_forward_body,
        [jax.ShapeDtypeStruct((tiles, VX * VY * VZ, channels), BF)],
        [adjacency, turned, low, high, weights, inner],
        smem=(0,),
        far=(1, 4, 5),
        scratch=[
            pltpu.VMEM((3, 6, SHIFTED, channels), BF),
            pltpu.VMEM((NX, NY, NZ, channels), F32),
            pltpu.VMEM((2, channels, 2 * SLAB), BF),
            pltpu.VMEM(weights.shape, BF),
            pltpu.VMEM(inner.shape, BF),
            pltpu.SemaphoreType.DMA((4,)),
        ],
        flops=4 * SLAB * KOFF * channels * channels,
        limit=20,
    )[0]


def read_slots(cap_rows, adj_ref, msg_ref, table_ref):
    regions = msg_ref.shape[0]
    tiles = adj_ref.shape[0]
    segs = up_to(cap_rows, LANES) // LANES
    lowest = lax.axis_index("region") * tiles
    for r in range(regions):
        tile = msg_ref[r, cap_rows : cap_rows + 16, :].astype(F32)
        for s in range(segs):
            lanes = slice(s * LANES, (s + 1) * LANES)
            table_ref[r : r + 1, lanes] = tile[s : s + 1]
            table_ref[regions + r : regions + r + 1, lanes] = tile[segs + s : segs + s + 1]
    high = table_ref[0:regions, :].astype(jnp.int32)
    low = table_ref[regions : 2 * regions, :].astype(jnp.int32)
    start = jnp.full(high.shape, -DENSE, jnp.int32)
    for t in range(tiles):
        x, y, z = corner(adj_ref, t, lowest)
        start = jnp.where(high == t + 1, (x * NY + y) * NZ + z, start)
    inside = ((low >> 5) * NY + ((low >> 3) & 3)) * NZ + (low & 7)
    spot = jnp.where(start < 0, -LANES, start + inside)
    blocks = (spot >> 7).astype(F32)
    withins = (spot & (LANES - 1)).astype(F32)
    return jnp.transpose(jnp.concatenate([blocks, withins], axis=0))


def fill_picks(pick_ref, columns, r, regions, cap_rows, row):
    shape = (cap_rows, LANES)
    lane = iota(shape, 1, F32).astype(BF)
    block = jnp.broadcast_to(columns[0:cap_rows, r : r + 1], shape).astype(BF)
    place = regions + r
    within = jnp.broadcast_to(columns[0:cap_rows, place : place + 1], shape).astype(BF)
    one = jnp.where(lane == within, jnp.ones_like(lane), jnp.zeros_like(lane))
    for q in range(DENSE // LANES):
        pick_ref[row : row + cap_rows, q * LANES : (q + 1) * LANES] = jnp.where(
            block == jnp.asarray(q, BF), one, jnp.zeros_like(one)
        )


def voxel_body(
    cap_rows, scaling,
    adj_far, msg_far, below_far, above_far, dense_far, weights_far, grad_far,
    turned_far, low_far, high_far, back_far, keep_far, send_far,
    adj_ref, msg_ref, below_ref, above_ref, dense_ref, weights_ref, grad_ref,
    turned_ref, back_ref,
    table_ref, feats_ref, pick_ref, all_ref, shift_ref, in_sems, out_sems,
):
    pairs = (
        (adj_far, adj_ref),
        (msg_far, msg_ref),
        (below_far, below_ref),
        (above_far, above_ref),
        (dense_far, dense_ref),
        (weights_far, weights_ref),
        (grad_far, grad_ref.at[1 : NX - 1]),
    )
    copies = [pltpu.make_async_copy(a, b, in_sems.at[i]) for i, (a, b) in enumerate(pairs)]
    for copy in copies:
        copy.start()
    regions, rows, channels = msg_ref.shape
    total = regions * cap_rows
    for copy in copies[2:]:
        copy.wait()
    slabs = [below_ref[...]] + [dense_ref[x] for x in range(NX)] + [above_ref[...]]
    for x, slab in enumerate(slabs):
        put_shifts(shift_ref, x, slab)
    for x in (0, NX - 1):
        grad_ref[x] = conv_slab(shift_ref, weights_ref, x)
    copies[0].wait()
    copies[1].wait()
    columns = read_slots(cap_rows, adj_ref, msg_ref, table_ref)
    for r in range(regions):
        feats_ref[r * cap_rows : (r + 1) * cap_rows, :] = msg_ref[r, 0:cap_rows, :]
        fill_picks(pick_ref, columns, r, regions, cap_rows, r * cap_rows)
    flipped = jnp.transpose(feats_ref[...].astype(F32)).astype(BF)
    left = jnp.concatenate([flipped, jnp.ones((16, total), BF)], axis=0)
    width = 2 * LANES
    for q in range(0, DENSE, width):
        part = jnp.dot(left, pick_ref[:, q : q + width], preferred_element_type=F32)
        denom = jnp.maximum(part[channels : channels + 8], 1.0)
        turned_ref[:, q : q + width] = (part[0:channels] / denom[0:1]).astype(BF)
        x = q // SLAB
        grad_ref[x] = grad_ref[x] / jnp.transpose(denom)[:, 0:1]
    core = lax.rem(lax.axis_index("region"), 2)
    half = keep_far.shape[0]
    outs = (
        (turned_ref, turned_far),
        (turned_ref.at[:, 0:SLAB], low_far),
        (turned_ref.at[:, DENSE - SLAB : DENSE], high_far),
        (back_ref, back_far),
        (all_ref.at[pl.ds(pl.multiple_of(core * half, 16), half)], keep_far),
        (all_ref.at[pl.ds(pl.multiple_of((1 - core) * half, 16), half)], send_far),
    )
    results = [pltpu.make_async_copy(a, b, out_sems.at[i]) for i, (a, b) in enumerate(outs)]
    for copy in results[:3]:
        copy.start()
    voxel_grad = grad_ref[...].reshape(DENSE, channels).astype(BF)
    group = regions // 4
    for r in range(0, regions, group):
        picked = jnp.dot(
            pick_ref[r * cap_rows : (r + group) * cap_rows, :], voxel_grad, preferred_element_type=F32
        ).astype(BF)
        for i in range(group):
            back_ref[r + i] = picked[i * cap_rows : (i + 1) * cap_rows]
    results[3].start()
    left = turned_ref[...]
    for k in range(0, KOFF, 2):
        pieces = []
        for j in range(k, min(k + 2, KOFF)):
            a, b, c = j // 9, j // 3 % 3, j % 3
            window = shift_ref[c, a : a + NX, b * NZ : b * NZ + SLAB, :]
            pieces.append(window.reshape(DENSE, channels))
        right = jnp.concatenate(pieces, axis=1)
        term = jnp.dot(left, right, preferred_element_type=F32) * scaling
        for i in range(len(pieces)):
            at = (KOFF - 1 - k - i) * channels
            all_ref[at : at + channels, :] = term[:, i * channels : (i + 1) * channels]
    results[4].start()
    results[5].start()
    for copy in results:
        copy.wait()


def voxels(adjacency, msg, below, above, dense, weights, grad, cap_rows, scaling):
    regions, rows, channels = msg.shape
    segs = up_to(cap_rows, LANES) // LANES
    total = regions * cap_rows
    half = (KOFF * channels // 2, channels)
    turned, back = (channels, DENSE), (regions, cap_rows, channels)
    face = jax.ShapeDtypeStruct((channels, SLAB), BF)
    return call(
        functools.partial(voxel_body, cap_rows, scaling),
        [
            jax.ShapeDtypeStruct(turned, BF),
            face,
            face,
            jax.ShapeDtypeStruct(back, BF),
            jax.ShapeDtypeStruct(half, F32),
            jax.ShapeDtypeStruct(half, F32),
        ],
        [adjacency, msg, below, above, dense, weights, grad],
        far=range(7),
        far_outs=range(6),
        scratch=[
            pltpu.SMEM(adjacency.shape, jnp.int32),
            pltpu.VMEM(msg.shape, BF),
            pltpu.VMEM(below.shape, BF),
            pltpu.VMEM(above.shape, BF),
            pltpu.VMEM(dense.shape, BF),
            pltpu.VMEM(weights.shape, BF),
            pltpu.VMEM((NX, SLAB, channels), F32),
            pltpu.VMEM(turned, BF),
            pltpu.VMEM(back, BF),
            pltpu.VMEM((2 * regions, segs * LANES), F32),
            pltpu.VMEM((total, channels), BF),
            pltpu.VMEM((total, DENSE), BF),
            pltpu.VMEM((KOFF * channels, channels), F32),
            pltpu.VMEM((3, NX + 2, SHIFTED, channels), BF),
            pltpu.SemaphoreType.DMA((7,)),
            pltpu.SemaphoreType.DMA((6,)),
        ],
        flops=2 * DENSE * (KOFF * channels + 2 * total) * channels,
        limit=VOXEL_LIMIT,
    )


def split_body(keep_ref, got_ref, own_ref, *sent_refs):
    rows = own_ref.shape[0]
    size = 1 + len(sent_refs)
    side = lax.rem(lax.axis_index("region") // 2, size)
    for i in range(size):
        part = pl.ds(pl.multiple_of((side ^ i) * rows, 16), rows)
        total = keep_ref[part, :] + got_ref[part, :]
        if i == 0:
            own_ref[...] = total
        else:
            sent_refs[i - 1][...] = total.astype(BF)


def split(keep, got, size):
    rows, channels = keep.shape[0] // size, keep.shape[1]
    return call(
        split_body,
        [jax.ShapeDtypeStruct((rows, channels), F32)]
        + [jax.ShapeDtypeStruct((rows, channels), BF)] * (size - 1),
        [keep, got],
    )


def unpack_body(place_ref, rows_ref, out_ref):
    regions, cap_rows, channels = rows_ref.shape
    points = out_ref.shape[0]
    total = regions * cap_rows
    place = jnp.transpose(place_ref[...])[:, 0:1].astype(jnp.int32)
    block = jnp.broadcast_to((place >> 7).astype(F32), (points, LANES)).astype(BF)
    within = jnp.broadcast_to((place & (LANES - 1)).astype(F32), (points, LANES)).astype(BF)
    lane = iota((points, LANES), 1, F32).astype(BF)
    one = jnp.where(lane == within, jnp.ones_like(lane), jnp.zeros_like(lane))
    rows = rows_ref[...].reshape(total, channels)
    chunk = 256
    for start in range(0, points, chunk):
        keep = slice(start, start + chunk)
        picks = [
            jnp.where(block[keep] == jnp.asarray(q, BF), one[keep], jnp.zeros_like(one[keep]))
            for q in range(total // LANES)
        ]
        picker = jnp.concatenate(picks, axis=1)
        out_ref[keep, :] = jnp.dot(picker, rows, preferred_element_type=F32).astype(BF)


def unpack(place, rows, points):
    regions, cap_rows, channels = rows.shape
    return call(
        unpack_body,
        [jax.ShapeDtypeStruct((points, channels), BF)],
        [place, rows],
        flops=2 * regions * cap_rows * points * channels,
    )[0]


def from_sides(low, high):
    count = lax.axis_size("region")
    up = [(i, i + 1) for i in range(count - 1)]
    down = [(j, i) for i, j in up]
    return lax.ppermute(high, "region", up), lax.ppermute(low, "region", down)


def swapped(array, bit):
    count = lax.axis_size("region")
    return lax.ppermute(array, "region", [(i, i ^ bit) for i in range(count)])


def in_order(pieces, side):
    return jnp.concatenate(
        [lax.select_n(side ^ q, *pieces) for q in range(len(pieces))], axis=0
    )


def reduce_group(term, bit, size):
    side = (lax.axis_index("region") // bit) % size
    rows = term.shape[0] // size
    parts = [lax.dynamic_slice_in_dim(term, (side ^ i) * rows, rows) for i in range(size)]
    return sum_group(parts[0], [part.astype(BF) for part in parts[1:]], bit)


def exchange_group(term, bit, size, beside):
    side = (lax.axis_index("region") // bit) % size
    term, beside = lax.optimization_barrier((term.astype(BF), beside))
    terms = gather_group(term, bit, size)
    total = lax.select_n(side, *terms).astype(F32)
    for q in range(1, size):
        total = total + lax.select_n(side ^ q, *terms).astype(F32)
    return total.astype(BF), beside


def sum_group(total, sent, bit):
    for i, part in enumerate(sent):
        total = total + swapped(part, bit * (i + 1)).astype(F32)
    return total


def gather_group(term, bit, size):
    return [term] + [swapped(term, bit * i) for i in range(1, size)]


def groups_of(count):
    found, bit = [], 2
    while bit < count:
        size = min(4, count // bit)
        found.append((bit, size))
        bit *= size
    return found


def last_body(own_ref, other_ref, out_ref):
    size, rows, channels = own_ref.shape
    me = lax.axis_index("region")
    core = lax.rem(me, 2)
    side = lax.rem(me // 2, size)
    for half, ref in ((core, own_ref), (1 - core, other_ref)):
        for i in range(size):
            at = pl.multiple_of((half * size + (side ^ i)) * rows, 16)
            out_ref[pl.ds(at, rows), :] = ref[i].astype(F32)


def last_step(own, other):
    size, rows, channels = own.shape
    return call(
        last_body,
        [jax.ShapeDtypeStruct((2 * size * rows, channels), F32)],
        [own, other],
    )[0]


def exchange(array):
    return lax.all_to_all(array, "region", split_axis=0, concat_axis=0, tiled=True)


def local(point_feats, point_owner, point_slot, adjacency, kernel, cotangent):
    regions = lax.axis_size("region")
    points, channels = point_feats.shape
    tiles, vox = cotangent.shape[0], cotangent.shape[1]
    capacity = (5 * points + 2 * regions - 1) // (2 * regions)
    cap_rows = up_to(capacity, 16)
    msg, place = pack(
        point_owner.reshape(1, points), point_slot.reshape(1, points), point_feats, regions, cap_rows
    )
    received = exchange(msg)
    cot, cot_low, cot_high = to_dense(adjacency, cotangent)
    below, above = from_sides(cot_low, cot_high)
    mirrored = jnp.transpose(kernel[::-1], (0, 2, 1)).reshape(KOFF * channels, channels)
    grad = inner_gradient(cot, mirrored)
    scaling = 1.0 / math.sqrt(tiles * regions * vox)
    turned, low, high, back, keep, send = voxels(
        adjacency, received, below, above, cot, mirrored, grad, cap_rows, scaling
    )
    returned = exchange(back)
    groups = groups_of(regions)
    bit, size = groups[0]
    term, *sent = split(keep, swapped(send, 1), size)
    weights = kernel.reshape(KOFF * channels, channels)
    turned, low, high, *sent = lax.optimization_barrier((turned, low, high, *sent))
    feats_below, feats_above = from_sides(low, high)
    inner = inner_forward(turned, weights)
    term = sum_group(term, sent, bit)
    term, returned, inner, feats_below, feats_above = lax.optimization_barrier(
        (term, returned, inner, feats_below, feats_above)
    )
    for bit, size in groups[1:-1]:
        term = reduce_group(term, bit, size)
    bit, size = groups[-1]
    term, returned = exchange_group(term, bit, size, returned)
    grad_points = unpack(place, returned, points)
    for bit, size in groups[-2:0:-1]:
        side = (lax.axis_index("region") // bit) % size
        term = in_order(gather_group(term, bit, size), side)
    term, grad_points = lax.optimization_barrier((term, grad_points))
    out_tiles = edge_forward(adjacency, turned, feats_below, feats_above, weights, inner, tiles)
    own = jnp.stack(gather_group(term, *groups[0]))
    own, out_tiles = lax.optimization_barrier((own, out_tiles))
    grad_weight = last_step(own, swapped(own, 1)).reshape(KOFF, channels, channels)
    return out_tiles, grad_points, grad_weight


def solution(mesh):
    placed = (
        P(("groups", "region"), None),
        P(("groups", "region"), None),
        P(("groups", "region")),
        P(("groups", "region"), None),
        P(),
        P(("groups", "region"), None, None),
    )
    return jax.shard_map(
        local,
        mesh=mesh,
        in_specs=placed,
        out_specs=(
            P(("groups", "region"), None, None),
            P(("groups", "region"), None),
            P("groups", None, None),
        ),
        check_vma=False,
    )
```

```python
import functools
import math

import jax
import jax.numpy as jnp
from jax import lax
from jax.experimental import pallas as pl
from jax.experimental.pallas import tpu as pltpu
from jax.sharding import PartitionSpec as P

VX = 4
VY = 4
VZ = 8
GY = 4
GZ = 2
SX = 2
KOFF = 27
NY = GY * VY
NZ = GZ * VZ
NX = SX * VX
SLAB = NY * NZ
DENSE = NX * SLAB
HALF = DENSE // 2
LANES = 128
BF = jnp.bfloat16
F32 = jnp.float32
VMEM = pl.BlockSpec(memory_space=pltpu.VMEM)
SMEM = pl.BlockSpec(memory_space=pltpu.SMEM)
FAR = pl.BlockSpec(memory_space=pltpu.HBM)
MIB = 1024 * 1024


def up_to(value, unit):
    return (value + unit - 1) // unit * unit


def iota(shape, dim, dtype=jnp.int32):
    return lax.broadcasted_iota(jnp.int32, shape, dim).astype(dtype)


def call(body, outs, args, smem=(), far=(), far_outs=(), scratch=(), flops=0, limit=16, quick=False):
    moved = sum(math.prod(o.shape) * o.dtype.itemsize for o in outs)
    moved += sum(math.prod(a.shape) * a.dtype.itemsize for a in args)
    if quick:
        flops, moved = 0, 1024
    return pl.pallas_call(
        body,
        out_shape=outs,
        in_specs=[SMEM if i in smem else FAR if i in far else VMEM for i in range(len(args))],
        out_specs=[FAR if i in far_outs else VMEM for i in range(len(outs))],
        scratch_shapes=list(scratch),
        compiler_params=pltpu.CompilerParams(vmem_limit_bytes=limit * MIB),
        cost_estimate=pl.CostEstimate(flops=flops, bytes_accessed=moved, transcendentals=0),
    )(*args)


def start_all(pairs, sems):
    copies = [pltpu.make_async_copy(a, b, sems.at[i]) for i, (a, b) in enumerate(pairs)]
    for copy in copies:
        copy.start()
    return copies


def corner(adj_ref, t, lowest):
    tiles = adj_ref.shape[0]
    left = adj_ref[t, 4]
    layer = jnp.where((left >= lowest) & (left < lowest + tiles), 1, 0)
    before = adj_ref[t, 10]
    second = adj_ref[jnp.clip(before - lowest, 0, tiles - 1), 10] < 0
    inner = jnp.where(second, 1, 2)
    across = jnp.where(before < 0, 0, jnp.where(adj_ref[t, 16] < 0, GY - 1, inner))
    height = jnp.where(adj_ref[t, 12] >= 0, 1, 0)
    return layer * VX, across * VY, height * VZ


def pack_body(
    cap_rows, owner_far, slot_far, feats_far, msg_ref, place_ref, table_ref, owner_ref, slot_ref, feats_ref, sems
):
    regions = msg_ref.shape[0]
    points = feats_ref.shape[0]
    pairs = ((owner_far, owner_ref), (slot_far, slot_ref), (feats_far, feats_ref))
    copies = [pltpu.make_async_copy(a, b, sems.at[i]) for i, (a, b) in enumerate(pairs)]
    for copy in copies:
        copy.start()
    copies[0].wait()
    copies[1].wait()
    segs = up_to(cap_rows, LANES) // LANES
    owner = owner_ref[...]
    slot = slot_ref[...]
    mine = iota((regions, points), 0) == owner
    marks = jnp.where(mine, 1.0, 0.0)
    marks_bf = marks.astype(BF)
    earlier = jnp.where(iota((LANES, LANES), 0) < iota((LANES, LANES), 1), 1.0, 0.0).astype(BF)
    carry = jnp.zeros((regions, 1), F32)
    ranks = []
    for start in range(0, points, LANES):
        seg = marks[:, start : start + LANES]
        pre = jnp.dot(marks_bf[:, start : start + LANES], earlier, preferred_element_type=F32)
        ranks.append(jnp.sum((pre + carry) * seg, axis=0, keepdims=True))
        carry = carry + jnp.sum(seg, axis=1, keepdims=True)
    rank = jnp.concatenate(ranks, axis=1).astype(jnp.int32)
    place = owner * cap_rows + rank
    place_ref[...] = jnp.broadcast_to(place, (8, points)).astype(F32)
    block = jnp.broadcast_to((place >> 7).astype(F32), (LANES, points)).astype(BF)
    within = jnp.broadcast_to((place & (LANES - 1)).astype(F32), (LANES, points)).astype(BF)
    row = iota((LANES, points), 0, F32).astype(BF)
    one = jnp.where(row == within, jnp.ones_like(row), jnp.zeros_like(row))
    copies[2].wait()
    feats = feats_ref[...]
    chunk = math.lcm(cap_rows, LANES)
    for start in range(0, regions * cap_rows, chunk):
        picks = [
            jnp.where(block == jnp.asarray(q, BF), one, jnp.zeros_like(one))
            for q in range(start // LANES, (start + chunk) // LANES)
        ]
        picker = jnp.concatenate(picks, axis=0)
        rows = jnp.dot(picker, feats, preferred_element_type=F32).astype(BF)
        for i in range(chunk // cap_rows):
            msg_ref[start // cap_rows + i, 0:cap_rows, :] = rows[i * cap_rows : (i + 1) * cap_rows]
    high = jnp.where(mine, (slot >> 7) + 1, 0).astype(F32)
    low = jnp.where(mine, slot & (LANES - 1), 0).astype(F32)
    values = jnp.concatenate([high, low], axis=0).astype(BF)
    by_rank = jnp.where(iota((segs * LANES, points), 0) == rank, 1.0, 0.0).astype(BF)
    table_ref[...] = lax.dot_general(
        values, by_rank, (((1,), (1,)), ((), ())), preferred_element_type=F32
    )
    line = iota((16, LANES), 0)
    for o in range(regions):
        tile = jnp.zeros((16, LANES), F32)
        for s in range(segs):
            lanes = slice(s * LANES, (s + 1) * LANES)
            tile = jnp.where(line == s, table_ref[o : o + 1, lanes], tile)
            tile = jnp.where(line == segs + s, table_ref[regions + o : regions + o + 1, lanes], tile)
        msg_ref[o, cap_rows : cap_rows + 16, :] = tile.astype(BF)


def pack(owner, slot, feats, regions, cap_rows):
    points, channels = feats.shape
    segs = up_to(cap_rows, LANES) // LANES
    return call(
        functools.partial(pack_body, cap_rows),
        [
            jax.ShapeDtypeStruct((regions, cap_rows + 16, channels), BF),
            jax.ShapeDtypeStruct((8, points), F32),
        ],
        [owner, slot, feats],
        far=(0, 1, 2),
        scratch=[
            pltpu.VMEM((2 * regions, segs * LANES), F32),
            pltpu.VMEM((1, points), jnp.int32),
            pltpu.VMEM((1, points), jnp.int32),
            pltpu.VMEM((points, channels), BF),
            pltpu.SemaphoreType.DMA((3,)),
        ],
        limit=60,
        flops=2 * regions * cap_rows * points * channels,
    )


def dense_body(adj_ref, bricks_ref, dense_ref, low_ref, high_ref, grid_ref):
    tiles, vox, channels = bricks_ref.shape
    lowest = lax.axis_index("region") * tiles
    for t in range(tiles):
        x, y, z = corner(adj_ref, t, lowest)
        brick = bricks_ref[t].astype(F32).reshape(VX, VY, VZ, channels)
        grid_ref[pl.ds(x, VX), pl.ds(y, VY), pl.ds(pl.multiple_of(z, VZ), VZ), :] = brick
    for x in range(NX):
        slab = grid_ref[x].reshape(SLAB, channels).astype(BF)
        dense_ref[x] = slab
        if x == 0:
            low_ref[...] = slab
        if x == NX - 1:
            high_ref[...] = slab


def to_dense(adjacency, bricks):
    channels = bricks.shape[2]
    face = jax.ShapeDtypeStruct((SLAB, channels), BF)
    return call(
        dense_body,
        [jax.ShapeDtypeStruct((NX, SLAB, channels), BF), face, face],
        [adjacency, bricks],
        smem=(0,),
        scratch=[pltpu.VMEM((NX, NY, NZ, channels), F32)],
    )


SHIFTED = SLAB + 2 * NZ
INNER = NX - 2


def put_shifts(shift_ref, x, slab):
    border = jnp.zeros((NZ, slab.shape[1]), BF)
    height = iota(slab.shape, 0) % NZ
    wide = slab.astype(F32)
    lower = jnp.where(height == 0, 0.0, pltpu.roll(wide, 1, 0))
    upper = jnp.where(height == NZ - 1, 0.0, pltpu.roll(wide, SLAB - 1, 0))
    for c, copy in enumerate((lower.astype(BF), slab, upper.astype(BF))):
        shift_ref[c, x, 0:NZ, :] = border
        shift_ref[c, x, NZ : NZ + SLAB, :] = copy
        shift_ref[c, x, NZ + SLAB : SHIFTED, :] = border


def conv_slab(shift_ref, weights_ref, x):
    pieces = []
    for k in range(KOFF):
        a, b, c = k // 9, k // 3 % 3, k % 3
        pieces.append(shift_ref[c, x + a, b * NZ : b * NZ + SLAB, :])
    return jnp.dot(
        jnp.concatenate(pieces, axis=1), weights_ref[...], preferred_element_type=F32
    )


def conv_inner(shift_ref, weights_ref, store):
    def step(x, carry):
        store(x, conv_slab(shift_ref, weights_ref, x))
        return carry

    lax.fori_loop(0, INNER, step, 0)


def conv_edges(shift_ref, weights_ref, slabs):
    for i, slab in enumerate(slabs):
        put_shifts(shift_ref, i, slab)
    return conv_slab(shift_ref, weights_ref, 0), conv_slab(shift_ref, weights_ref, 3)


def inner_gradient_body(dense_ref, weights_ref, grad_ref, shift_ref):
    for x in range(NX):
        put_shifts(shift_ref, x, dense_ref[x])

    def store(x, value):
        grad_ref[x] = value

    conv_inner(shift_ref, weights_ref, store)


def inner_gradient(dense, weights):
    channels = dense.shape[2]
    return call(
        inner_gradient_body,
        [jax.ShapeDtypeStruct((INNER, SLAB, channels), F32)],
        [dense, weights],
        scratch=[pltpu.VMEM((3, NX, SHIFTED, channels), BF)],
        flops=2 * INNER * SLAB * KOFF * channels * channels,
    )[0]


def upright(turned):
    return jnp.transpose(turned.astype(F32)).astype(BF)


def inner_forward_body(turned_far, weights_far, out_ref, shift_ref, turned_ref, weights_ref, sems):
    turned_in = pltpu.make_async_copy(turned_far, turned_ref, sems.at[0])
    weights_in = pltpu.make_async_copy(weights_far, weights_ref, sems.at[1])
    turned_in.start()
    weights_in.start()
    turned_in.wait()
    for x in range(NX):
        put_shifts(shift_ref, x, upright(turned_ref[:, x * SLAB : (x + 1) * SLAB]))
    weights_in.wait()

    def store(x, value):
        out_ref[x] = value.astype(BF)

    conv_inner(shift_ref, weights_ref, store)


def inner_forward(turned, weights):
    channels = turned.shape[0]
    return call(
        inner_forward_body,
        [jax.ShapeDtypeStruct((INNER, SLAB, channels), BF)],
        [turned, weights],
        far=(0, 1),
        scratch=[
            pltpu.VMEM((3, NX, SHIFTED, channels), BF),
            pltpu.VMEM(turned.shape, BF),
            pltpu.VMEM(weights.shape, BF),
            pltpu.SemaphoreType.DMA((2,)),
        ],
        flops=2 * INNER * SLAB * KOFF * channels * channels,
        limit=20,
        quick=True,
    )[0]


def edge_forward_body(
    adj_ref, turned_far, low_ref, high_ref, weights_far, inner_far, out_ref,
    shift_ref, grid_ref, turned_ref, weights_ref, inner_ref, sems,
):
    ends = ((0, 2 * SLAB), (DENSE - 2 * SLAB, DENSE))
    copies = [
        pltpu.make_async_copy(turned_far.at[:, a:b], turned_ref.at[i], sems.at[i])
        for i, (a, b) in enumerate(ends)
    ]
    copies.append(pltpu.make_async_copy(weights_far, weights_ref, sems.at[2]))
    copies.append(pltpu.make_async_copy(inner_far, inner_ref, sems.at[3]))
    for copy in copies:
        copy.start()
    tiles, vox, channels = out_ref.shape
    lowest = lax.axis_index("region") * tiles
    before, after = upright(low_ref[...]), upright(high_ref[...])
    for copy in copies:
        copy.wait()
    own = [upright(turned_ref[i, :, j * SLAB : (j + 1) * SLAB]) for i in range(2) for j in range(2)]
    first, last = conv_edges(shift_ref, weights_ref, [before] + own + [after])
    grid_ref[0] = first.reshape(NY, NZ, channels)
    grid_ref[NX - 1] = last.reshape(NY, NZ, channels)
    for x in range(INNER):
        grid_ref[x + 1] = inner_ref[x].astype(F32).reshape(NY, NZ, channels)
    for t in range(tiles):
        x, y, z = corner(adj_ref, t, lowest)
        brick = grid_ref[pl.ds(x, VX), pl.ds(y, VY), pl.ds(pl.multiple_of(z, VZ), VZ), :]
        out_ref[t] = brick.reshape(vox, channels).astype(BF)


def edge_forward(adjacency, turned, low, high, weights, inner, tiles):
    channels = turned.shape[0]
    return call(
        edge_forward_body,
        [jax.ShapeDtypeStruct((tiles, VX * VY * VZ, channels), BF)],
        [adjacency, turned, low, high, weights, inner],
        smem=(0,),
        far=(1, 4, 5),
        scratch=[
            pltpu.VMEM((3, 6, SHIFTED, channels), BF),
            pltpu.VMEM((NX, NY, NZ, channels), F32),
            pltpu.VMEM((2, channels, 2 * SLAB), BF),
            pltpu.VMEM(weights.shape, BF),
            pltpu.VMEM(inner.shape, BF),
            pltpu.SemaphoreType.DMA((4,)),
        ],
        flops=4 * SLAB * KOFF * channels * channels,
        limit=20,
    )[0]


def read_slots(cap_rows, adj_ref, slots_ref, table_ref):
    regions = slots_ref.shape[0]
    tiles = adj_ref.shape[0]
    segs = up_to(cap_rows, LANES) // LANES
    lowest = lax.axis_index("region") * tiles
    for r in range(regions):
        tile = slots_ref[r].astype(F32)
        for s in range(segs):
            lanes = slice(s * LANES, (s + 1) * LANES)
            table_ref[r : r + 1, lanes] = tile[s : s + 1]
            table_ref[regions + r : regions + r + 1, lanes] = tile[segs + s : segs + s + 1]
    high = table_ref[0:regions, :].astype(jnp.int32)
    low = table_ref[regions : 2 * regions, :].astype(jnp.int32)
    start = jnp.full(high.shape, -DENSE, jnp.int32)
    for t in range(tiles):
        x, y, z = corner(adj_ref, t, lowest)
        start = jnp.where(high == t + 1, (x * NY + y) * NZ + z, start)
    inside = ((low >> 5) * NY + ((low >> 3) & 3)) * NZ + (low & 7)
    spot = jnp.where(start < 0, -LANES, start + inside)
    blocks = (spot >> 7).astype(F32)
    withins = (spot & (LANES - 1)).astype(F32)
    return jnp.transpose(jnp.concatenate([blocks, withins], axis=0))


def fill_picks(pick_ref, side_ref, columns, r, regions, cap_rows):
    shape = (cap_rows, LANES)
    rows = slice(r * cap_rows, (r + 1) * cap_rows)
    lane = iota(shape, 1, F32).astype(BF)
    whole = jnp.broadcast_to(columns[0:cap_rows, r : r + 1], shape)
    upper = whole >= HALF // LANES
    block = jnp.where(upper, whole - HALF // LANES, whole).astype(BF)
    side_ref[rows, :] = jnp.where(upper, 1.0, jnp.where(whole < 0.0, -1.0, 0.0))
    place = regions + r
    within = jnp.broadcast_to(columns[0:cap_rows, place : place + 1], shape).astype(BF)
    one = jnp.where(lane == within, jnp.ones_like(lane), jnp.zeros_like(lane))
    for q in range(HALF // LANES):
        pick_ref[rows, q * LANES : (q + 1) * LANES] = jnp.where(
            block == jnp.asarray(q, BF), one, jnp.zeros_like(one)
        )


def flip(array):
    return jnp.transpose(array).astype(BF)


def sum_rows(rows, side):
    lower, upper = side == 0.0, side == 1.0
    return jnp.concatenate(
        [
            flip(jnp.where(lower, rows, 0.0)),
            flip(jnp.where(upper, rows, 0.0)),
            flip(jnp.where(lower, 1.0, 0.0))[0:16],
            flip(jnp.where(upper, 1.0, 0.0))[0:16],
        ],
        axis=0,
    )


def voxel_body(
    cap_rows,
    adj_far, msg_far, below_far, above_far, dense_far, weights_far, grad_far,
    turned_far, low_far, high_far, back_far,
    adj_ref, slots_ref, rows_ref, below_ref, above_ref, dense_ref, weights_ref, grad_ref,
    turned_ref, back_ref,
    table_ref, pick_ref, side_ref, shift_ref, in_sems, out_sems,
):
    pairs = (
        (adj_far, adj_ref),
        (msg_far.at[:, cap_rows : cap_rows + 16], slots_ref),
        (below_far, below_ref),
        (above_far, above_ref),
        (dense_far.at[0:2], dense_ref.at[0:2]),
        (dense_far.at[NX - 2 : NX], dense_ref.at[2:4]),
        (weights_far, weights_ref),
        (msg_far.at[:, 0:cap_rows], rows_ref),
        (grad_far, grad_ref.at[1 : NX - 1]),
    )
    copies = start_all(pairs, in_sems)
    regions, _, channels = rows_ref.shape
    total = regions * cap_rows
    copies[0].wait()
    copies[1].wait()
    columns = read_slots(cap_rows, adj_ref, slots_ref, table_ref)
    for r in range(regions):
        fill_picks(pick_ref, side_ref, columns, r, regions, cap_rows)
    for copy in copies[2:7]:
        copy.wait()
    slabs = [below_ref[...]] + [dense_ref[i] for i in range(4)] + [above_ref[...]]
    grad_ref[0], grad_ref[NX - 1] = conv_edges(shift_ref, weights_ref, slabs)
    for copy in copies[7:]:
        copy.wait()
    left = sum_rows(rows_ref[...].reshape(total, channels).astype(F32), side_ref[...])
    width = 2 * LANES
    for q in range(0, HALF, width):
        part = jnp.dot(left, pick_ref[:, q : q + width], preferred_element_type=F32)
        for h in range(2):
            at = 2 * channels + 16 * h
            denom = jnp.maximum(part[at : at + 8], 1.0)
            start = h * HALF + q
            turned_ref[:, start : start + width] = (
                part[h * channels : (h + 1) * channels] / denom[0:1]
            ).astype(BF)
            x = start // SLAB
            grad_ref[x] = grad_ref[x] / jnp.transpose(denom)[:, 0:1]
    results = start_all(
        (
            (turned_ref, turned_far),
            (turned_ref.at[:, 0:SLAB], low_far),
            (turned_ref.at[:, DENSE - SLAB : DENSE], high_far),
        ),
        out_sems,
    )
    voxel_grad = grad_ref[...].reshape(DENSE, channels).astype(BF)
    halves = jnp.concatenate([voxel_grad[0:HALF], voxel_grad[HALF:DENSE]], axis=1)
    group = regions // 4
    for n in range(4):
        r = n * group
        rows = slice(r * cap_rows, (r + group) * cap_rows)
        both = jnp.dot(pick_ref[rows, :], halves, preferred_element_type=F32)
        picked = jnp.where(side_ref[rows, :] == 1.0, both[:, channels:], both[:, 0:channels]).astype(BF)
        for i in range(group):
            back_ref[r + i] = picked[i * cap_rows : (i + 1) * cap_rows]
        part = pl.ds(r, group)
        results += start_all([(back_ref.at[part], back_far.at[part])], out_sems.at[3 + n : 4 + n])
    for copy in results:
        copy.wait()


def voxels(adjacency, msg, below, above, dense, weights, grad, cap_rows):
    regions, rows, channels = msg.shape
    segs = up_to(cap_rows, LANES) // LANES
    total = regions * cap_rows
    turned, back = (channels, DENSE), (regions, cap_rows, channels)
    face = jax.ShapeDtypeStruct((channels, SLAB), BF)
    return call(
        functools.partial(voxel_body, cap_rows),
        [
            jax.ShapeDtypeStruct(turned, BF),
            face,
            face,
            jax.ShapeDtypeStruct(back, BF),
        ],
        [adjacency, msg, below, above, dense, weights, grad],
        far=range(7),
        far_outs=range(4),
        scratch=[
            pltpu.SMEM(adjacency.shape, jnp.int32),
            pltpu.VMEM((regions, 16, channels), BF),
            pltpu.VMEM(back, BF),
            pltpu.VMEM(below.shape, BF),
            pltpu.VMEM(above.shape, BF),
            pltpu.VMEM((4, SLAB, channels), BF),
            pltpu.VMEM(weights.shape, BF),
            pltpu.VMEM((NX, SLAB, channels), F32),
            pltpu.VMEM(turned, BF),
            pltpu.VMEM(back, BF),
            pltpu.VMEM((2 * regions, segs * LANES), F32),
            pltpu.VMEM((total, HALF), BF),
            pltpu.VMEM((total, LANES), F32),
            pltpu.VMEM((3, 6, SHIFTED, channels), BF),
            pltpu.SemaphoreType.DMA((9,)),
            pltpu.SemaphoreType.DMA((7,)),
        ],
        flops=4 * total * DENSE * channels,
        limit=60,
    )


def weight_body(
    scaling, turned_ref, below_ref, above_ref, dense_ref, keep_ref, send_ref, shift_ref, all_ref
):
    channels = turned_ref.shape[0]
    slabs = [below_ref[...]] + [dense_ref[x] for x in range(NX)] + [above_ref[...]]
    for x, slab in enumerate(slabs):
        put_shifts(shift_ref, x, slab)
    left = turned_ref[...]
    for k in range(0, KOFF, 2):
        pieces = []
        for j in range(k, min(k + 2, KOFF)):
            a, b, c = j // 9, j // 3 % 3, j % 3
            window = shift_ref[c, a : a + NX, b * NZ : b * NZ + SLAB, :]
            pieces.append(window.reshape(DENSE, channels))
        right = jnp.concatenate(pieces, axis=1)
        term = jnp.dot(left, right, preferred_element_type=F32) * scaling
        for i in range(len(pieces)):
            at = (KOFF - 1 - k - i) * channels
            all_ref[at : at + channels, :] = term[:, i * channels : (i + 1) * channels]
    core = lax.rem(lax.axis_index("region"), 2)
    half = keep_ref.shape[0]
    keep_ref[...] = all_ref[pl.ds(pl.multiple_of(core * half, 16), half), :]
    send_ref[...] = all_ref[pl.ds(pl.multiple_of((1 - core) * half, 16), half), :]


def weight_terms(turned, below, above, dense, scaling):
    channels = turned.shape[0]
    half = jax.ShapeDtypeStruct((KOFF * channels // 2, channels), F32)
    return call(
        functools.partial(weight_body, scaling),
        [half, half],
        [turned, below, above, dense],
        scratch=[
            pltpu.VMEM((3, NX + 2, SHIFTED, channels), BF),
            pltpu.VMEM((KOFF * channels, channels), F32),
        ],
        flops=2 * DENSE * KOFF * channels * channels,
    )


def split_body(keep_ref, got_ref, own_ref, *sent_refs):
    rows = own_ref.shape[0]
    size = 1 + len(sent_refs)
    side = lax.rem(lax.axis_index("region") // 2, size)
    for i in range(size):
        part = pl.ds(pl.multiple_of((side ^ i) * rows, 16), rows)
        total = keep_ref[part, :] + got_ref[part, :]
        if i == 0:
            own_ref[...] = total
        else:
            sent_refs[i - 1][...] = total.astype(BF)


def split(keep, got, size):
    rows, channels = keep.shape[0] // size, keep.shape[1]
    return call(
        split_body,
        [jax.ShapeDtypeStruct((rows, channels), F32)]
        + [jax.ShapeDtypeStruct((rows, channels), BF)] * (size - 1),
        [keep, got],
    )


def unpack_body(place_ref, rows_ref, out_ref):
    regions, cap_rows, channels = rows_ref.shape
    points = out_ref.shape[0]
    total = regions * cap_rows
    place = jnp.transpose(place_ref[...])[:, 0:1].astype(jnp.int32)
    block = jnp.broadcast_to((place >> 7).astype(F32), (points, LANES)).astype(BF)
    within = jnp.broadcast_to((place & (LANES - 1)).astype(F32), (points, LANES)).astype(BF)
    lane = iota((points, LANES), 1, F32).astype(BF)
    one = jnp.where(lane == within, jnp.ones_like(lane), jnp.zeros_like(lane))
    rows = rows_ref[...].reshape(total, channels)
    chunk = 256
    for start in range(0, points, chunk):
        keep = slice(start, start + chunk)
        picks = [
            jnp.where(block[keep] == jnp.asarray(q, BF), one[keep], jnp.zeros_like(one[keep]))
            for q in range(total // LANES)
        ]
        picker = jnp.concatenate(picks, axis=1)
        out_ref[keep, :] = jnp.dot(picker, rows, preferred_element_type=F32).astype(BF)


def unpack(place, rows, points):
    regions, cap_rows, channels = rows.shape
    return call(
        unpack_body,
        [jax.ShapeDtypeStruct((points, channels), BF)],
        [place, rows],
        flops=2 * regions * cap_rows * points * channels,
    )[0]


def from_sides(low, high):
    count = lax.axis_size("region")
    up = [(i, i + 1) for i in range(count - 1)]
    down = [(j, i) for i, j in up]
    return lax.ppermute(high, "region", up), lax.ppermute(low, "region", down)


def swapped(array, bit):
    count = lax.axis_size("region")
    return lax.ppermute(array, "region", [(i, i ^ bit) for i in range(count)])


def in_order(pieces, side):
    return jnp.concatenate(
        [lax.select_n(side ^ q, *pieces) for q in range(len(pieces))], axis=0
    )


def reduce_group(term, bit, size):
    side = (lax.axis_index("region") // bit) % size
    rows = term.shape[0] // size
    parts = [lax.dynamic_slice_in_dim(term, (side ^ i) * rows, rows) for i in range(size)]
    return sum_group(parts[0], [part.astype(BF) for part in parts[1:]], bit)


def exchange_group(term, bit, size, beside):
    side = (lax.axis_index("region") // bit) % size
    term, beside = lax.optimization_barrier((term.astype(BF), beside))
    terms = gather_group(term, bit, size)
    total = lax.select_n(side, *terms).astype(F32)
    for q in range(1, size):
        total = total + lax.select_n(side ^ q, *terms).astype(F32)
    return total.astype(BF), beside


def sum_group(total, sent, bit):
    for i, part in enumerate(sent):
        total = total + swapped(part, bit * (i + 1)).astype(F32)
    return total


def gather_group(term, bit, size):
    return [term] + [swapped(term, bit * i) for i in range(1, size)]


def groups_of(count):
    found, bit = [], 2
    while bit < count:
        size = min(4, count // bit)
        found.append((bit, size))
        bit *= size
    return found


def last_body(own_ref, other_ref, out_ref):
    size, rows, channels = own_ref.shape
    me = lax.axis_index("region")
    core = lax.rem(me, 2)
    side = lax.rem(me // 2, size)
    for half, ref in ((core, own_ref), (1 - core, other_ref)):
        for i in range(size):
            at = pl.multiple_of((half * size + (side ^ i)) * rows, 16)
            out_ref[pl.ds(at, rows), :] = ref[i].astype(F32)


def last_step(own, other):
    size, rows, channels = own.shape
    return call(
        last_body,
        [jax.ShapeDtypeStruct((2 * size * rows, channels), F32)],
        [own, other],
    )[0]


def exchange(array):
    return lax.all_to_all(array, "region", split_axis=0, concat_axis=0, tiled=True)


def local(point_feats, point_owner, point_slot, adjacency, kernel, cotangent):
    regions = lax.axis_size("region")
    points, channels = point_feats.shape
    tiles, vox = cotangent.shape[0], cotangent.shape[1]
    capacity = (5 * points + 2 * regions - 1) // (2 * regions)
    cap_rows = up_to(capacity, 16)
    msg, place = pack(
        point_owner.reshape(1, points), point_slot.reshape(1, points), point_feats, regions, cap_rows
    )
    received = exchange(msg)
    cot, cot_low, cot_high = to_dense(adjacency, cotangent)
    below, above = from_sides(cot_low, cot_high)
    mirrored = jnp.transpose(kernel[::-1], (0, 2, 1)).reshape(KOFF * channels, channels)
    grad = inner_gradient(cot, mirrored)
    scaling = 1.0 / math.sqrt(tiles * regions * vox)
    turned, low, high, back = voxels(
        adjacency, received, below, above, cot, mirrored, grad, cap_rows
    )
    returned = exchange(back)
    keep, send = weight_terms(turned, below, above, cot, scaling)
    groups = groups_of(regions)
    bit, size = groups[0]
    term, *sent = split(keep, swapped(send, 1), size)
    weights = kernel.reshape(KOFF * channels, channels)
    turned, low, high, *sent = lax.optimization_barrier((turned, low, high, *sent))
    feats_below, feats_above = from_sides(low, high)
    inner = inner_forward(turned, weights)
    got = [swapped(part, bit * (i + 1)) for i, part in enumerate(sent)]
    got, returned, inner, feats_below, feats_above = lax.optimization_barrier(
        (got, returned, inner, feats_below, feats_above)
    )
    for part in got:
        term = term + part.astype(F32)
    for bit, size in groups[1:-1]:
        term = reduce_group(term, bit, size)
    bit, size = groups[-1]
    term, returned = exchange_group(term, bit, size, returned)
    grad_points = unpack(place, returned, points)
    for bit, size in groups[-2:0:-1]:
        side = (lax.axis_index("region") // bit) % size
        term = in_order(gather_group(term, bit, size), side)
    term, grad_points = lax.optimization_barrier((term, grad_points))
    out_tiles = edge_forward(adjacency, turned, feats_below, feats_above, weights, inner, tiles)
    own = jnp.stack(gather_group(term, *groups[0]))
    own, out_tiles = lax.optimization_barrier((own, out_tiles))
    grad_weight = last_step(own, swapped(own, 1)).reshape(KOFF, channels, channels)
    return out_tiles, grad_points, grad_weight


def solution(mesh):
    placed = (
        P(("groups", "region"), None),
        P(("groups", "region"), None),
        P(("groups", "region")),
        P(("groups", "region"), None),
        P(),
        P(("groups", "region"), None, None),
    )
    return jax.shard_map(
        local,
        mesh=mesh,
        in_specs=placed,
        out_specs=(
            P(("groups", "region"), None, None),
            P(("groups", "region"), None),
            P("groups", None, None),
        ),
        check_vma=False,
    )
```

```python
import functools
import math

import jax
import jax.numpy as jnp
from jax import lax
from jax.experimental import pallas as pl
from jax.experimental.pallas import tpu as pltpu
from jax.sharding import PartitionSpec as P

VX = 4
VY = 4
VZ = 8
GY = 4
GZ = 2
SX = 2
KOFF = 27
NY = GY * VY
NZ = GZ * VZ
NX = SX * VX
SLAB = NY * NZ
DENSE = NX * SLAB
HALF = DENSE // 2
LANES = 128
BF = jnp.bfloat16
F32 = jnp.float32
VMEM = pl.BlockSpec(memory_space=pltpu.VMEM)
SMEM = pl.BlockSpec(memory_space=pltpu.SMEM)
FAR = pl.BlockSpec(memory_space=pltpu.HBM)
MIB = 1024 * 1024


def up_to(value, unit):
    return (value + unit - 1) // unit * unit


def iota(shape, dim, dtype=jnp.int32):
    return lax.broadcasted_iota(jnp.int32, shape, dim).astype(dtype)


def call(body, outs, args, smem=(), far=(), far_outs=(), scratch=(), flops=0, limit=16, quick=False):
    moved = sum(math.prod(o.shape) * o.dtype.itemsize for o in outs)
    moved += sum(math.prod(a.shape) * a.dtype.itemsize for a in args)
    if quick:
        flops, moved = 0, 1024
    return pl.pallas_call(
        body,
        out_shape=outs,
        in_specs=[SMEM if i in smem else FAR if i in far else VMEM for i in range(len(args))],
        out_specs=[FAR if i in far_outs else VMEM for i in range(len(outs))],
        scratch_shapes=list(scratch),
        compiler_params=pltpu.CompilerParams(vmem_limit_bytes=limit * MIB),
        cost_estimate=pl.CostEstimate(flops=flops, bytes_accessed=moved, transcendentals=0),
    )(*args)


def start_all(pairs, sems):
    copies = [pltpu.make_async_copy(a, b, sems.at[i]) for i, (a, b) in enumerate(pairs)]
    for copy in copies:
        copy.start()
    return copies


def this_core():
    return lax.rem(lax.axis_index("region"), 2)


def in_place(dense_ref, near_ref, away_ref):
    first = this_core() == 0
    near, away = near_ref[...], away_ref[...]
    before, after = jnp.where(first, away, near), jnp.where(first, near, away)
    return [before] + [dense_ref[x] for x in range(dense_ref.shape[0])] + [after]


def corner(adj_ref, t, lowest):
    tiles = adj_ref.shape[0]
    left = adj_ref[t, 4]
    layer = jnp.where((left >= lowest) & (left < lowest + tiles), 1, 0)
    before = adj_ref[t, 10]
    second = adj_ref[jnp.clip(before - lowest, 0, tiles - 1), 10] < 0
    inner = jnp.where(second, 1, 2)
    across = jnp.where(before < 0, 0, jnp.where(adj_ref[t, 16] < 0, GY - 1, inner))
    height = jnp.where(adj_ref[t, 12] >= 0, 1, 0)
    return layer * VX, across * VY, height * VZ


def pack_body(
    cap_rows, owner_far, slot_far, feats_far, msg_ref, place_ref, table_ref, owner_ref, slot_ref, feats_ref, sems
):
    regions = msg_ref.shape[0]
    points = feats_ref.shape[0]
    pairs = ((owner_far, owner_ref), (slot_far, slot_ref), (feats_far, feats_ref))
    copies = [pltpu.make_async_copy(a, b, sems.at[i]) for i, (a, b) in enumerate(pairs)]
    for copy in copies:
        copy.start()
    copies[0].wait()
    copies[1].wait()
    segs = up_to(cap_rows, LANES) // LANES
    owner = owner_ref[...]
    slot = slot_ref[...]
    mine = iota((regions, points), 0) == owner
    marks = jnp.where(mine, 1.0, 0.0)
    marks_bf = marks.astype(BF)
    earlier = jnp.where(iota((LANES, LANES), 0) < iota((LANES, LANES), 1), 1.0, 0.0).astype(BF)
    carry = jnp.zeros((regions, 1), F32)
    ranks = []
    for start in range(0, points, LANES):
        seg = marks[:, start : start + LANES]
        pre = jnp.dot(marks_bf[:, start : start + LANES], earlier, preferred_element_type=F32)
        ranks.append(jnp.sum((pre + carry) * seg, axis=0, keepdims=True))
        carry = carry + jnp.sum(seg, axis=1, keepdims=True)
    rank = jnp.concatenate(ranks, axis=1).astype(jnp.int32)
    place = owner * cap_rows + rank
    place_ref[...] = jnp.broadcast_to(place, (8, points)).astype(F32)
    block = jnp.broadcast_to((place >> 7).astype(F32), (LANES, points)).astype(BF)
    within = jnp.broadcast_to((place & (LANES - 1)).astype(F32), (LANES, points)).astype(BF)
    row = iota((LANES, points), 0, F32).astype(BF)
    one = jnp.where(row == within, jnp.ones_like(row), jnp.zeros_like(row))
    copies[2].wait()
    feats = feats_ref[...]
    chunk = math.lcm(cap_rows, LANES)
    for start in range(0, regions * cap_rows, chunk):
        picks = [
            jnp.where(block == jnp.asarray(q, BF), one, jnp.zeros_like(one))
            for q in range(start // LANES, (start + chunk) // LANES)
        ]
        picker = jnp.concatenate(picks, axis=0)
        rows = jnp.dot(picker, feats, preferred_element_type=F32).astype(BF)
        for i in range(chunk // cap_rows):
            msg_ref[start // cap_rows + i, 0:cap_rows, :] = rows[i * cap_rows : (i + 1) * cap_rows]
    high = jnp.where(mine, (slot >> 7) + 1, 0).astype(F32)
    low = jnp.where(mine, slot & (LANES - 1), 0).astype(F32)
    values = jnp.concatenate([high, low], axis=0).astype(BF)
    by_rank = jnp.where(iota((segs * LANES, points), 0) == rank, 1.0, 0.0).astype(BF)
    table_ref[...] = lax.dot_general(
        values, by_rank, (((1,), (1,)), ((), ())), preferred_element_type=F32
    )
    line = iota((16, LANES), 0)
    for o in range(regions):
        tile = jnp.zeros((16, LANES), F32)
        for s in range(segs):
            lanes = slice(s * LANES, (s + 1) * LANES)
            tile = jnp.where(line == s, table_ref[o : o + 1, lanes], tile)
            tile = jnp.where(line == segs + s, table_ref[regions + o : regions + o + 1, lanes], tile)
        msg_ref[o, cap_rows : cap_rows + 16, :] = tile.astype(BF)


def pack(owner, slot, feats, regions, cap_rows):
    points, channels = feats.shape
    segs = up_to(cap_rows, LANES) // LANES
    return call(
        functools.partial(pack_body, cap_rows),
        [
            jax.ShapeDtypeStruct((regions, cap_rows + 16, channels), BF),
            jax.ShapeDtypeStruct((8, points), F32),
        ],
        [owner, slot, feats],
        far=(0, 1, 2),
        scratch=[
            pltpu.VMEM((2 * regions, segs * LANES), F32),
            pltpu.VMEM((1, points), jnp.int32),
            pltpu.VMEM((1, points), jnp.int32),
            pltpu.VMEM((points, channels), BF),
            pltpu.SemaphoreType.DMA((3,)),
        ],
        limit=60,
        flops=2 * regions * cap_rows * points * channels,
    )


def dense_body(adj_ref, bricks_ref, dense_ref, near_ref, away_ref, grid_ref):
    tiles, vox, channels = bricks_ref.shape
    lowest = lax.axis_index("region") * tiles
    core = this_core()
    for t in range(tiles):
        x, y, z = corner(adj_ref, t, lowest)
        brick = bricks_ref[t].astype(F32).reshape(VX, VY, VZ, channels)
        grid_ref[pl.ds(x, VX), pl.ds(y, VY), pl.ds(pl.multiple_of(z, VZ), VZ), :] = brick
    for x in range(NX):
        slab = grid_ref[x].reshape(SLAB, channels).astype(BF)
        dense_ref[x] = slab
    near_ref[...] = dense_ref[(1 - core) * (NX - 1)]
    away_ref[...] = dense_ref[core * (NX - 1)]


def to_dense(adjacency, bricks):
    channels = bricks.shape[2]
    face = jax.ShapeDtypeStruct((SLAB, channels), BF)
    return call(
        dense_body,
        [jax.ShapeDtypeStruct((NX, SLAB, channels), BF), face, face],
        [adjacency, bricks],
        smem=(0,),
        scratch=[pltpu.VMEM((NX, NY, NZ, channels), F32)],
    )


SHIFTED = SLAB + 2 * NZ
INNER = NX - 2


def put_shifts(shift_ref, x, slab):
    border = jnp.zeros((NZ, slab.shape[1]), BF)
    height = iota(slab.shape, 0) % NZ
    wide = slab.astype(F32)
    lower = jnp.where(height == 0, 0.0, pltpu.roll(wide, 1, 0))
    upper = jnp.where(height == NZ - 1, 0.0, pltpu.roll(wide, SLAB - 1, 0))
    for c, copy in enumerate((lower.astype(BF), slab, upper.astype(BF))):
        shift_ref[c, x, 0:NZ, :] = border
        shift_ref[c, x, NZ : NZ + SLAB, :] = copy
        shift_ref[c, x, NZ + SLAB : SHIFTED, :] = border


def conv_slab(shift_ref, weights_ref, x):
    pieces = []
    for k in range(KOFF):
        a, b, c = k // 9, k // 3 % 3, k % 3
        pieces.append(shift_ref[c, x + a, b * NZ : b * NZ + SLAB, :])
    return jnp.dot(
        jnp.concatenate(pieces, axis=1), weights_ref[...], preferred_element_type=F32
    )


def conv_slabs(count, shift_ref, weights_ref, store):
    def step(x, carry):
        store(x, conv_slab(shift_ref, weights_ref, x))
        return carry

    lax.fori_loop(0, count, step, 0)


def conv_edges(shift_ref, weights_ref, slabs):
    for i, slab in enumerate(slabs):
        put_shifts(shift_ref, i, slab)
    return conv_slab(shift_ref, weights_ref, 0), conv_slab(shift_ref, weights_ref, 3)


def inner_gradient_body(dense_ref, weights_ref, grad_ref, shift_ref):
    for x in range(NX):
        put_shifts(shift_ref, x, dense_ref[x])

    def store(x, value):
        grad_ref[x] = value

    conv_slabs(INNER, shift_ref, weights_ref, store)


def inner_gradient(dense, weights):
    channels = dense.shape[2]
    return call(
        inner_gradient_body,
        [jax.ShapeDtypeStruct((INNER, SLAB, channels), F32)],
        [dense, weights],
        scratch=[pltpu.VMEM((3, NX, SHIFTED, channels), BF)],
        flops=2 * INNER * SLAB * KOFF * channels * channels,
    )[0]


def edge_gradient_body(dense_ref, near_ref, away_ref, weights_ref, grad_ref, shift_ref):
    slabs = in_place(dense_ref, near_ref, away_ref)
    first, last = conv_edges(shift_ref, weights_ref, slabs[:3] + slabs[-3:])
    grad_ref[0] = first
    grad_ref[1] = last


def edge_gradient(dense, near, away, weights):
    channels = dense.shape[2]
    return call(
        edge_gradient_body,
        [jax.ShapeDtypeStruct((2, SLAB, channels), F32)],
        [dense, near, away, weights],
        scratch=[pltpu.VMEM((3, 6, SHIFTED, channels), BF)],
        flops=4 * SLAB * KOFF * channels * channels,
    )[0]


def upright(turned):
    return jnp.transpose(turned.astype(F32)).astype(BF)


def inner_forward_body(turned_far, weights_far, out_ref, shift_ref, turned_ref, weights_ref, sems):
    turned_in = pltpu.make_async_copy(turned_far, turned_ref, sems.at[0])
    weights_in = pltpu.make_async_copy(weights_far, weights_ref, sems.at[1])
    turned_in.start()
    weights_in.start()
    turned_in.wait()
    for x in range(NX):
        put_shifts(shift_ref, x, upright(turned_ref[:, x * SLAB : (x + 1) * SLAB]))
    weights_in.wait()

    def store(x, value):
        out_ref[x] = value.astype(BF)

    conv_slabs(INNER, shift_ref, weights_ref, store)


def inner_forward(turned, weights):
    channels = turned.shape[0]
    return call(
        inner_forward_body,
        [jax.ShapeDtypeStruct((INNER, SLAB, channels), BF)],
        [turned, weights],
        far=(0, 1),
        scratch=[
            pltpu.VMEM((3, NX, SHIFTED, channels), BF),
            pltpu.VMEM(turned.shape, BF),
            pltpu.VMEM(weights.shape, BF),
            pltpu.SemaphoreType.DMA((2,)),
        ],
        flops=2 * INNER * SLAB * KOFF * channels * channels,
        limit=20,
        quick=True,
    )[0]


def edge_forward_body(
    adj_ref, turned_far, near_ref, away_ref, weights_far, inner_far, out_ref,
    shift_ref, grid_ref, turned_ref, weights_ref, inner_ref, sems,
):
    ends = ((0, 2 * SLAB), (DENSE - 2 * SLAB, DENSE))
    copies = [
        pltpu.make_async_copy(turned_far.at[:, a:b], turned_ref.at[i], sems.at[i])
        for i, (a, b) in enumerate(ends)
    ]
    copies.append(pltpu.make_async_copy(weights_far, weights_ref, sems.at[2]))
    copies.append(pltpu.make_async_copy(inner_far, inner_ref, sems.at[3]))
    for copy in copies:
        copy.start()
    tiles, vox, channels = out_ref.shape
    lowest = lax.axis_index("region") * tiles
    first = this_core() == 0
    near, away = near_ref[...], away_ref[...]
    before = upright(jnp.where(first, away, near))
    after = upright(jnp.where(first, near, away))
    for copy in copies:
        copy.wait()
    own = [upright(turned_ref[i, :, j * SLAB : (j + 1) * SLAB]) for i in range(2) for j in range(2)]
    first, last = conv_edges(shift_ref, weights_ref, [before] + own + [after])
    grid_ref[0] = first.reshape(NY, NZ, channels)
    grid_ref[NX - 1] = last.reshape(NY, NZ, channels)
    for x in range(INNER):
        grid_ref[x + 1] = inner_ref[x].astype(F32).reshape(NY, NZ, channels)
    for t in range(tiles):
        x, y, z = corner(adj_ref, t, lowest)
        brick = grid_ref[pl.ds(x, VX), pl.ds(y, VY), pl.ds(pl.multiple_of(z, VZ), VZ), :]
        out_ref[t] = brick.reshape(vox, channels).astype(BF)


def edge_forward(adjacency, turned, near, away, weights, inner, tiles):
    channels = turned.shape[0]
    return call(
        edge_forward_body,
        [jax.ShapeDtypeStruct((tiles, VX * VY * VZ, channels), BF)],
        [adjacency, turned, near, away, weights, inner],
        smem=(0,),
        far=(1, 4, 5),
        scratch=[
            pltpu.VMEM((3, 6, SHIFTED, channels), BF),
            pltpu.VMEM((NX, NY, NZ, channels), F32),
            pltpu.VMEM((2, channels, 2 * SLAB), BF),
            pltpu.VMEM(weights.shape, BF),
            pltpu.VMEM(inner.shape, BF),
            pltpu.SemaphoreType.DMA((4,)),
        ],
        flops=4 * SLAB * KOFF * channels * channels,
        limit=20,
    )[0]


def read_slots(cap_rows, adj_ref, slots_ref, table_ref):
    regions = slots_ref.shape[0]
    tiles = adj_ref.shape[0]
    segs = up_to(cap_rows, LANES) // LANES
    lowest = lax.axis_index("region") * tiles
    for r in range(regions):
        tile = slots_ref[r].astype(F32)
        for s in range(segs):
            lanes = slice(s * LANES, (s + 1) * LANES)
            table_ref[r : r + 1, lanes] = tile[s : s + 1]
            table_ref[regions + r : regions + r + 1, lanes] = tile[segs + s : segs + s + 1]
    high = table_ref[0:regions, :].astype(jnp.int32)
    low = table_ref[regions : 2 * regions, :].astype(jnp.int32)
    start = jnp.full(high.shape, -DENSE, jnp.int32)
    for t in range(tiles):
        x, y, z = corner(adj_ref, t, lowest)
        start = jnp.where(high == t + 1, (x * NY + y) * NZ + z, start)
    inside = ((low >> 5) * NY + ((low >> 3) & 3)) * NZ + (low & 7)
    spot = jnp.where(start < 0, -LANES, start + inside)
    blocks = (spot >> 7).astype(F32)
    withins = (spot & (LANES - 1)).astype(F32)
    return jnp.transpose(jnp.concatenate([blocks, withins], axis=0))


def fill_picks(pick_ref, side_ref, columns, r, regions, cap_rows):
    shape = (cap_rows, LANES)
    rows = slice(r * cap_rows, (r + 1) * cap_rows)
    lane = iota(shape, 1, F32).astype(BF)
    whole = jnp.broadcast_to(columns[0:cap_rows, r : r + 1], shape)
    upper = whole >= HALF // LANES
    block = jnp.where(upper, whole - HALF // LANES, whole).astype(BF)
    side_ref[rows, :] = jnp.where(upper, 1.0, jnp.where(whole < 0.0, -1.0, 0.0))
    place = regions + r
    within = jnp.broadcast_to(columns[0:cap_rows, place : place + 1], shape).astype(BF)
    one = jnp.where(lane == within, jnp.ones_like(lane), jnp.zeros_like(lane))
    for q in range(HALF // LANES):
        pick_ref[rows, q * LANES : (q + 1) * LANES] = jnp.where(
            block == jnp.asarray(q, BF), one, jnp.zeros_like(one)
        )


def sum_rows(rows, side):
    across, half = jnp.transpose(rows), jnp.transpose(side)[0:1]
    parts = [jnp.where(half == h, across, 0.0) for h in (0.0, 1.0)]
    counts = [
        jnp.broadcast_to(jnp.where(half == h, 1.0, 0.0), (16, half.shape[1])) for h in (0.0, 1.0)
    ]
    return jnp.concatenate([x.astype(BF) for x in parts + counts], axis=0)


def voxel_body(
    cap_rows,
    adj_far, msg_far, grad_far, edge_far,
    turned_far, near_far, away_far, back_far,
    adj_ref, slots_ref, rows_ref, grad_ref, turned_ref, back_ref,
    table_ref, pick_ref, side_ref, in_sems, out_sems,
):
    pairs = (
        (adj_far, adj_ref),
        (msg_far.at[:, cap_rows : cap_rows + 16], slots_ref),
        (msg_far.at[:, 0:cap_rows], rows_ref),
        (grad_far, grad_ref.at[1 : NX - 1]),
        (edge_far.at[0], grad_ref.at[0]),
        (edge_far.at[1], grad_ref.at[NX - 1]),
    )
    copies = start_all(pairs, in_sems)
    regions, _, channels = rows_ref.shape
    total = regions * cap_rows
    copies[0].wait()
    copies[1].wait()
    columns = read_slots(cap_rows, adj_ref, slots_ref, table_ref)
    for r in range(regions):
        fill_picks(pick_ref, side_ref, columns, r, regions, cap_rows)
    for copy in copies[2:]:
        copy.wait()
    left = sum_rows(rows_ref[...].reshape(total, channels).astype(F32), side_ref[...])
    width = 2 * LANES
    for q in range(0, HALF, width):
        part = jnp.dot(left, pick_ref[:, q : q + width], preferred_element_type=F32)
        for h in range(2):
            at = 2 * channels + 16 * h
            denom = jnp.maximum(part[at : at + 8], 1.0)
            start = h * HALF + q
            turned_ref[:, start : start + width] = (
                part[h * channels : (h + 1) * channels] / denom[0:1]
            ).astype(BF)
            x = start // SLAB
            grad_ref[x] = grad_ref[x] / jnp.transpose(denom)[:, 0:1]
    core, last = this_core(), DENSE - SLAB
    results = start_all(
        (
            (turned_ref, turned_far),
            (turned_ref.at[:, pl.ds(pl.multiple_of((1 - core) * last, SLAB), SLAB)], near_far),
            (turned_ref.at[:, pl.ds(pl.multiple_of(core * last, SLAB), SLAB)], away_far),
        ),
        out_sems,
    )
    voxel_grad = grad_ref[...].reshape(DENSE, channels).astype(BF)
    halves = jnp.concatenate([voxel_grad[0:HALF], voxel_grad[HALF:DENSE]], axis=1)
    group = regions // 4
    for n in range(4):
        r = n * group
        rows = slice(r * cap_rows, (r + group) * cap_rows)
        both = jnp.dot(pick_ref[rows, :], halves, preferred_element_type=F32)
        picked = jnp.where(side_ref[rows, :] == 1.0, both[:, channels:], both[:, 0:channels]).astype(BF)
        for i in range(group):
            back_ref[r + i] = picked[i * cap_rows : (i + 1) * cap_rows]
        part = pl.ds(r, group)
        results += start_all([(back_ref.at[part], back_far.at[part])], out_sems.at[3 + n : 4 + n])
    for copy in results:
        copy.wait()


def voxels(adjacency, msg, grad, edge_grad, cap_rows):
    regions, rows, channels = msg.shape
    segs = up_to(cap_rows, LANES) // LANES
    total = regions * cap_rows
    turned, back = (channels, DENSE), (regions, cap_rows, channels)
    face = jax.ShapeDtypeStruct((channels, SLAB), BF)
    return call(
        functools.partial(voxel_body, cap_rows),
        [
            jax.ShapeDtypeStruct(turned, BF),
            face,
            face,
            jax.ShapeDtypeStruct(back, BF),
        ],
        [adjacency, msg, grad, edge_grad],
        far=range(4),
        far_outs=range(4),
        scratch=[
            pltpu.SMEM(adjacency.shape, jnp.int32),
            pltpu.VMEM((regions, 16, channels), BF),
            pltpu.VMEM(back, BF),
            pltpu.VMEM((NX, SLAB, channels), F32),
            pltpu.VMEM(turned, BF),
            pltpu.VMEM(back, BF),
            pltpu.VMEM((2 * regions, segs * LANES), F32),
            pltpu.VMEM((total, HALF), BF),
            pltpu.VMEM((total, LANES), F32),
            pltpu.SemaphoreType.DMA((6,)),
            pltpu.SemaphoreType.DMA((7,)),
        ],
        flops=4 * total * DENSE * channels,
        limit=60,
    )


def weight_body(
    scaling, turned_ref, near_ref, away_ref, dense_ref, keep_ref, send_ref, shift_ref, all_ref
):
    channels = turned_ref.shape[0]
    for x, slab in enumerate(in_place(dense_ref, near_ref, away_ref)):
        put_shifts(shift_ref, x, slab)
    left = turned_ref[...]
    for k in range(0, KOFF, 2):
        pieces = []
        for j in range(k, min(k + 2, KOFF)):
            a, b, c = j // 9, j // 3 % 3, j % 3
            window = shift_ref[c, a : a + NX, b * NZ : b * NZ + SLAB, :]
            pieces.append(window.reshape(DENSE, channels))
        right = jnp.concatenate(pieces, axis=1)
        term = jnp.dot(left, right, preferred_element_type=F32) * scaling
        for i in range(len(pieces)):
            at = (KOFF - 1 - k - i) * channels
            all_ref[at : at + channels, :] = term[:, i * channels : (i + 1) * channels]
    core = lax.rem(lax.axis_index("region"), 2)
    half = keep_ref.shape[0]
    keep_ref[...] = all_ref[pl.ds(pl.multiple_of(core * half, 16), half), :]
    send_ref[...] = all_ref[pl.ds(pl.multiple_of((1 - core) * half, 16), half), :]


def weight_terms(turned, near, away, dense, scaling):
    channels = turned.shape[0]
    half = jax.ShapeDtypeStruct((KOFF * channels // 2, channels), F32)
    return call(
        functools.partial(weight_body, scaling),
        [half, half],
        [turned, near, away, dense],
        scratch=[
            pltpu.VMEM((3, NX + 2, SHIFTED, channels), BF),
            pltpu.VMEM((KOFF * channels, channels), F32),
        ],
        flops=2 * DENSE * KOFF * channels * channels,
    )


def split_body(keep_ref, got_ref, own_ref, *sent_refs):
    rows = own_ref.shape[0]
    size = 1 + len(sent_refs)
    side = lax.rem(lax.axis_index("region") // 2, size)
    for i in range(size):
        part = pl.ds(pl.multiple_of((side ^ i) * rows, 16), rows)
        total = keep_ref[part, :] + got_ref[part, :]
        if i == 0:
            own_ref[...] = total
        else:
            sent_refs[i - 1][...] = total.astype(BF)


def split(keep, got, size):
    rows, channels = keep.shape[0] // size, keep.shape[1]
    return call(
        split_body,
        [jax.ShapeDtypeStruct((rows, channels), F32)]
        + [jax.ShapeDtypeStruct((rows, channels), BF)] * (size - 1),
        [keep, got],
    )


def unpack_body(place_ref, rows_ref, out_ref):
    regions, cap_rows, channels = rows_ref.shape
    points = out_ref.shape[0]
    total = regions * cap_rows
    place = jnp.transpose(place_ref[...])[:, 0:1].astype(jnp.int32)
    block = jnp.broadcast_to((place >> 7).astype(F32), (points, LANES)).astype(BF)
    within = jnp.broadcast_to((place & (LANES - 1)).astype(F32), (points, LANES)).astype(BF)
    lane = iota((points, LANES), 1, F32).astype(BF)
    one = jnp.where(lane == within, jnp.ones_like(lane), jnp.zeros_like(lane))
    rows = rows_ref[...].reshape(total, channels)
    chunk = 256
    for start in range(0, points, chunk):
        keep = slice(start, start + chunk)
        picks = [
            jnp.where(block[keep] == jnp.asarray(q, BF), one[keep], jnp.zeros_like(one[keep]))
            for q in range(total // LANES)
        ]
        picker = jnp.concatenate(picks, axis=1)
        out_ref[keep, :] = jnp.dot(picker, rows, preferred_element_type=F32).astype(BF)


def unpack(place, rows, points):
    regions, cap_rows, channels = rows.shape
    return call(
        unpack_body,
        [jax.ShapeDtypeStruct((points, channels), BF)],
        [place, rows],
        flops=2 * regions * cap_rows * points * channels,
    )[0]


def from_sides(near, away):
    count = lax.axis_size("region")
    pairs = [(i, i + 1) for i in range(1, count - 1, 2)]
    return swapped(near, 1), lax.ppermute(away, "region", pairs + [(j, i) for i, j in pairs])


def swapped(array, bit):
    count = lax.axis_size("region")
    return lax.ppermute(array, "region", [(i, i ^ bit) for i in range(count)])


def in_order(pieces, side):
    return jnp.concatenate(
        [lax.select_n(side ^ q, *pieces) for q in range(len(pieces))], axis=0
    )


def reduce_group(term, bit, size):
    side = (lax.axis_index("region") // bit) % size
    rows = term.shape[0] // size
    parts = [lax.dynamic_slice_in_dim(term, (side ^ i) * rows, rows) for i in range(size)]
    return sum_group(parts[0], [part.astype(BF) for part in parts[1:]], bit)


def exchange_group(term, bit, size, beside):
    side = (lax.axis_index("region") // bit) % size
    term, beside = lax.optimization_barrier((term.astype(BF), beside))
    terms = gather_group(term, bit, size)
    total = lax.select_n(side, *terms).astype(F32)
    for q in range(1, size):
        total = total + lax.select_n(side ^ q, *terms).astype(F32)
    return total.astype(BF), beside


def sum_group(total, sent, bit):
    for i, part in enumerate(sent):
        total = total + swapped(part, bit * (i + 1)).astype(F32)
    return total


def gather_group(term, bit, size):
    return [term] + [swapped(term, bit * i) for i in range(1, size)]


def groups_of(count):
    found, bit = [], 2
    while bit < count:
        size = min(4, count // bit)
        found.append((bit, size))
        bit *= size
    return found


def last_body(other, pieces_ref, *refs):
    out_far, wide_ref, sems = refs[-3:]
    size, rows, channels = pieces_ref.shape
    core = this_core()
    half = 1 - core if other else core
    side = lax.rem(lax.axis_index("region") // 2, size)
    copies = []
    for i in range(size):
        wide_ref[i] = pieces_ref[i].astype(F32)
        at = pl.multiple_of((half * size + (side ^ i)) * rows, 16)
        copies += start_all([(wide_ref.at[i], out_far.at[pl.ds(at, rows)])], sems.at[i : i + 1])
    for copy in copies:
        copy.wait()


def last_step(pieces, out=None):
    size, rows, channels = pieces.shape
    other = out is not None
    return pl.pallas_call(
        functools.partial(last_body, other),
        out_shape=jax.ShapeDtypeStruct((2 * size * rows, channels), F32),
        in_specs=[VMEM] + [FAR] * other,
        out_specs=FAR,
        scratch_shapes=[
            pltpu.VMEM((size, rows, channels), F32),
            pltpu.SemaphoreType.DMA((size,)),
        ],
        input_output_aliases={1: 0} if other else {},
        compiler_params=pltpu.CompilerParams(vmem_limit_bytes=16 * MIB),
        cost_estimate=pl.CostEstimate(flops=0, bytes_accessed=6 * size * rows * channels, transcendentals=0),
    )(pieces, *([out] if other else []))


def exchange(array):
    return lax.all_to_all(array, "region", split_axis=0, concat_axis=0, tiled=True)


def local(point_feats, point_owner, point_slot, adjacency, kernel, cotangent):
    regions = lax.axis_size("region")
    points, channels = point_feats.shape
    tiles, vox = cotangent.shape[0], cotangent.shape[1]
    capacity = (5 * points + 2 * regions - 1) // (2 * regions)
    cap_rows = up_to(capacity, 16)
    msg, place = pack(
        point_owner.reshape(1, points), point_slot.reshape(1, points), point_feats, regions, cap_rows
    )
    received = exchange(msg)
    cot, cot_near, cot_away = to_dense(adjacency, cotangent)
    near, away = from_sides(cot_near, cot_away)
    mirrored = jnp.transpose(kernel[::-1], (0, 2, 1)).reshape(KOFF * channels, channels)
    grad = inner_gradient(cot, mirrored)
    edge_grad = edge_gradient(cot, near, away, mirrored)
    scaling = 1.0 / math.sqrt(tiles * regions * vox)
    turned, feats_near, feats_away, back = voxels(adjacency, received, grad, edge_grad, cap_rows)
    returned = exchange(back)
    keep, send = weight_terms(turned, near, away, cot, scaling)
    groups = groups_of(regions)
    bit, size = groups[0]
    term, *sent = split(keep, swapped(send, 1), size)
    weights = kernel.reshape(KOFF * channels, channels)
    turned, feats_near, feats_away, *sent = lax.optimization_barrier(
        (turned, feats_near, feats_away, *sent)
    )
    feats_near, feats_away = from_sides(feats_near, feats_away)
    inner = inner_forward(turned, weights)
    got = [swapped(part, bit * (i + 1)) for i, part in enumerate(sent)]
    got, returned, inner, feats_near, feats_away = lax.optimization_barrier(
        (got, returned, inner, feats_near, feats_away)
    )
    for part in got:
        term = term + part.astype(F32)
    for bit, size in groups[1:-1]:
        term = reduce_group(term, bit, size)
    bit, size = groups[-1]
    term, returned = exchange_group(term, bit, size, returned)
    grad_points = unpack(place, returned, points)
    for bit, size in groups[-2:0:-1]:
        side = (lax.axis_index("region") // bit) % size
        term = in_order(gather_group(term, bit, size), side)
    term, grad_points = lax.optimization_barrier((term, grad_points))
    out_tiles = edge_forward(adjacency, turned, feats_near, feats_away, weights, inner, tiles)
    own = jnp.stack(gather_group(term, *groups[0]))
    own, out_tiles = lax.optimization_barrier((own, out_tiles))
    grad_weight = last_step(swapped(own, 1), last_step(own)).reshape(KOFF, channels, channels)
    return out_tiles, grad_points, grad_weight


def solution(mesh):
    placed = (
        P(("groups", "region"), None),
        P(("groups", "region"), None),
        P(("groups", "region")),
        P(("groups", "region"), None),
        P(),
        P(("groups", "region"), None, None),
    )
    return jax.shard_map(
        local,
        mesh=mesh,
        in_specs=placed,
        out_specs=(
            P(("groups", "region"), None, None),
            P(("groups", "region"), None),
            P("groups", None, None),
        ),
        check_vma=False,
    )
```

```python
import functools
import math

import jax
import jax.numpy as jnp
from jax import lax
from jax.experimental import pallas as pl
from jax.experimental.pallas import tpu as pltpu
from jax.sharding import PartitionSpec as P

VX = 4
VY = 4
VZ = 8
GY = 4
GZ = 2
SX = 2
KOFF = 27
NY = GY * VY
NZ = GZ * VZ
NX = SX * VX
SLAB = NY * NZ
DENSE = NX * SLAB
HALF = DENSE // 2
LANES = 128
BF = jnp.bfloat16
F32 = jnp.float32
VMEM = pl.BlockSpec(memory_space=pltpu.VMEM)
SMEM = pl.BlockSpec(memory_space=pltpu.SMEM)
FAR = pl.BlockSpec(memory_space=pltpu.HBM)
MIB = 1024 * 1024


def up_to(value, unit):
    return (value + unit - 1) // unit * unit


def iota(shape, dim, dtype=jnp.int32):
    return lax.broadcasted_iota(jnp.int32, shape, dim).astype(dtype)


def call(body, outs, args, smem=(), far=(), far_outs=(), scratch=(), flops=0, limit=16, quick=False):
    moved = sum(math.prod(o.shape) * o.dtype.itemsize for o in outs)
    moved += sum(math.prod(a.shape) * a.dtype.itemsize for a in args)
    if quick:
        flops, moved = 0, 1024
    return pl.pallas_call(
        body,
        out_shape=outs,
        in_specs=[SMEM if i in smem else FAR if i in far else VMEM for i in range(len(args))],
        out_specs=[FAR if i in far_outs else VMEM for i in range(len(outs))],
        scratch_shapes=list(scratch),
        compiler_params=pltpu.CompilerParams(vmem_limit_bytes=limit * MIB),
        cost_estimate=pl.CostEstimate(flops=flops, bytes_accessed=moved, transcendentals=0),
    )(*args)


def start_all(pairs, sems):
    copies = [pltpu.make_async_copy(a, b, sems.at[i]) for i, (a, b) in enumerate(pairs)]
    for copy in copies:
        copy.start()
    return copies


def this_core():
    return lax.rem(lax.axis_index("region"), 2)


def in_place(dense_ref, near_ref, away_ref):
    first = this_core() == 0
    near, away = near_ref[...], away_ref[...]
    before, after = jnp.where(first, away, near), jnp.where(first, near, away)
    return [before] + [dense_ref[x] for x in range(dense_ref.shape[0])] + [after]


def corner(adj_ref, t, lowest):
    tiles = adj_ref.shape[0]
    left = adj_ref[t, 4]
    layer = jnp.where((left >= lowest) & (left < lowest + tiles), 1, 0)
    before = adj_ref[t, 10]
    second = adj_ref[jnp.clip(before - lowest, 0, tiles - 1), 10] < 0
    inner = jnp.where(second, 1, 2)
    across = jnp.where(before < 0, 0, jnp.where(adj_ref[t, 16] < 0, GY - 1, inner))
    height = jnp.where(adj_ref[t, 12] >= 0, 1, 0)
    return layer * VX, across * VY, height * VZ


def pack_body(
    cap_rows, owner_far, slot_far, feats_far, msg_ref, place_ref, table_ref, owner_ref, slot_ref, feats_ref, sems
):
    regions = msg_ref.shape[0]
    points = feats_ref.shape[0]
    pairs = ((owner_far, owner_ref), (slot_far, slot_ref), (feats_far, feats_ref))
    copies = [pltpu.make_async_copy(a, b, sems.at[i]) for i, (a, b) in enumerate(pairs)]
    for copy in copies:
        copy.start()
    copies[0].wait()
    copies[1].wait()
    segs = up_to(cap_rows, LANES) // LANES
    owner = owner_ref[...]
    slot = slot_ref[...]
    mine = iota((regions, points), 0) == owner
    marks = jnp.where(mine, 1.0, 0.0)
    marks_bf = marks.astype(BF)
    earlier = jnp.where(iota((LANES, LANES), 0) < iota((LANES, LANES), 1), 1.0, 0.0).astype(BF)
    carry = jnp.zeros((regions, 1), F32)
    ranks = []
    for start in range(0, points, LANES):
        if start == points // 2:
            early = carry
        seg = marks[:, start : start + LANES]
        pre = jnp.dot(marks_bf[:, start : start + LANES], earlier, preferred_element_type=F32)
        ranks.append(jnp.sum((pre + carry) * seg, axis=0, keepdims=True))
        carry = carry + jnp.sum(seg, axis=1, keepdims=True)
    rank = jnp.concatenate(ranks, axis=1).astype(jnp.int32)
    place = owner * cap_rows + rank
    place_ref[...] = jnp.broadcast_to(place, (8, points)).astype(F32)
    block = jnp.broadcast_to((place >> 7).astype(F32), (LANES, points)).astype(BF)
    within = jnp.broadcast_to((place & (LANES - 1)).astype(F32), (LANES, points)).astype(BF)
    row = iota((LANES, points), 0, F32).astype(BF)
    one = jnp.where(row == within, jnp.ones_like(row), jnp.zeros_like(row))
    copies[2].wait()
    halves = jnp.concatenate([feats_ref[0 : points // 2], feats_ref[points // 2 : points]], axis=1)
    rank_row = iota((cap_rows, LANES), 0, F32)
    chunk = math.lcm(cap_rows, LANES)
    for start in range(0, regions * cap_rows, chunk):
        picks = [
            jnp.where(block == jnp.asarray(q, BF), one, jnp.zeros_like(one))
            for q in range(start // LANES, (start + chunk) // LANES)
        ]
        picks = [pick[:, 0 : points // 2] + pick[:, points // 2 : points] for pick in picks]
        picker = jnp.concatenate(picks, axis=0)
        both = jnp.dot(picker, halves, preferred_element_type=F32)
        for i in range(chunk // cap_rows):
            o = start // cap_rows + i
            late = rank_row >= jnp.broadcast_to(early[o : o + 1], (cap_rows, LANES))
            rows = both[i * cap_rows : (i + 1) * cap_rows]
            msg_ref[o, 0:cap_rows, :] = jnp.where(late, rows[:, LANES:], rows[:, 0:LANES]).astype(BF)
    high = jnp.where(mine, (slot >> 7) + 1, 0).astype(F32)
    low = jnp.where(mine, slot & (LANES - 1), 0).astype(F32)
    values = jnp.concatenate([high, low], axis=0).astype(BF)
    by_rank = jnp.where(iota((segs * LANES, points), 0) == rank, 1.0, 0.0).astype(BF)
    table_ref[...] = lax.dot_general(
        values, by_rank, (((1,), (1,)), ((), ())), preferred_element_type=F32
    )
    line = iota((16, LANES), 0)
    for o in range(regions):
        tile = jnp.zeros((16, LANES), F32)
        for s in range(segs):
            lanes = slice(s * LANES, (s + 1) * LANES)
            tile = jnp.where(line == s, table_ref[o : o + 1, lanes], tile)
            tile = jnp.where(line == segs + s, table_ref[regions + o : regions + o + 1, lanes], tile)
        msg_ref[o, cap_rows : cap_rows + 16, :] = tile.astype(BF)


def pack(owner, slot, feats, regions, cap_rows):
    points, channels = feats.shape
    segs = up_to(cap_rows, LANES) // LANES
    return call(
        functools.partial(pack_body, cap_rows),
        [
            jax.ShapeDtypeStruct((regions, cap_rows + 16, channels), BF),
            jax.ShapeDtypeStruct((8, points), F32),
        ],
        [owner, slot, feats],
        far=(0, 1, 2),
        scratch=[
            pltpu.VMEM((2 * regions, segs * LANES), F32),
            pltpu.VMEM((1, points), jnp.int32),
            pltpu.VMEM((1, points), jnp.int32),
            pltpu.VMEM((points, channels), BF),
            pltpu.SemaphoreType.DMA((3,)),
        ],
        limit=60,
        flops=2 * regions * cap_rows * points * channels,
    )


def dense_body(adj_ref, bricks_ref, dense_ref, near_ref, away_ref, grid_ref):
    tiles, vox, channels = bricks_ref.shape
    lowest = lax.axis_index("region") * tiles
    core = this_core()
    for t in range(tiles):
        x, y, z = corner(adj_ref, t, lowest)
        brick = bricks_ref[t].astype(F32).reshape(VX, VY, VZ, channels)
        grid_ref[pl.ds(x, VX), pl.ds(y, VY), pl.ds(pl.multiple_of(z, VZ), VZ), :] = brick
    for x in range(NX):
        slab = grid_ref[x].reshape(SLAB, channels).astype(BF)
        dense_ref[x] = slab
    near_ref[...] = dense_ref[(1 - core) * (NX - 1)]
    away_ref[...] = dense_ref[core * (NX - 1)]


def to_dense(adjacency, bricks):
    channels = bricks.shape[2]
    face = jax.ShapeDtypeStruct((SLAB, channels), BF)
    return call(
        dense_body,
        [jax.ShapeDtypeStruct((NX, SLAB, channels), BF), face, face],
        [adjacency, bricks],
        smem=(0,),
        scratch=[pltpu.VMEM((NX, NY, NZ, channels), F32)],
    )


SHIFTED = SLAB + 2 * NZ
INNER = NX - 2


def put_shifts(shift_ref, x, slab):
    border = jnp.zeros((NZ, slab.shape[1]), BF)
    height = iota(slab.shape, 0) % NZ
    wide = slab.astype(F32)
    lower = jnp.where(height == 0, 0.0, pltpu.roll(wide, 1, 0))
    upper = jnp.where(height == NZ - 1, 0.0, pltpu.roll(wide, SLAB - 1, 0))
    for c, copy in enumerate((lower.astype(BF), slab, upper.astype(BF))):
        shift_ref[c, x, 0:NZ, :] = border
        shift_ref[c, x, NZ : NZ + SLAB, :] = copy
        shift_ref[c, x, NZ + SLAB : SHIFTED, :] = border


def conv_slab(shift_ref, weights_ref, x):
    pieces = []
    for k in range(KOFF):
        a, b, c = k // 9, k // 3 % 3, k % 3
        pieces.append(shift_ref[c, x + a, b * NZ : b * NZ + SLAB, :])
    return jnp.dot(
        jnp.concatenate(pieces, axis=1), weights_ref[...], preferred_element_type=F32
    )


def conv_slabs(count, shift_ref, weights_ref, store):
    def step(x, carry):
        store(x, conv_slab(shift_ref, weights_ref, x))
        return carry

    lax.fori_loop(0, count, step, 0)


def conv_edges(shift_ref, weights_ref, slabs):
    for i, slab in enumerate(slabs):
        put_shifts(shift_ref, i, slab)
    return conv_slab(shift_ref, weights_ref, 0), conv_slab(shift_ref, weights_ref, 3)


def inner_gradient_body(dense_ref, weights_ref, grad_ref, shift_ref):
    for x in range(NX):
        put_shifts(shift_ref, x, dense_ref[x])

    def store(x, value):
        grad_ref[x] = value

    conv_slabs(INNER, shift_ref, weights_ref, store)


def inner_gradient(dense, weights):
    channels = dense.shape[2]
    return call(
        inner_gradient_body,
        [jax.ShapeDtypeStruct((INNER, SLAB, channels), F32)],
        [dense, weights],
        scratch=[pltpu.VMEM((3, NX, SHIFTED, channels), BF)],
        flops=2 * INNER * SLAB * KOFF * channels * channels,
    )[0]


def edge_gradient_body(dense_ref, near_ref, away_ref, weights_ref, grad_ref, shift_ref):
    slabs = in_place(dense_ref, near_ref, away_ref)
    first, last = conv_edges(shift_ref, weights_ref, slabs[:3] + slabs[-3:])
    grad_ref[0] = first
    grad_ref[1] = last


def edge_gradient(dense, near, away, weights):
    channels = dense.shape[2]
    return call(
        edge_gradient_body,
        [jax.ShapeDtypeStruct((2, SLAB, channels), F32)],
        [dense, near, away, weights],
        scratch=[pltpu.VMEM((3, 6, SHIFTED, channels), BF)],
        flops=4 * SLAB * KOFF * channels * channels,
    )[0]


def upright(turned):
    return jnp.transpose(turned.astype(F32)).astype(BF)


def inner_forward_body(turned_far, weights_far, out_ref, shift_ref, turned_ref, weights_ref, sems):
    turned_in = pltpu.make_async_copy(turned_far, turned_ref, sems.at[0])
    weights_in = pltpu.make_async_copy(weights_far, weights_ref, sems.at[1])
    turned_in.start()
    weights_in.start()
    turned_in.wait()
    for x in range(NX):
        put_shifts(shift_ref, x, upright(turned_ref[:, x * SLAB : (x + 1) * SLAB]))
    weights_in.wait()

    def store(x, value):
        out_ref[x] = value.astype(BF)

    conv_slabs(INNER, shift_ref, weights_ref, store)


def inner_forward(turned, weights):
    channels = turned.shape[0]
    return call(
        inner_forward_body,
        [jax.ShapeDtypeStruct((INNER, SLAB, channels), BF)],
        [turned, weights],
        far=(0, 1),
        scratch=[
            pltpu.VMEM((3, NX, SHIFTED, channels), BF),
            pltpu.VMEM(turned.shape, BF),
            pltpu.VMEM(weights.shape, BF),
            pltpu.SemaphoreType.DMA((2,)),
        ],
        flops=2 * INNER * SLAB * KOFF * channels * channels,
        limit=20,
        quick=True,
    )[0]


def edge_forward_body(
    adj_ref, turned_far, near_ref, away_ref, weights_far, inner_far, out_ref,
    shift_ref, grid_ref, turned_ref, weights_ref, inner_ref, sems,
):
    ends = ((0, 2 * SLAB), (DENSE - 2 * SLAB, DENSE))
    copies = [
        pltpu.make_async_copy(turned_far.at[:, a:b], turned_ref.at[i], sems.at[i])
        for i, (a, b) in enumerate(ends)
    ]
    copies.append(pltpu.make_async_copy(weights_far, weights_ref, sems.at[2]))
    copies.append(pltpu.make_async_copy(inner_far, inner_ref, sems.at[3]))
    for copy in copies:
        copy.start()
    tiles, vox, channels = out_ref.shape
    lowest = lax.axis_index("region") * tiles
    first = this_core() == 0
    near, away = near_ref[...], away_ref[...]
    before = upright(jnp.where(first, away, near))
    after = upright(jnp.where(first, near, away))
    for copy in copies:
        copy.wait()
    own = [upright(turned_ref[i, :, j * SLAB : (j + 1) * SLAB]) for i in range(2) for j in range(2)]
    first, last = conv_edges(shift_ref, weights_ref, [before] + own + [after])
    grid_ref[0] = first.reshape(NY, NZ, channels)
    grid_ref[NX - 1] = last.reshape(NY, NZ, channels)
    for x in range(INNER):
        grid_ref[x + 1] = inner_ref[x].astype(F32).reshape(NY, NZ, channels)
    for t in range(tiles):
        x, y, z = corner(adj_ref, t, lowest)
        brick = grid_ref[pl.ds(x, VX), pl.ds(y, VY), pl.ds(pl.multiple_of(z, VZ), VZ), :]
        out_ref[t] = brick.reshape(vox, channels).astype(BF)


def edge_forward(adjacency, turned, near, away, weights, inner, tiles):
    channels = turned.shape[0]
    return call(
        edge_forward_body,
        [jax.ShapeDtypeStruct((tiles, VX * VY * VZ, channels), BF)],
        [adjacency, turned, near, away, weights, inner],
        smem=(0,),
        far=(1, 4, 5),
        scratch=[
            pltpu.VMEM((3, 6, SHIFTED, channels), BF),
            pltpu.VMEM((NX, NY, NZ, channels), F32),
            pltpu.VMEM((2, channels, 2 * SLAB), BF),
            pltpu.VMEM(weights.shape, BF),
            pltpu.VMEM(inner.shape, BF),
            pltpu.SemaphoreType.DMA((4,)),
        ],
        flops=4 * SLAB * KOFF * channels * channels,
        limit=20,
    )[0]


def read_slots(cap_rows, adj_ref, slots_ref, table_ref):
    regions = slots_ref.shape[0]
    tiles = adj_ref.shape[0]
    segs = up_to(cap_rows, LANES) // LANES
    lowest = lax.axis_index("region") * tiles
    for r in range(regions):
        tile = slots_ref[r].astype(F32)
        for s in range(segs):
            lanes = slice(s * LANES, (s + 1) * LANES)
            table_ref[r : r + 1, lanes] = tile[s : s + 1]
            table_ref[regions + r : regions + r + 1, lanes] = tile[segs + s : segs + s + 1]
    high = table_ref[0:regions, :].astype(jnp.int32)
    low = table_ref[regions : 2 * regions, :].astype(jnp.int32)
    start = jnp.full(high.shape, -DENSE, jnp.int32)
    for t in range(tiles):
        x, y, z = corner(adj_ref, t, lowest)
        start = jnp.where(high == t + 1, (x * NY + y) * NZ + z, start)
    inside = ((low >> 5) * NY + ((low >> 3) & 3)) * NZ + (low & 7)
    spot = jnp.where(start < 0, -LANES, start + inside)
    blocks = (spot >> 7).astype(F32)
    withins = (spot & (LANES - 1)).astype(F32)
    return jnp.transpose(jnp.concatenate([blocks, withins], axis=0))


def fill_picks(pick_ref, side_ref, columns, r, regions, cap_rows):
    shape = (cap_rows, LANES)
    rows = slice(r * cap_rows, (r + 1) * cap_rows)
    lane = iota(shape, 1, F32).astype(BF)
    whole = jnp.broadcast_to(columns[0:cap_rows, r : r + 1], shape)
    upper = whole >= HALF // LANES
    block = jnp.where(upper, whole - HALF // LANES, whole).astype(BF)
    side_ref[rows, :] = jnp.where(upper, 1.0, jnp.where(whole < 0.0, -1.0, 0.0))
    place = regions + r
    within = jnp.broadcast_to(columns[0:cap_rows, place : place + 1], shape).astype(BF)
    one = jnp.where(lane == within, jnp.ones_like(lane), jnp.zeros_like(lane))
    for q in range(HALF // LANES):
        pick_ref[rows, q * LANES : (q + 1) * LANES] = jnp.where(
            block == jnp.asarray(q, BF), one, jnp.zeros_like(one)
        )


def sum_rows(rows, side):
    across, half = jnp.transpose(rows), jnp.transpose(side)[0:1]
    parts = [jnp.where(half == h, across, 0.0) for h in (0.0, 1.0)]
    counts = [
        jnp.broadcast_to(jnp.where(half == h, 1.0, 0.0), (16, half.shape[1])) for h in (0.0, 1.0)
    ]
    return jnp.concatenate([x.astype(BF) for x in parts + counts], axis=0)


def voxel_body(
    cap_rows,
    adj_far, msg_far, grad_far, edge_far,
    turned_far, near_far, away_far, back_far,
    adj_ref, slots_ref, rows_ref, grad_ref, turned_ref, back_ref,
    table_ref, pick_ref, side_ref, in_sems, out_sems,
):
    pairs = (
        (adj_far, adj_ref),
        (msg_far.at[:, cap_rows : cap_rows + 16], slots_ref),
        (msg_far.at[:, 0:cap_rows], rows_ref),
        (grad_far, grad_ref.at[1 : NX - 1]),
        (edge_far.at[0], grad_ref.at[0]),
        (edge_far.at[1], grad_ref.at[NX - 1]),
    )
    copies = start_all(pairs, in_sems)
    regions, _, channels = rows_ref.shape
    total = regions * cap_rows
    copies[0].wait()
    copies[1].wait()
    columns = read_slots(cap_rows, adj_ref, slots_ref, table_ref)
    for r in range(regions):
        fill_picks(pick_ref, side_ref, columns, r, regions, cap_rows)
    for copy in copies[2:]:
        copy.wait()
    left = sum_rows(rows_ref[...].reshape(total, channels).astype(F32), side_ref[...])
    width = 2 * LANES
    for q in range(0, HALF, width):
        part = jnp.dot(left, pick_ref[:, q : q + width], preferred_element_type=F32)
        for h in range(2):
            at = 2 * channels + 16 * h
            denom = jnp.maximum(part[at : at + 8], 1.0)
            start = h * HALF + q
            turned_ref[:, start : start + width] = (
                part[h * channels : (h + 1) * channels] / denom[0:1]
            ).astype(BF)
            x = start // SLAB
            grad_ref[x] = grad_ref[x] / jnp.transpose(denom)[:, 0:1]
    core, last = this_core(), DENSE - SLAB
    results = start_all(
        (
            (turned_ref, turned_far),
            (turned_ref.at[:, pl.ds(pl.multiple_of((1 - core) * last, SLAB), SLAB)], near_far),
            (turned_ref.at[:, pl.ds(pl.multiple_of(core * last, SLAB), SLAB)], away_far),
        ),
        out_sems,
    )
    voxel_grad = grad_ref[...].reshape(DENSE, channels).astype(BF)
    halves = jnp.concatenate([voxel_grad[0:HALF], voxel_grad[HALF:DENSE]], axis=1)
    group = regions // 4
    for n in range(4):
        r = n * group
        rows = slice(r * cap_rows, (r + group) * cap_rows)
        both = jnp.dot(pick_ref[rows, :], halves, preferred_element_type=F32)
        picked = jnp.where(side_ref[rows, :] == 1.0, both[:, channels:], both[:, 0:channels]).astype(BF)
        for i in range(group):
            back_ref[r + i] = picked[i * cap_rows : (i + 1) * cap_rows]
        part = pl.ds(r, group)
        results += start_all([(back_ref.at[part], back_far.at[part])], out_sems.at[3 + n : 4 + n])
    for copy in results:
        copy.wait()


def voxels(adjacency, msg, grad, edge_grad, cap_rows):
    regions, rows, channels = msg.shape
    segs = up_to(cap_rows, LANES) // LANES
    total = regions * cap_rows
    turned, back = (channels, DENSE), (regions, cap_rows, channels)
    face = jax.ShapeDtypeStruct((channels, SLAB), BF)
    return call(
        functools.partial(voxel_body, cap_rows),
        [
            jax.ShapeDtypeStruct(turned, BF),
            face,
            face,
            jax.ShapeDtypeStruct(back, BF),
        ],
        [adjacency, msg, grad, edge_grad],
        far=range(4),
        far_outs=range(4),
        scratch=[
            pltpu.SMEM(adjacency.shape, jnp.int32),
            pltpu.VMEM((regions, 16, channels), BF),
            pltpu.VMEM(back, BF),
            pltpu.VMEM((NX, SLAB, channels), F32),
            pltpu.VMEM(turned, BF),
            pltpu.VMEM(back, BF),
            pltpu.VMEM((2 * regions, segs * LANES), F32),
            pltpu.VMEM((total, HALF), BF),
            pltpu.VMEM((total, LANES), F32),
            pltpu.SemaphoreType.DMA((6,)),
            pltpu.SemaphoreType.DMA((7,)),
        ],
        flops=4 * total * DENSE * channels,
        limit=60,
    )


def weight_body(
    scaling, turned_ref, near_ref, away_ref, dense_ref, keep_ref, send_ref, shift_ref, all_ref
):
    channels = turned_ref.shape[0]
    for x, slab in enumerate(in_place(dense_ref, near_ref, away_ref)):
        put_shifts(shift_ref, x, slab)
    left = turned_ref[...]
    for k in range(0, KOFF, 2):
        pieces = []
        for j in range(k, min(k + 2, KOFF)):
            a, b, c = j // 9, j // 3 % 3, j % 3
            window = shift_ref[c, a : a + NX, b * NZ : b * NZ + SLAB, :]
            pieces.append(window.reshape(DENSE, channels))
        right = jnp.concatenate(pieces, axis=1)
        term = jnp.dot(left, right, preferred_element_type=F32) * scaling
        for i in range(len(pieces)):
            at = (KOFF - 1 - k - i) * channels
            all_ref[at : at + channels, :] = term[:, i * channels : (i + 1) * channels]
    core = lax.rem(lax.axis_index("region"), 2)
    half = keep_ref.shape[0]
    keep_ref[...] = all_ref[pl.ds(pl.multiple_of(core * half, 16), half), :]
    send_ref[...] = all_ref[pl.ds(pl.multiple_of((1 - core) * half, 16), half), :]


def weight_terms(turned, near, away, dense, scaling):
    channels = turned.shape[0]
    half = jax.ShapeDtypeStruct((KOFF * channels // 2, channels), F32)
    return call(
        functools.partial(weight_body, scaling),
        [half, half],
        [turned, near, away, dense],
        scratch=[
            pltpu.VMEM((3, NX + 2, SHIFTED, channels), BF),
            pltpu.VMEM((KOFF * channels, channels), F32),
        ],
        flops=2 * DENSE * KOFF * channels * channels,
    )


def split_body(keep_ref, got_ref, own_ref, *sent_refs):
    rows = own_ref.shape[0]
    size = 1 + len(sent_refs)
    side = lax.rem(lax.axis_index("region") // 2, size)
    for i in range(size):
        part = pl.ds(pl.multiple_of((side ^ i) * rows, 16), rows)
        total = keep_ref[part, :] + got_ref[part, :]
        if i == 0:
            own_ref[...] = total
        else:
            sent_refs[i - 1][...] = total.astype(BF)


def split(keep, got, size):
    rows, channels = keep.shape[0] // size, keep.shape[1]
    return call(
        split_body,
        [jax.ShapeDtypeStruct((rows, channels), F32)]
        + [jax.ShapeDtypeStruct((rows, channels), BF)] * (size - 1),
        [keep, got],
    )


def unpack_body(place_ref, rows_ref, out_ref):
    regions, cap_rows, channels = rows_ref.shape
    points = out_ref.shape[0]
    total = regions * cap_rows
    place = jnp.transpose(place_ref[...])[:, 0:1].astype(jnp.int32)
    block = jnp.broadcast_to((place >> 7).astype(F32), (points, LANES)).astype(BF)
    within = jnp.broadcast_to((place & (LANES - 1)).astype(F32), (points, LANES)).astype(BF)
    lane = iota((points, LANES), 1, F32).astype(BF)
    one = jnp.where(lane == within, jnp.ones_like(lane), jnp.zeros_like(lane))
    rows = rows_ref[...].reshape(total, channels)
    chunk = 256
    for start in range(0, points, chunk):
        keep = slice(start, start + chunk)
        picks = [
            jnp.where(block[keep] == jnp.asarray(q, BF), one[keep], jnp.zeros_like(one[keep]))
            for q in range(total // LANES)
        ]
        picker = jnp.concatenate(picks, axis=1)
        out_ref[keep, :] = jnp.dot(picker, rows, preferred_element_type=F32).astype(BF)


def unpack(place, rows, points):
    regions, cap_rows, channels = rows.shape
    return call(
        unpack_body,
        [jax.ShapeDtypeStruct((points, channels), BF)],
        [place, rows],
        flops=2 * regions * cap_rows * points * channels,
    )[0]


def from_sides(near, away):
    count = lax.axis_size("region")
    pairs = [(i, i + 1) for i in range(1, count - 1, 2)]
    return swapped(near, 1), lax.ppermute(away, "region", pairs + [(j, i) for i, j in pairs])


def swapped(array, bit):
    count = lax.axis_size("region")
    return lax.ppermute(array, "region", [(i, i ^ bit) for i in range(count)])


def in_order(pieces, side):
    return jnp.concatenate(
        [lax.select_n(side ^ q, *pieces) for q in range(len(pieces))], axis=0
    )


def reduce_group(term, bit, size):
    side = (lax.axis_index("region") // bit) % size
    rows = term.shape[0] // size
    parts = [lax.dynamic_slice_in_dim(term, (side ^ i) * rows, rows) for i in range(size)]
    return sum_group(parts[0], [part.astype(BF) for part in parts[1:]], bit)


def exchange_group(term, bit, size, beside):
    side = (lax.axis_index("region") // bit) % size
    term, beside = lax.optimization_barrier((term.astype(BF), beside))
    terms = gather_group(term, bit, size)
    total = lax.select_n(side, *terms).astype(F32)
    for q in range(1, size):
        total = total + lax.select_n(side ^ q, *terms).astype(F32)
    return total.astype(BF), beside


def sum_group(total, sent, bit):
    for i, part in enumerate(sent):
        total = total + swapped(part, bit * (i + 1)).astype(F32)
    return total


def gather_group(term, bit, size):
    return [term] + [swapped(term, bit * i) for i in range(1, size)]


def groups_of(count):
    found, bit = [], 2
    while bit < count:
        size = min(4, count // bit)
        found.append((bit, size))
        bit *= size
    return found


def last_body(other, pieces_ref, *refs):
    out_far, wide_ref, sems = refs[-3:]
    size, rows, channels = pieces_ref.shape
    core = this_core()
    half = 1 - core if other else core
    side = lax.rem(lax.axis_index("region") // 2, size)
    copies = []
    for i in range(size):
        wide_ref[i] = pieces_ref[i].astype(F32)
        at = pl.multiple_of((half * size + (side ^ i)) * rows, 16)
        copies += start_all([(wide_ref.at[i], out_far.at[pl.ds(at, rows)])], sems.at[i : i + 1])
    for copy in copies:
        copy.wait()


def last_step(pieces, out=None):
    size, rows, channels = pieces.shape
    other = out is not None
    return pl.pallas_call(
        functools.partial(last_body, other),
        out_shape=jax.ShapeDtypeStruct((2 * size * rows, channels), F32),
        in_specs=[VMEM] + [FAR] * other,
        out_specs=FAR,
        scratch_shapes=[
            pltpu.VMEM((size, rows, channels), F32),
            pltpu.SemaphoreType.DMA((size,)),
        ],
        input_output_aliases={1: 0} if other else {},
        compiler_params=pltpu.CompilerParams(vmem_limit_bytes=16 * MIB),
        cost_estimate=pl.CostEstimate(flops=0, bytes_accessed=6 * size * rows * channels, transcendentals=0),
    )(pieces, *([out] if other else []))


def exchange(array):
    return lax.all_to_all(array, "region", split_axis=0, concat_axis=0, tiled=True)


def local(point_feats, point_owner, point_slot, adjacency, kernel, cotangent):
    regions = lax.axis_size("region")
    points, channels = point_feats.shape
    tiles, vox = cotangent.shape[0], cotangent.shape[1]
    capacity = (5 * points + 2 * regions - 1) // (2 * regions)
    cap_rows = up_to(capacity, 16)
    msg, place = pack(
        point_owner.reshape(1, points), point_slot.reshape(1, points), point_feats, regions, cap_rows
    )
    received = exchange(msg)
    cot, cot_near, cot_away = to_dense(adjacency, cotangent)
    near, away = from_sides(cot_near, cot_away)
    mirrored = jnp.transpose(kernel[::-1], (0, 2, 1)).reshape(KOFF * channels, channels)
    grad = inner_gradient(cot, mirrored)
    edge_grad = edge_gradient(cot, near, away, mirrored)
    scaling = 1.0 / math.sqrt(tiles * regions * vox)
    turned, feats_near, feats_away, back = voxels(adjacency, received, grad, edge_grad, cap_rows)
    returned = exchange(back)
    keep, send = weight_terms(turned, near, away, cot, scaling)
    groups = groups_of(regions)
    bit, size = groups[0]
    term, *sent = split(keep, swapped(send, 1), size)
    weights = kernel.reshape(KOFF * channels, channels)
    turned, feats_near, feats_away, *sent = lax.optimization_barrier(
        (turned, feats_near, feats_away, *sent)
    )
    feats_near, feats_away = from_sides(feats_near, feats_away)
    inner = inner_forward(turned, weights)
    got = [swapped(part, bit * (i + 1)) for i, part in enumerate(sent)]
    got, returned, inner, feats_near, feats_away = lax.optimization_barrier(
        (got, returned, inner, feats_near, feats_away)
    )
    for part in got:
        term = term + part.astype(F32)
    for bit, size in groups[1:-1]:
        term = reduce_group(term, bit, size)
    bit, size = groups[-1]
    term, returned = exchange_group(term, bit, size, returned)
    grad_points = unpack(place, returned, points)
    for bit, size in groups[-2:0:-1]:
        side = (lax.axis_index("region") // bit) % size
        term = in_order(gather_group(term, bit, size), side)
    term, grad_points = lax.optimization_barrier((term, grad_points))
    out_tiles = edge_forward(adjacency, turned, feats_near, feats_away, weights, inner, tiles)
    own = jnp.stack(gather_group(term, *groups[0]))
    own, out_tiles = lax.optimization_barrier((own, out_tiles))
    grad_weight = last_step(swapped(own, 1), last_step(own)).reshape(KOFF, channels, channels)
    return out_tiles, grad_points, grad_weight


def solution(mesh):
    placed = (
        P(("groups", "region"), None),
        P(("groups", "region"), None),
        P(("groups", "region")),
        P(("groups", "region"), None),
        P(),
        P(("groups", "region"), None, None),
    )
    return jax.shard_map(
        local,
        mesh=mesh,
        in_specs=placed,
        out_specs=(
            P(("groups", "region"), None, None),
            P(("groups", "region"), None),
            P("groups", None, None),
        ),
        check_vma=False,
    )
```

```python
import functools
import math

import jax
import jax.numpy as jnp
from jax import lax
from jax.experimental import pallas as pl
from jax.experimental.pallas import tpu as pltpu
from jax.sharding import PartitionSpec as P

VX = 4
VY = 4
VZ = 8
GY = 4
GZ = 2
SX = 2
KOFF = 27
NY = GY * VY
NZ = GZ * VZ
NX = SX * VX
SLAB = NY * NZ
DENSE = NX * SLAB
HALF = DENSE // 2
LANES = 128
BF = jnp.bfloat16
F32 = jnp.float32
VMEM = pl.BlockSpec(memory_space=pltpu.VMEM)
SMEM = pl.BlockSpec(memory_space=pltpu.SMEM)
FAR = pl.BlockSpec(memory_space=pltpu.HBM)
MIB = 1024 * 1024


def up_to(value, unit):
    return (value + unit - 1) // unit * unit


def iota(shape, dim, dtype=jnp.int32):
    return lax.broadcasted_iota(jnp.int32, shape, dim).astype(dtype)


def call(body, outs, args, smem=(), far=(), far_outs=(), scratch=(), flops=0, limit=16, quick=False):
    moved = sum(math.prod(o.shape) * o.dtype.itemsize for o in outs)
    moved += sum(math.prod(a.shape) * a.dtype.itemsize for a in args)
    if quick:
        flops, moved = 0, 1024
    return pl.pallas_call(
        body,
        out_shape=outs,
        in_specs=[SMEM if i in smem else FAR if i in far else VMEM for i in range(len(args))],
        out_specs=[FAR if i in far_outs else VMEM for i in range(len(outs))],
        scratch_shapes=list(scratch),
        compiler_params=pltpu.CompilerParams(vmem_limit_bytes=limit * MIB),
        cost_estimate=pl.CostEstimate(flops=flops, bytes_accessed=moved, transcendentals=0),
    )(*args)


def start_all(pairs, sems):
    copies = [pltpu.make_async_copy(a, b, sems.at[i]) for i, (a, b) in enumerate(pairs)]
    for copy in copies:
        copy.start()
    return copies


def this_core():
    return lax.rem(lax.axis_index("region"), 2)


def in_place(dense_ref, near_ref, away_ref):
    first = this_core() == 0
    near, away = near_ref[...], away_ref[...]
    before, after = jnp.where(first, away, near), jnp.where(first, near, away)
    return [before] + [dense_ref[x] for x in range(dense_ref.shape[0])] + [after]


def corner(adj_ref, t, lowest):
    tiles = adj_ref.shape[0]
    left = adj_ref[t, 4]
    layer = jnp.where((left >= lowest) & (left < lowest + tiles), 1, 0)
    before = adj_ref[t, 10]
    second = adj_ref[jnp.clip(before - lowest, 0, tiles - 1), 10] < 0
    inner = jnp.where(second, 1, 2)
    across = jnp.where(before < 0, 0, jnp.where(adj_ref[t, 16] < 0, GY - 1, inner))
    height = jnp.where(adj_ref[t, 12] >= 0, 1, 0)
    return layer * VX, across * VY, height * VZ


def pack_body(
    cap_rows, owner_far, slot_far, feats_far, msg_ref, place_ref, table_ref, owner_ref, slot_ref, feats_ref, sems
):
    regions = msg_ref.shape[0]
    points = feats_ref.shape[0]
    pairs = ((owner_far, owner_ref), (slot_far, slot_ref), (feats_far, feats_ref))
    copies = [pltpu.make_async_copy(a, b, sems.at[i]) for i, (a, b) in enumerate(pairs)]
    for copy in copies:
        copy.start()
    copies[0].wait()
    copies[1].wait()
    segs = up_to(cap_rows, LANES) // LANES
    owner = owner_ref[...]
    slot = slot_ref[...]
    mine = iota((regions, points), 0) == owner
    marks = jnp.where(mine, 1.0, 0.0)
    marks_bf = marks.astype(BF)
    earlier = jnp.where(iota((LANES, LANES), 0) < iota((LANES, LANES), 1), 1.0, 0.0).astype(BF)
    carry = jnp.zeros((regions, 1), F32)
    ranks = []
    for start in range(0, points, LANES):
        if start == points // 2:
            early = carry
        seg = marks[:, start : start + LANES]
        pre = jnp.dot(marks_bf[:, start : start + LANES], earlier, preferred_element_type=F32)
        ranks.append(jnp.sum((pre + carry) * seg, axis=0, keepdims=True))
        carry = carry + jnp.sum(seg, axis=1, keepdims=True)
    rank = jnp.concatenate(ranks, axis=1).astype(jnp.int32)
    place = owner * cap_rows + rank
    place_ref[...] = jnp.broadcast_to(place, (8, points)).astype(F32)
    block = jnp.broadcast_to((place >> 7).astype(F32), (LANES, points)).astype(BF)
    within = jnp.broadcast_to((place & (LANES - 1)).astype(F32), (LANES, points)).astype(BF)
    row = iota((LANES, points), 0, F32).astype(BF)
    one = jnp.where(row == within, jnp.ones_like(row), jnp.zeros_like(row))
    copies[2].wait()
    halves = jnp.concatenate([feats_ref[0 : points // 2], feats_ref[points // 2 : points]], axis=1)
    rank_row = iota((cap_rows, LANES), 0, F32)
    chunk = math.lcm(cap_rows, LANES)
    for start in range(0, regions * cap_rows, chunk):
        picks = [
            jnp.where(block == jnp.asarray(q, BF), one, jnp.zeros_like(one))
            for q in range(start // LANES, (start + chunk) // LANES)
        ]
        picks = [pick[:, 0 : points // 2] + pick[:, points // 2 : points] for pick in picks]
        picker = jnp.concatenate(picks, axis=0)
        both = jnp.dot(picker, halves, preferred_element_type=F32)
        for i in range(chunk // cap_rows):
            o = start // cap_rows + i
            late = rank_row >= jnp.broadcast_to(early[o : o + 1], (cap_rows, LANES))
            rows = both[i * cap_rows : (i + 1) * cap_rows]
            msg_ref[o, 0:cap_rows, :] = jnp.where(late, rows[:, LANES:], rows[:, 0:LANES]).astype(BF)
    high = jnp.where(mine, (slot >> 7) + 1, 0).astype(F32)
    low = jnp.where(mine, slot & (LANES - 1), 0).astype(F32)
    values = jnp.concatenate([high, low], axis=0).astype(BF)
    by_rank = jnp.where(iota((segs * LANES, points), 0) == rank, 1.0, 0.0).astype(BF)
    table_ref[...] = lax.dot_general(
        values, by_rank, (((1,), (1,)), ((), ())), preferred_element_type=F32
    )
    line = iota((16, LANES), 0)
    for o in range(regions):
        tile = jnp.zeros((16, LANES), F32)
        for s in range(segs):
            lanes = slice(s * LANES, (s + 1) * LANES)
            tile = jnp.where(line == s, table_ref[o : o + 1, lanes], tile)
            tile = jnp.where(line == segs + s, table_ref[regions + o : regions + o + 1, lanes], tile)
        msg_ref[o, cap_rows : cap_rows + 16, :] = tile.astype(BF)


def pack(owner, slot, feats, regions, cap_rows):
    points, channels = feats.shape
    segs = up_to(cap_rows, LANES) // LANES
    return call(
        functools.partial(pack_body, cap_rows),
        [
            jax.ShapeDtypeStruct((regions, cap_rows + 16, channels), BF),
            jax.ShapeDtypeStruct((8, points), F32),
        ],
        [owner, slot, feats],
        far=(0, 1, 2),
        scratch=[
            pltpu.VMEM((2 * regions, segs * LANES), F32),
            pltpu.VMEM((1, points), jnp.int32),
            pltpu.VMEM((1, points), jnp.int32),
            pltpu.VMEM((points, channels), BF),
            pltpu.SemaphoreType.DMA((3,)),
        ],
        limit=60,
        flops=2 * regions * cap_rows * points * channels,
    )


def dense_body(adj_ref, bricks_ref, dense_ref, near_ref, away_ref, grid_ref):
    tiles, vox, channels = bricks_ref.shape
    lowest = lax.axis_index("region") * tiles
    core = this_core()
    for t in range(tiles):
        x, y, z = corner(adj_ref, t, lowest)
        brick = bricks_ref[t].astype(F32).reshape(VX, VY, VZ, channels)
        grid_ref[pl.ds(x, VX), pl.ds(y, VY), pl.ds(pl.multiple_of(z, VZ), VZ), :] = brick
    for x in range(NX):
        slab = grid_ref[x].reshape(SLAB, channels).astype(BF)
        dense_ref[x] = slab
    near_ref[...] = dense_ref[(1 - core) * (NX - 1)]
    away_ref[...] = dense_ref[core * (NX - 1)]


def to_dense(adjacency, bricks):
    channels = bricks.shape[2]
    face = jax.ShapeDtypeStruct((SLAB, channels), BF)
    return call(
        dense_body,
        [jax.ShapeDtypeStruct((NX, SLAB, channels), BF), face, face],
        [adjacency, bricks],
        smem=(0,),
        scratch=[pltpu.VMEM((NX, NY, NZ, channels), F32)],
    )


SHIFTED = SLAB + 2 * NZ
INNER = NX - 2


def put_shifts(shift_ref, x, slab):
    border = jnp.zeros((NZ, slab.shape[1]), BF)
    height = iota(slab.shape, 0) % NZ
    wide = slab.astype(F32)
    lower = jnp.where(height == 0, 0.0, pltpu.roll(wide, 1, 0))
    upper = jnp.where(height == NZ - 1, 0.0, pltpu.roll(wide, SLAB - 1, 0))
    for c, copy in enumerate((lower.astype(BF), slab, upper.astype(BF))):
        shift_ref[c, x, 0:NZ, :] = border
        shift_ref[c, x, NZ : NZ + SLAB, :] = copy
        shift_ref[c, x, NZ + SLAB : SHIFTED, :] = border


def conv_slab(shift_ref, weights_ref, x):
    pieces = []
    for k in range(KOFF):
        a, b, c = k // 9, k // 3 % 3, k % 3
        pieces.append(shift_ref[c, x + a, b * NZ : b * NZ + SLAB, :])
    return jnp.dot(
        jnp.concatenate(pieces, axis=1), weights_ref[...], preferred_element_type=F32
    )


def conv_slabs(count, shift_ref, weights_ref, store):
    def step(x, carry):
        store(x, conv_slab(shift_ref, weights_ref, x))
        return carry

    lax.fori_loop(0, count, step, 0)


def conv_edges(shift_ref, weights_ref, slabs):
    for i, slab in enumerate(slabs):
        put_shifts(shift_ref, i, slab)
    return conv_slab(shift_ref, weights_ref, 0), conv_slab(shift_ref, weights_ref, 3)


def inner_gradient_body(dense_ref, weights_ref, grad_ref, shift_ref):
    for x in range(NX):
        put_shifts(shift_ref, x, dense_ref[x])

    def store(x, value):
        grad_ref[x] = value

    conv_slabs(INNER, shift_ref, weights_ref, store)


def inner_gradient(dense, weights):
    channels = dense.shape[2]
    return call(
        inner_gradient_body,
        [jax.ShapeDtypeStruct((INNER, SLAB, channels), F32)],
        [dense, weights],
        scratch=[pltpu.VMEM((3, NX, SHIFTED, channels), BF)],
        flops=2 * INNER * SLAB * KOFF * channels * channels,
    )[0]


def edge_gradient_body(dense_ref, near_ref, away_ref, weights_ref, grad_ref, shift_ref):
    slabs = in_place(dense_ref, near_ref, away_ref)
    first, last = conv_edges(shift_ref, weights_ref, slabs[:3] + slabs[-3:])
    grad_ref[0] = first
    grad_ref[1] = last


def edge_gradient(dense, near, away, weights):
    channels = dense.shape[2]
    return call(
        edge_gradient_body,
        [jax.ShapeDtypeStruct((2, SLAB, channels), F32)],
        [dense, near, away, weights],
        scratch=[pltpu.VMEM((3, 6, SHIFTED, channels), BF)],
        flops=4 * SLAB * KOFF * channels * channels,
    )[0]


def upright(turned):
    return jnp.transpose(turned.astype(F32)).astype(BF)


def inner_forward_body(turned_far, weights_far, out_ref, shift_ref, turned_ref, weights_ref, sems):
    turned_in = pltpu.make_async_copy(turned_far, turned_ref, sems.at[0])
    weights_in = pltpu.make_async_copy(weights_far, weights_ref, sems.at[1])
    turned_in.start()
    weights_in.start()
    turned_in.wait()
    for x in range(NX):
        put_shifts(shift_ref, x, upright(turned_ref[:, x * SLAB : (x + 1) * SLAB]))
    weights_in.wait()

    def store(x, value):
        out_ref[x] = value.astype(BF)

    conv_slabs(INNER, shift_ref, weights_ref, store)


def inner_forward(turned, weights):
    channels = turned.shape[0]
    return call(
        inner_forward_body,
        [jax.ShapeDtypeStruct((INNER, SLAB, channels), BF)],
        [turned, weights],
        far=(0, 1),
        scratch=[
            pltpu.VMEM((3, NX, SHIFTED, channels), BF),
            pltpu.VMEM(turned.shape, BF),
            pltpu.VMEM(weights.shape, BF),
            pltpu.SemaphoreType.DMA((2,)),
        ],
        flops=2 * INNER * SLAB * KOFF * channels * channels,
        limit=20,
        quick=True,
    )[0]


def edge_forward_body(
    adj_ref, turned_far, near_ref, away_ref, weights_far, inner_far, out_ref,
    shift_ref, grid_ref, turned_ref, weights_ref, inner_ref, sems,
):
    ends = ((0, 2 * SLAB), (DENSE - 2 * SLAB, DENSE))
    copies = [
        pltpu.make_async_copy(turned_far.at[:, a:b], turned_ref.at[i], sems.at[i])
        for i, (a, b) in enumerate(ends)
    ]
    copies.append(pltpu.make_async_copy(weights_far, weights_ref, sems.at[2]))
    copies.append(pltpu.make_async_copy(inner_far, inner_ref, sems.at[3]))
    for copy in copies:
        copy.start()
    tiles, vox, channels = out_ref.shape
    lowest = lax.axis_index("region") * tiles
    first = this_core() == 0
    near, away = near_ref[...], away_ref[...]
    before = upright(jnp.where(first, away, near))
    after = upright(jnp.where(first, near, away))
    for copy in copies:
        copy.wait()
    own = [upright(turned_ref[i, :, j * SLAB : (j + 1) * SLAB]) for i in range(2) for j in range(2)]
    first, last = conv_edges(shift_ref, weights_ref, [before] + own + [after])
    grid_ref[0] = first.reshape(NY, NZ, channels)
    grid_ref[NX - 1] = last.reshape(NY, NZ, channels)
    for x in range(INNER):
        grid_ref[x + 1] = inner_ref[x].astype(F32).reshape(NY, NZ, channels)
    for t in range(tiles):
        x, y, z = corner(adj_ref, t, lowest)
        brick = grid_ref[pl.ds(x, VX), pl.ds(y, VY), pl.ds(pl.multiple_of(z, VZ), VZ), :]
        out_ref[t] = brick.reshape(vox, channels).astype(BF)


def edge_forward(adjacency, turned, near, away, weights, inner, tiles):
    channels = turned.shape[0]
    return call(
        edge_forward_body,
        [jax.ShapeDtypeStruct((tiles, VX * VY * VZ, channels), BF)],
        [adjacency, turned, near, away, weights, inner],
        smem=(0,),
        far=(1, 4, 5),
        scratch=[
            pltpu.VMEM((3, 6, SHIFTED, channels), BF),
            pltpu.VMEM((NX, NY, NZ, channels), F32),
            pltpu.VMEM((2, channels, 2 * SLAB), BF),
            pltpu.VMEM(weights.shape, BF),
            pltpu.VMEM(inner.shape, BF),
            pltpu.SemaphoreType.DMA((4,)),
        ],
        flops=4 * SLAB * KOFF * channels * channels,
        limit=20,
    )[0]


def read_slots(cap_rows, adj_ref, slots_ref, table_ref):
    regions = slots_ref.shape[0]
    tiles = adj_ref.shape[0]
    segs = up_to(cap_rows, LANES) // LANES
    lowest = lax.axis_index("region") * tiles
    for r in range(regions):
        tile = slots_ref[r].astype(F32)
        for s in range(segs):
            lanes = slice(s * LANES, (s + 1) * LANES)
            table_ref[r : r + 1, lanes] = tile[s : s + 1]
            table_ref[regions + r : regions + r + 1, lanes] = tile[segs + s : segs + s + 1]
    high = table_ref[0:regions, :].astype(jnp.int32)
    low = table_ref[regions : 2 * regions, :].astype(jnp.int32)
    start = jnp.full(high.shape, -DENSE, jnp.int32)
    for t in range(tiles):
        x, y, z = corner(adj_ref, t, lowest)
        start = jnp.where(high == t + 1, (x * NY + y) * NZ + z, start)
    inside = ((low >> 5) * NY + ((low >> 3) & 3)) * NZ + (low & 7)
    spot = jnp.where(start < 0, -LANES, start + inside)
    blocks = (spot >> 7).astype(F32)
    withins = (spot & (LANES - 1)).astype(F32)
    return jnp.transpose(jnp.concatenate([blocks, withins], axis=0))


def fill_picks(pick_ref, side_ref, columns, r, regions, cap_rows):
    shape = (cap_rows, LANES)
    rows = slice(r * cap_rows, (r + 1) * cap_rows)
    lane = iota(shape, 1, F32).astype(BF)
    whole = jnp.broadcast_to(columns[0:cap_rows, r : r + 1], shape)
    upper = whole >= HALF // LANES
    block = jnp.where(upper, whole - HALF // LANES, whole).astype(BF)
    side_ref[rows, :] = jnp.where(upper, 1.0, jnp.where(whole < 0.0, -1.0, 0.0))
    place = regions + r
    within = jnp.broadcast_to(columns[0:cap_rows, place : place + 1], shape).astype(BF)
    one = jnp.where(lane == within, jnp.ones_like(lane), jnp.zeros_like(lane))
    for q in range(HALF // LANES):
        pick_ref[rows, q * LANES : (q + 1) * LANES] = jnp.where(
            block == jnp.asarray(q, BF), one, jnp.zeros_like(one)
        )


def sum_rows(rows, side):
    across, half = jnp.transpose(rows), jnp.transpose(side)[0:1]
    parts = [jnp.where(half == h, across, 0.0) for h in (0.0, 1.0)]
    counts = [
        jnp.broadcast_to(jnp.where(half == h, 1.0, 0.0), (16, half.shape[1])) for h in (0.0, 1.0)
    ]
    return jnp.concatenate([x.astype(BF) for x in parts + counts], axis=0)


def voxel_body(
    cap_rows,
    adj_far, msg_far, grad_far, edge_far,
    turned_far, near_far, away_far, back_far,
    adj_ref, slots_ref, rows_ref, grad_ref, turned_ref, back_ref,
    table_ref, pick_ref, side_ref, in_sems, out_sems,
):
    pairs = (
        (adj_far, adj_ref),
        (msg_far.at[:, cap_rows : cap_rows + 16], slots_ref),
        (msg_far.at[:, 0:cap_rows], rows_ref),
        (grad_far, grad_ref.at[1 : NX - 1]),
        (edge_far.at[0], grad_ref.at[0]),
        (edge_far.at[1], grad_ref.at[NX - 1]),
    )
    copies = start_all(pairs, in_sems)
    regions, _, channels = rows_ref.shape
    total = regions * cap_rows
    copies[0].wait()
    copies[1].wait()
    columns = read_slots(cap_rows, adj_ref, slots_ref, table_ref)
    for r in range(regions):
        fill_picks(pick_ref, side_ref, columns, r, regions, cap_rows)
    for copy in copies[2:]:
        copy.wait()
    left = sum_rows(rows_ref[...].reshape(total, channels).astype(F32), side_ref[...])
    width = 2 * LANES
    for q in range(0, HALF, width):
        part = jnp.dot(left, pick_ref[:, q : q + width], preferred_element_type=F32)
        for h in range(2):
            at = 2 * channels + 16 * h
            denom = jnp.maximum(part[at : at + 8], 1.0)
            start = h * HALF + q
            turned_ref[:, start : start + width] = (
                part[h * channels : (h + 1) * channels] / denom[0:1]
            ).astype(BF)
            x = start // SLAB
            grad_ref[x] = grad_ref[x] / jnp.transpose(denom)[:, 0:1]
    core, last = this_core(), DENSE - SLAB
    results = start_all(
        (
            (turned_ref, turned_far),
            (turned_ref.at[:, pl.ds(pl.multiple_of((1 - core) * last, SLAB), SLAB)], near_far),
            (turned_ref.at[:, pl.ds(pl.multiple_of(core * last, SLAB), SLAB)], away_far),
        ),
        out_sems,
    )
    voxel_grad = grad_ref[...].reshape(DENSE, channels).astype(BF)
    halves = jnp.concatenate([voxel_grad[0:HALF], voxel_grad[HALF:DENSE]], axis=1)
    group = regions // 4
    for n in range(4):
        r = n * group
        rows = slice(r * cap_rows, (r + group) * cap_rows)
        both = jnp.dot(pick_ref[rows, :], halves, preferred_element_type=F32)
        picked = jnp.where(side_ref[rows, :] == 1.0, both[:, channels:], both[:, 0:channels]).astype(BF)
        for i in range(group):
            back_ref[r + i] = picked[i * cap_rows : (i + 1) * cap_rows]
        part = pl.ds(r, group)
        results += start_all([(back_ref.at[part], back_far.at[part])], out_sems.at[3 + n : 4 + n])
    for copy in results:
        copy.wait()


def voxels(adjacency, msg, grad, edge_grad, cap_rows):
    regions, rows, channels = msg.shape
    segs = up_to(cap_rows, LANES) // LANES
    total = regions * cap_rows
    turned, back = (channels, DENSE), (regions, cap_rows, channels)
    face = jax.ShapeDtypeStruct((channels, SLAB), BF)
    return call(
        functools.partial(voxel_body, cap_rows),
        [
            jax.ShapeDtypeStruct(turned, BF),
            face,
            face,
            jax.ShapeDtypeStruct(back, BF),
        ],
        [adjacency, msg, grad, edge_grad],
        far=range(4),
        far_outs=range(4),
        scratch=[
            pltpu.SMEM(adjacency.shape, jnp.int32),
            pltpu.VMEM((regions, 16, channels), BF),
            pltpu.VMEM(back, BF),
            pltpu.VMEM((NX, SLAB, channels), F32),
            pltpu.VMEM(turned, BF),
            pltpu.VMEM(back, BF),
            pltpu.VMEM((2 * regions, segs * LANES), F32),
            pltpu.VMEM((total, HALF), BF),
            pltpu.VMEM((total, LANES), F32),
            pltpu.SemaphoreType.DMA((6,)),
            pltpu.SemaphoreType.DMA((7,)),
        ],
        flops=4 * total * DENSE * channels,
        limit=60,
    )


def weight_body(
    scaling, turned_ref, near_ref, away_ref, dense_ref, keep_ref, send_ref, shift_ref, all_ref
):
    channels = turned_ref.shape[0]
    for x, slab in enumerate(in_place(dense_ref, near_ref, away_ref)):
        put_shifts(shift_ref, x, slab)
    left = turned_ref[...]
    for k in range(0, KOFF, 2):
        pieces = []
        for j in range(k, min(k + 2, KOFF)):
            a, b, c = j // 9, j // 3 % 3, j % 3
            window = shift_ref[c, a : a + NX, b * NZ : b * NZ + SLAB, :]
            pieces.append(window.reshape(DENSE, channels))
        right = jnp.concatenate(pieces, axis=1)
        term = jnp.dot(left, right, preferred_element_type=F32) * scaling
        for i in range(len(pieces)):
            at = (KOFF - 1 - k - i) * channels
            all_ref[at : at + channels, :] = term[:, i * channels : (i + 1) * channels]
    core = lax.rem(lax.axis_index("region"), 2)
    half = keep_ref.shape[0]
    keep_ref[...] = all_ref[pl.ds(pl.multiple_of(core * half, 16), half), :]
    send_ref[...] = all_ref[pl.ds(pl.multiple_of((1 - core) * half, 16), half), :]


def weight_terms(turned, near, away, dense, scaling):
    channels = turned.shape[0]
    half = jax.ShapeDtypeStruct((KOFF * channels // 2, channels), F32)
    return call(
        functools.partial(weight_body, scaling),
        [half, half],
        [turned, near, away, dense],
        scratch=[
            pltpu.VMEM((3, NX + 2, SHIFTED, channels), BF),
            pltpu.VMEM((KOFF * channels, channels), F32),
        ],
        flops=2 * DENSE * KOFF * channels * channels,
    )


def split_body(keep_ref, got_ref, own_ref, *sent_refs):
    rows = own_ref.shape[0]
    size = 1 + len(sent_refs)
    side = lax.rem(lax.axis_index("region") // 2, size)
    for i in range(size):
        part = pl.ds(pl.multiple_of((side ^ i) * rows, 16), rows)
        total = keep_ref[part, :] + got_ref[part, :]
        if i == 0:
            own_ref[...] = total
        else:
            sent_refs[i - 1][...] = total.astype(BF)


def split(keep, got, size):
    rows, channels = keep.shape[0] // size, keep.shape[1]
    return call(
        split_body,
        [jax.ShapeDtypeStruct((rows, channels), F32)]
        + [jax.ShapeDtypeStruct((rows, channels), BF)] * (size - 1),
        [keep, got],
    )


def unpack_body(place_ref, rows_ref, out_ref):
    regions, cap_rows, channels = rows_ref.shape
    points = out_ref.shape[0]
    total = regions * cap_rows
    place = jnp.transpose(place_ref[...])[:, 0:1].astype(jnp.int32)
    block = jnp.broadcast_to((place >> 7).astype(F32), (points, LANES)).astype(BF)
    within = jnp.broadcast_to((place & (LANES - 1)).astype(F32), (points, LANES)).astype(BF)
    lane = iota((points, LANES), 1, F32).astype(BF)
    one = jnp.where(lane == within, jnp.ones_like(lane), jnp.zeros_like(lane))
    rows = rows_ref[...].reshape(total, channels)
    chunk = 256
    for start in range(0, points, chunk):
        keep = slice(start, start + chunk)
        picks = [
            jnp.where(block[keep] == jnp.asarray(q, BF), one[keep], jnp.zeros_like(one[keep]))
            for q in range(total // LANES)
        ]
        picker = jnp.concatenate(picks, axis=1)
        out_ref[keep, :] = jnp.dot(picker, rows, preferred_element_type=F32).astype(BF)


def unpack(place, rows, points):
    regions, cap_rows, channels = rows.shape
    return call(
        unpack_body,
        [jax.ShapeDtypeStruct((points, channels), BF)],
        [place, rows],
        flops=2 * regions * cap_rows * points * channels,
    )[0]


def from_sides(near, away):
    count = lax.axis_size("region")
    pairs = [(i, i + 1) for i in range(1, count - 1, 2)]
    return swapped(near, 1), lax.ppermute(away, "region", pairs + [(j, i) for i, j in pairs])


def swapped(array, bit):
    count = lax.axis_size("region")
    return lax.ppermute(array, "region", [(i, i ^ bit) for i in range(count)])


def in_order(pieces, side):
    return jnp.concatenate(
        [lax.select_n(side ^ q, *pieces) for q in range(len(pieces))], axis=0
    )


def reduce_group(term, bit, size):
    side = (lax.axis_index("region") // bit) % size
    rows = term.shape[0] // size
    parts = [lax.dynamic_slice_in_dim(term, (side ^ i) * rows, rows) for i in range(size)]
    return sum_group(parts[0], [part.astype(BF) for part in parts[1:]], bit)


def exchange_group(term, bit, size, beside):
    side = (lax.axis_index("region") // bit) % size
    term, beside = lax.optimization_barrier((term.astype(BF), beside))
    terms = gather_group(term, bit, size)
    total = lax.select_n(side, *terms).astype(F32)
    for q in range(1, size):
        total = total + lax.select_n(side ^ q, *terms).astype(F32)
    return total.astype(BF), beside


def sum_group(total, sent, bit):
    for i, part in enumerate(sent):
        total = total + swapped(part, bit * (i + 1)).astype(F32)
    return total


def gather_group(term, bit, size):
    return [term] + [swapped(term, bit * i) for i in range(1, size)]


def groups_of(count):
    found, bit = [], 2
    while bit < count:
        size = min(4, count // bit)
        found.append((bit, size))
        bit *= size
    return found


def last_body(size, places, *refs):
    out_far, wide_ref, sems = refs[-3:]
    rows = refs[0].shape[0]
    core = this_core()
    side = lax.rem(lax.axis_index("region") // 2, size)
    copies = []
    for n, (other, i) in enumerate(places):
        wide_ref[n] = refs[n][...].astype(F32)
        half = 1 - core if other else core
        at = pl.multiple_of((half * size + (side ^ i)) * rows, 16)
        copies += start_all([(wide_ref.at[n], out_far.at[pl.ds(at, rows)])], sems.at[n : n + 1])
    for copy in copies:
        copy.wait()


def last_step(size, places, pieces, out=None):
    count, (rows, channels) = len(pieces), pieces[0].shape
    again = out is not None
    return pl.pallas_call(
        functools.partial(last_body, size, places),
        out_shape=jax.ShapeDtypeStruct((2 * size * rows, channels), F32),
        in_specs=[VMEM] * count + [FAR] * again,
        out_specs=FAR,
        scratch_shapes=[
            pltpu.VMEM((count, rows, channels), F32),
            pltpu.SemaphoreType.DMA((count,)),
        ],
        input_output_aliases={count: 0} if again else {},
        compiler_params=pltpu.CompilerParams(vmem_limit_bytes=16 * MIB),
        cost_estimate=pl.CostEstimate(
            flops=0, bytes_accessed=6 * count * rows * channels, transcendentals=0
        ),
    )(*pieces, *([out] if again else []))


def exchange(array):
    return lax.all_to_all(array, "region", split_axis=0, concat_axis=0, tiled=True)


def local(point_feats, point_owner, point_slot, adjacency, kernel, cotangent):
    regions = lax.axis_size("region")
    points, channels = point_feats.shape
    tiles, vox = cotangent.shape[0], cotangent.shape[1]
    capacity = (5 * points + 2 * regions - 1) // (2 * regions)
    cap_rows = up_to(capacity, 16)
    msg, place = pack(
        point_owner.reshape(1, points), point_slot.reshape(1, points), point_feats, regions, cap_rows
    )
    received = exchange(msg)
    cot, cot_near, cot_away = to_dense(adjacency, cotangent)
    near, away = from_sides(cot_near, cot_away)
    mirrored = jnp.transpose(kernel[::-1], (0, 2, 1)).reshape(KOFF * channels, channels)
    grad = inner_gradient(cot, mirrored)
    edge_grad = edge_gradient(cot, near, away, mirrored)
    scaling = 1.0 / math.sqrt(tiles * regions * vox)
    turned, feats_near, feats_away, back = voxels(adjacency, received, grad, edge_grad, cap_rows)
    returned = exchange(back)
    keep, send = weight_terms(turned, near, away, cot, scaling)
    groups = groups_of(regions)
    bit, size = groups[0]
    term, *sent = split(keep, swapped(send, 1), size)
    weights = kernel.reshape(KOFF * channels, channels)
    turned, feats_near, feats_away, *sent = lax.optimization_barrier(
        (turned, feats_near, feats_away, *sent)
    )
    feats_near, feats_away = from_sides(feats_near, feats_away)
    inner = inner_forward(turned, weights)
    got = [swapped(part, bit * (i + 1)) for i, part in enumerate(sent)]
    got, returned, inner, feats_near, feats_away = lax.optimization_barrier(
        (got, returned, inner, feats_near, feats_away)
    )
    for part in got:
        term = term + part.astype(F32)
    for bit, size in groups[1:-1]:
        term = reduce_group(term, bit, size)
    bit, size = groups[-1]
    term, (returned, feats_near, feats_away) = exchange_group(
        term, bit, size, (returned, feats_near, feats_away)
    )
    grad_points = unpack(place, returned, points)
    out_tiles = edge_forward(adjacency, turned, feats_near, feats_away, weights, inner, tiles)
    for bit, size in groups[-2:0:-1]:
        side = (lax.axis_index("region") // bit) % size
        term = in_order(gather_group(term, bit, size), side)
    term, grad_points, out_tiles = lax.optimization_barrier((term, grad_points, out_tiles))
    bit, size = groups[0]
    own = gather_group(term, bit, size)
    others = [swapped(piece, 1) for piece in own]
    first = [(False, i) for i in range(size)] + [(True, 0)]
    summed = last_step(size, first, own + others[:1])
    summed = last_step(size, [(True, i) for i in range(1, size)], others[1:], summed)
    grad_weight = summed.reshape(KOFF, channels, channels)
    return out_tiles, grad_points, grad_weight


def solution(mesh):
    placed = (
        P(("groups", "region"), None),
        P(("groups", "region"), None),
        P(("groups", "region")),
        P(("groups", "region"), None),
        P(),
        P(("groups", "region"), None, None),
    )
    return jax.shard_map(
        local,
        mesh=mesh,
        in_specs=placed,
        out_specs=(
            P(("groups", "region"), None, None),
            P(("groups", "region"), None),
            P("groups", None, None),
        ),
        check_vma=False,
    )
```

```python
import functools
import math

import jax
import jax.numpy as jnp
from jax import lax
from jax.experimental import pallas as pl
from jax.experimental.pallas import tpu as pltpu
from jax.sharding import PartitionSpec as P

VX = 4
VY = 4
VZ = 8
GY = 4
GZ = 2
SX = 2
KOFF = 27
NY = GY * VY
NZ = GZ * VZ
NX = SX * VX
SLAB = NY * NZ
DENSE = NX * SLAB
HALF = DENSE // 2
LANES = 128
BF = jnp.bfloat16
F32 = jnp.float32
VMEM = pl.BlockSpec(memory_space=pltpu.VMEM)
SMEM = pl.BlockSpec(memory_space=pltpu.SMEM)
FAR = pl.BlockSpec(memory_space=pltpu.HBM)
MIB = 1024 * 1024


def up_to(value, unit):
    return (value + unit - 1) // unit * unit


def iota(shape, dim, dtype=jnp.int32):
    return lax.broadcasted_iota(jnp.int32, shape, dim).astype(dtype)


def call(body, outs, args, smem=(), far=(), far_outs=(), scratch=(), flops=0, limit=16, quick=False):
    moved = sum(math.prod(o.shape) * o.dtype.itemsize for o in outs)
    moved += sum(math.prod(a.shape) * a.dtype.itemsize for a in args)
    if quick:
        flops, moved = 0, 1024
    return pl.pallas_call(
        body,
        out_shape=outs,
        in_specs=[SMEM if i in smem else FAR if i in far else VMEM for i in range(len(args))],
        out_specs=[FAR if i in far_outs else VMEM for i in range(len(outs))],
        scratch_shapes=list(scratch),
        compiler_params=pltpu.CompilerParams(vmem_limit_bytes=limit * MIB),
        cost_estimate=pl.CostEstimate(flops=flops, bytes_accessed=moved, transcendentals=0),
    )(*args)


def start_all(pairs, sems):
    copies = [pltpu.make_async_copy(a, b, sems.at[i]) for i, (a, b) in enumerate(pairs)]
    for copy in copies:
        copy.start()
    return copies


def this_core():
    return lax.rem(lax.axis_index("region"), 2)


def in_place(dense_ref, near_ref, away_ref):
    first = this_core() == 0
    near, away = near_ref[...], away_ref[...]
    before, after = jnp.where(first, away, near), jnp.where(first, near, away)
    return [before] + [dense_ref[x] for x in range(dense_ref.shape[0])] + [after]


def corner(adj_ref, t, lowest):
    tiles = adj_ref.shape[0]
    left = adj_ref[t, 4]
    layer = jnp.where((left >= lowest) & (left < lowest + tiles), 1, 0)
    before = adj_ref[t, 10]
    second = adj_ref[jnp.clip(before - lowest, 0, tiles - 1), 10] < 0
    inner = jnp.where(second, 1, 2)
    across = jnp.where(before < 0, 0, jnp.where(adj_ref[t, 16] < 0, GY - 1, inner))
    height = jnp.where(adj_ref[t, 12] >= 0, 1, 0)
    return layer * VX, across * VY, height * VZ


def pack_body(
    cap_rows, owner_far, slot_far, feats_far, msg_ref, place_ref, table_ref, owner_ref, slot_ref, feats_ref, sems
):
    regions = msg_ref.shape[0]
    points = feats_ref.shape[0]
    pairs = ((owner_far, owner_ref), (slot_far, slot_ref), (feats_far, feats_ref))
    copies = [pltpu.make_async_copy(a, b, sems.at[i]) for i, (a, b) in enumerate(pairs)]
    for copy in copies:
        copy.start()
    copies[0].wait()
    copies[1].wait()
    segs = up_to(cap_rows, LANES) // LANES
    owner = owner_ref[...]
    slot = slot_ref[...]
    mine = iota((regions, points), 0) == owner
    marks = jnp.where(mine, 1.0, 0.0)
    marks_bf = marks.astype(BF)
    earlier = jnp.where(iota((LANES, LANES), 0) < iota((LANES, LANES), 1), 1.0, 0.0).astype(BF)
    carry = jnp.zeros((regions, 1), F32)
    ranks = []
    for start in range(0, points, LANES):
        if start == points // 2:
            early = carry
        seg = marks[:, start : start + LANES]
        pre = jnp.dot(marks_bf[:, start : start + LANES], earlier, preferred_element_type=F32)
        ranks.append(jnp.sum((pre + carry) * seg, axis=0, keepdims=True))
        carry = carry + jnp.sum(seg, axis=1, keepdims=True)
    rank = jnp.concatenate(ranks, axis=1).astype(jnp.int32)
    place = owner * cap_rows + rank
    place_ref[...] = jnp.broadcast_to(place, (8, points)).astype(F32)
    block = jnp.broadcast_to((place >> 7).astype(F32), (LANES, points)).astype(BF)
    within = jnp.broadcast_to((place & (LANES - 1)).astype(F32), (LANES, points)).astype(BF)
    row = iota((LANES, points), 0, F32).astype(BF)
    one = jnp.where(row == within, jnp.ones_like(row), jnp.zeros_like(row))
    copies[2].wait()
    halves = jnp.concatenate([feats_ref[0 : points // 2], feats_ref[points // 2 : points]], axis=1)
    rank_row = iota((cap_rows, LANES), 0, F32)
    chunk = math.lcm(cap_rows, LANES)
    for start in range(0, regions * cap_rows, chunk):
        picks = [
            jnp.where(block == jnp.asarray(q, BF), one, jnp.zeros_like(one))
            for q in range(start // LANES, (start + chunk) // LANES)
        ]
        picks = [pick[:, 0 : points // 2] + pick[:, points // 2 : points] for pick in picks]
        picker = jnp.concatenate(picks, axis=0)
        both = jnp.dot(picker, halves, preferred_element_type=F32)
        for i in range(chunk // cap_rows):
            o = start // cap_rows + i
            late = rank_row >= jnp.broadcast_to(early[o : o + 1], (cap_rows, LANES))
            rows = both[i * cap_rows : (i + 1) * cap_rows]
            msg_ref[o, 0:cap_rows, :] = jnp.where(late, rows[:, LANES:], rows[:, 0:LANES]).astype(BF)
    high = jnp.where(mine, (slot >> 7) + 1, 0).astype(F32)
    low = jnp.where(mine, slot & (LANES - 1), 0).astype(F32)
    values = jnp.concatenate([high, low], axis=0).astype(BF)
    by_rank = jnp.where(iota((segs * LANES, points), 0) == rank, 1.0, 0.0).astype(BF)
    table_ref[...] = lax.dot_general(
        values, by_rank, (((1,), (1,)), ((), ())), preferred_element_type=F32
    )
    line = iota((16, LANES), 0)
    for o in range(regions):
        tile = jnp.zeros((16, LANES), F32)
        for s in range(segs):
            lanes = slice(s * LANES, (s + 1) * LANES)
            tile = jnp.where(line == s, table_ref[o : o + 1, lanes], tile)
            tile = jnp.where(line == segs + s, table_ref[regions + o : regions + o + 1, lanes], tile)
        msg_ref[o, cap_rows : cap_rows + 16, :] = tile.astype(BF)


def pack(owner, slot, feats, regions, cap_rows):
    points, channels = feats.shape
    segs = up_to(cap_rows, LANES) // LANES
    return call(
        functools.partial(pack_body, cap_rows),
        [
            jax.ShapeDtypeStruct((regions, cap_rows + 16, channels), BF),
            jax.ShapeDtypeStruct((8, points), F32),
        ],
        [owner, slot, feats],
        far=(0, 1, 2),
        scratch=[
            pltpu.VMEM((2 * regions, segs * LANES), F32),
            pltpu.VMEM((1, points), jnp.int32),
            pltpu.VMEM((1, points), jnp.int32),
            pltpu.VMEM((points, channels), BF),
            pltpu.SemaphoreType.DMA((3,)),
        ],
        limit=60,
        flops=2 * regions * cap_rows * points * channels,
    )


def dense_body(adj_ref, bricks_ref, dense_ref, near_ref, away_ref, grid_ref):
    tiles, vox, channels = bricks_ref.shape
    lowest = lax.axis_index("region") * tiles
    core = this_core()
    for t in range(tiles):
        x, y, z = corner(adj_ref, t, lowest)
        brick = bricks_ref[t].astype(F32).reshape(VX, VY, VZ, channels)
        grid_ref[pl.ds(x, VX), pl.ds(y, VY), pl.ds(pl.multiple_of(z, VZ), VZ), :] = brick
    for x in range(NX):
        slab = grid_ref[x].reshape(SLAB, channels).astype(BF)
        dense_ref[x] = slab
    near_ref[...] = dense_ref[(1 - core) * (NX - 1)]
    away_ref[...] = dense_ref[core * (NX - 1)]


def to_dense(adjacency, bricks):
    channels = bricks.shape[2]
    face = jax.ShapeDtypeStruct((SLAB, channels), BF)
    return call(
        dense_body,
        [jax.ShapeDtypeStruct((NX, SLAB, channels), BF), face, face],
        [adjacency, bricks],
        smem=(0,),
        scratch=[pltpu.VMEM((NX, NY, NZ, channels), F32)],
    )


SHIFTED = SLAB + 2 * NZ
INNER = NX - 2


def put_shifts(shift_ref, x, slab):
    border = jnp.zeros((NZ, slab.shape[1]), BF)
    height = iota(slab.shape, 0) % NZ
    wide = slab.astype(F32)
    lower = jnp.where(height == 0, 0.0, pltpu.roll(wide, 1, 0))
    upper = jnp.where(height == NZ - 1, 0.0, pltpu.roll(wide, SLAB - 1, 0))
    for c, copy in enumerate((lower.astype(BF), slab, upper.astype(BF))):
        shift_ref[c, x, 0:NZ, :] = border
        shift_ref[c, x, NZ : NZ + SLAB, :] = copy
        shift_ref[c, x, NZ + SLAB : SHIFTED, :] = border


def conv_slab(shift_ref, weights_ref, x):
    pieces = []
    for k in range(KOFF):
        a, b, c = k // 9, k // 3 % 3, k % 3
        pieces.append(shift_ref[c, x + a, b * NZ : b * NZ + SLAB, :])
    return jnp.dot(
        jnp.concatenate(pieces, axis=1), weights_ref[...], preferred_element_type=F32
    )


def conv_slabs(count, shift_ref, weights_ref, store):
    def step(x, carry):
        store(x, conv_slab(shift_ref, weights_ref, x))
        return carry

    lax.fori_loop(0, count, step, 0)


def conv_edges(shift_ref, weights_ref, slabs):
    for i, slab in enumerate(slabs):
        put_shifts(shift_ref, i, slab)
    return conv_slab(shift_ref, weights_ref, 0), conv_slab(shift_ref, weights_ref, 3)


def inner_gradient_body(dense_ref, weights_ref, grad_ref, shift_ref):
    for x in range(NX):
        put_shifts(shift_ref, x, dense_ref[x])

    def store(x, value):
        grad_ref[x] = value

    conv_slabs(INNER, shift_ref, weights_ref, store)


def inner_gradient(dense, weights):
    channels = dense.shape[2]
    return call(
        inner_gradient_body,
        [jax.ShapeDtypeStruct((INNER, SLAB, channels), F32)],
        [dense, weights],
        scratch=[pltpu.VMEM((3, NX, SHIFTED, channels), BF)],
        flops=2 * INNER * SLAB * KOFF * channels * channels,
    )[0]


def edge_gradient_body(dense_ref, near_ref, away_ref, weights_ref, grad_ref, shift_ref):
    slabs = in_place(dense_ref, near_ref, away_ref)
    first, last = conv_edges(shift_ref, weights_ref, slabs[:3] + slabs[-3:])
    grad_ref[0] = first
    grad_ref[1] = last


def edge_gradient(dense, near, away, weights):
    channels = dense.shape[2]
    return call(
        edge_gradient_body,
        [jax.ShapeDtypeStruct((2, SLAB, channels), F32)],
        [dense, near, away, weights],
        scratch=[pltpu.VMEM((3, 6, SHIFTED, channels), BF)],
        flops=4 * SLAB * KOFF * channels * channels,
    )[0]


def upright(turned):
    return jnp.transpose(turned.astype(F32)).astype(BF)


def inner_forward_body(turned_far, weights_far, out_ref, shift_ref, turned_ref, weights_ref, sems):
    turned_in = pltpu.make_async_copy(turned_far, turned_ref, sems.at[0])
    weights_in = pltpu.make_async_copy(weights_far, weights_ref, sems.at[1])
    turned_in.start()
    weights_in.start()
    turned_in.wait()
    for x in range(NX):
        put_shifts(shift_ref, x, upright(turned_ref[:, x * SLAB : (x + 1) * SLAB]))
    weights_in.wait()

    def store(x, value):
        out_ref[x] = value.astype(BF)

    conv_slabs(INNER, shift_ref, weights_ref, store)


def inner_forward(turned, weights):
    channels = turned.shape[0]
    return call(
        inner_forward_body,
        [jax.ShapeDtypeStruct((INNER, SLAB, channels), BF)],
        [turned, weights],
        far=(0, 1),
        scratch=[
            pltpu.VMEM((3, NX, SHIFTED, channels), BF),
            pltpu.VMEM(turned.shape, BF),
            pltpu.VMEM(weights.shape, BF),
            pltpu.SemaphoreType.DMA((2,)),
        ],
        flops=2 * INNER * SLAB * KOFF * channels * channels,
        limit=20,
        quick=True,
    )[0]


def edge_forward_body(
    adj_ref, turned_far, near_ref, away_ref, weights_far, inner_far, out_ref,
    shift_ref, grid_ref, turned_ref, weights_ref, inner_ref, sems,
):
    ends = ((0, 2 * SLAB), (DENSE - 2 * SLAB, DENSE))
    copies = [
        pltpu.make_async_copy(turned_far.at[:, a:b], turned_ref.at[i], sems.at[i])
        for i, (a, b) in enumerate(ends)
    ]
    copies.append(pltpu.make_async_copy(weights_far, weights_ref, sems.at[2]))
    copies.append(pltpu.make_async_copy(inner_far, inner_ref, sems.at[3]))
    for copy in copies:
        copy.start()
    tiles, vox, channels = out_ref.shape
    lowest = lax.axis_index("region") * tiles
    first = this_core() == 0
    near, away = near_ref[...], away_ref[...]
    before = upright(jnp.where(first, away, near))
    after = upright(jnp.where(first, near, away))
    for copy in copies:
        copy.wait()
    own = [upright(turned_ref[i, :, j * SLAB : (j + 1) * SLAB]) for i in range(2) for j in range(2)]
    first, last = conv_edges(shift_ref, weights_ref, [before] + own + [after])
    grid_ref[0] = first.reshape(NY, NZ, channels)
    grid_ref[NX - 1] = last.reshape(NY, NZ, channels)
    for x in range(INNER):
        grid_ref[x + 1] = inner_ref[x].astype(F32).reshape(NY, NZ, channels)
    for t in range(tiles):
        x, y, z = corner(adj_ref, t, lowest)
        brick = grid_ref[pl.ds(x, VX), pl.ds(y, VY), pl.ds(pl.multiple_of(z, VZ), VZ), :]
        out_ref[t] = brick.reshape(vox, channels).astype(BF)


def edge_forward(adjacency, turned, near, away, weights, inner, tiles):
    channels = turned.shape[0]
    return call(
        edge_forward_body,
        [jax.ShapeDtypeStruct((tiles, VX * VY * VZ, channels), BF)],
        [adjacency, turned, near, away, weights, inner],
        smem=(0,),
        far=(1, 4, 5),
        scratch=[
            pltpu.VMEM((3, 6, SHIFTED, channels), BF),
            pltpu.VMEM((NX, NY, NZ, channels), F32),
            pltpu.VMEM((2, channels, 2 * SLAB), BF),
            pltpu.VMEM(weights.shape, BF),
            pltpu.VMEM(inner.shape, BF),
            pltpu.SemaphoreType.DMA((4,)),
        ],
        flops=4 * SLAB * KOFF * channels * channels,
        limit=20,
    )[0]


def read_slots(cap_rows, adj_ref, slots_ref, table_ref):
    regions = slots_ref.shape[0]
    tiles = adj_ref.shape[0]
    segs = up_to(cap_rows, LANES) // LANES
    lowest = lax.axis_index("region") * tiles
    for r in range(regions):
        tile = slots_ref[r].astype(F32)
        for s in range(segs):
            lanes = slice(s * LANES, (s + 1) * LANES)
            table_ref[r : r + 1, lanes] = tile[s : s + 1]
            table_ref[regions + r : regions + r + 1, lanes] = tile[segs + s : segs + s + 1]
    high = table_ref[0:regions, :].astype(jnp.int32)
    low = table_ref[regions : 2 * regions, :].astype(jnp.int32)
    start = jnp.full(high.shape, -DENSE, jnp.int32)
    for t in range(tiles):
        x, y, z = corner(adj_ref, t, lowest)
        start = jnp.where(high == t + 1, (x * NY + y) * NZ + z, start)
    inside = ((low >> 5) * NY + ((low >> 3) & 3)) * NZ + (low & 7)
    spot = jnp.where(start < 0, -LANES, start + inside)
    blocks = (spot >> 7).astype(F32)
    withins = (spot & (LANES - 1)).astype(F32)
    return jnp.transpose(jnp.concatenate([blocks, withins], axis=0))


def fill_picks(pick_ref, side_ref, columns, r, regions, cap_rows):
    shape = (cap_rows, LANES)
    rows = slice(r * cap_rows, (r + 1) * cap_rows)
    lane = iota(shape, 1, F32).astype(BF)
    whole = jnp.broadcast_to(columns[0:cap_rows, r : r + 1], shape)
    upper = whole >= HALF // LANES
    block = jnp.where(upper, whole - HALF // LANES, whole).astype(BF)
    side_ref[rows, :] = jnp.where(upper, 1.0, jnp.where(whole < 0.0, -1.0, 0.0))
    place = regions + r
    within = jnp.broadcast_to(columns[0:cap_rows, place : place + 1], shape).astype(BF)
    one = jnp.where(lane == within, jnp.ones_like(lane), jnp.zeros_like(lane))
    for q in range(HALF // LANES):
        pick_ref[rows, q * LANES : (q + 1) * LANES] = jnp.where(
            block == jnp.asarray(q, BF), one, jnp.zeros_like(one)
        )


def sum_rows(rows, side):
    across, half = jnp.transpose(rows), jnp.transpose(side)[0:1]
    parts = [jnp.where(half == h, across, 0.0) for h in (0.0, 1.0)]
    counts = [
        jnp.broadcast_to(jnp.where(half == h, 1.0, 0.0), (16, half.shape[1])) for h in (0.0, 1.0)
    ]
    return jnp.concatenate([x.astype(BF) for x in parts + counts], axis=0)


def voxel_body(
    cap_rows,
    adj_far, msg_far, grad_far, edge_far,
    turned_far, near_far, away_far, back_far,
    adj_ref, slots_ref, rows_ref, grad_ref, turned_ref, back_ref,
    table_ref, pick_ref, side_ref, in_sems, out_sems,
):
    pairs = (
        (adj_far, adj_ref),
        (msg_far.at[:, cap_rows : cap_rows + 16], slots_ref),
        (msg_far.at[:, 0:cap_rows], rows_ref),
        (grad_far, grad_ref.at[1 : NX - 1]),
        (edge_far.at[0], grad_ref.at[0]),
        (edge_far.at[1], grad_ref.at[NX - 1]),
    )
    copies = start_all(pairs, in_sems)
    regions, _, channels = rows_ref.shape
    total = regions * cap_rows
    copies[0].wait()
    copies[1].wait()
    columns = read_slots(cap_rows, adj_ref, slots_ref, table_ref)
    for r in range(regions):
        fill_picks(pick_ref, side_ref, columns, r, regions, cap_rows)
    for copy in copies[2:]:
        copy.wait()
    left = sum_rows(rows_ref[...].reshape(total, channels).astype(F32), side_ref[...])
    width = 2 * LANES
    for q in range(0, HALF, width):
        part = jnp.dot(left, pick_ref[:, q : q + width], preferred_element_type=F32)
        for h in range(2):
            at = 2 * channels + 16 * h
            denom = jnp.maximum(part[at : at + 8], 1.0)
            start = h * HALF + q
            turned_ref[:, start : start + width] = (
                part[h * channels : (h + 1) * channels] / denom[0:1]
            ).astype(BF)
            x = start // SLAB
            grad_ref[x] = grad_ref[x] / jnp.transpose(denom)[:, 0:1]
    core, last = this_core(), DENSE - SLAB
    results = start_all(
        (
            (turned_ref, turned_far),
            (turned_ref.at[:, pl.ds(pl.multiple_of((1 - core) * last, SLAB), SLAB)], near_far),
            (turned_ref.at[:, pl.ds(pl.multiple_of(core * last, SLAB), SLAB)], away_far),
        ),
        out_sems,
    )
    voxel_grad = grad_ref[...].reshape(DENSE, channels).astype(BF)
    halves = jnp.concatenate([voxel_grad[0:HALF], voxel_grad[HALF:DENSE]], axis=1)
    group = regions // 4
    for n in range(4):
        r = n * group
        rows = slice(r * cap_rows, (r + group) * cap_rows)
        both = jnp.dot(pick_ref[rows, :], halves, preferred_element_type=F32)
        picked = jnp.where(side_ref[rows, :] == 1.0, both[:, channels:], both[:, 0:channels]).astype(BF)
        for i in range(group):
            back_ref[r + i] = picked[i * cap_rows : (i + 1) * cap_rows]
        part = pl.ds(r, group)
        results += start_all([(back_ref.at[part], back_far.at[part])], out_sems.at[3 + n : 4 + n])
    for copy in results:
        copy.wait()


def voxels(adjacency, msg, grad, edge_grad, cap_rows):
    regions, rows, channels = msg.shape
    segs = up_to(cap_rows, LANES) // LANES
    total = regions * cap_rows
    turned, back = (channels, DENSE), (regions, cap_rows, channels)
    face = jax.ShapeDtypeStruct((channels, SLAB), BF)
    return call(
        functools.partial(voxel_body, cap_rows),
        [
            jax.ShapeDtypeStruct(turned, BF),
            face,
            face,
            jax.ShapeDtypeStruct(back, BF),
        ],
        [adjacency, msg, grad, edge_grad],
        far=range(4),
        far_outs=range(4),
        scratch=[
            pltpu.SMEM(adjacency.shape, jnp.int32),
            pltpu.VMEM((regions, 16, channels), BF),
            pltpu.VMEM(back, BF),
            pltpu.VMEM((NX, SLAB, channels), F32),
            pltpu.VMEM(turned, BF),
            pltpu.VMEM(back, BF),
            pltpu.VMEM((2 * regions, segs * LANES), F32),
            pltpu.VMEM((total, HALF), BF),
            pltpu.VMEM((total, LANES), F32),
            pltpu.SemaphoreType.DMA((6,)),
            pltpu.SemaphoreType.DMA((7,)),
        ],
        flops=4 * total * DENSE * channels,
        limit=52,
    )


def weight_body(
    scaling, turned_ref, near_ref, away_ref, dense_ref, keep_ref, send_ref, shift_ref, all_ref
):
    channels = turned_ref.shape[0]
    for x, slab in enumerate(in_place(dense_ref, near_ref, away_ref)):
        put_shifts(shift_ref, x, slab)
    left = turned_ref[...]
    for k in range(0, KOFF, 2):
        pieces = []
        for j in range(k, min(k + 2, KOFF)):
            a, b, c = j // 9, j // 3 % 3, j % 3
            window = shift_ref[c, a : a + NX, b * NZ : b * NZ + SLAB, :]
            pieces.append(window.reshape(DENSE, channels))
        right = jnp.concatenate(pieces, axis=1)
        term = jnp.dot(left, right, preferred_element_type=F32) * scaling
        for i in range(len(pieces)):
            at = (KOFF - 1 - k - i) * channels
            all_ref[at : at + channels, :] = term[:, i * channels : (i + 1) * channels]
    core = lax.rem(lax.axis_index("region"), 2)
    half = keep_ref.shape[0]
    keep_ref[...] = all_ref[pl.ds(pl.multiple_of(core * half, 16), half), :]
    send_ref[...] = all_ref[pl.ds(pl.multiple_of((1 - core) * half, 16), half), :]


def weight_terms(turned, near, away, dense, scaling):
    channels = turned.shape[0]
    half = jax.ShapeDtypeStruct((KOFF * channels // 2, channels), F32)
    return call(
        functools.partial(weight_body, scaling),
        [half, half],
        [turned, near, away, dense],
        scratch=[
            pltpu.VMEM((3, NX + 2, SHIFTED, channels), BF),
            pltpu.VMEM((KOFF * channels, channels), F32),
        ],
        flops=2 * DENSE * KOFF * channels * channels,
    )


def split_body(keep_ref, got_ref, own_ref, *sent_refs):
    rows = own_ref.shape[0]
    size = 1 + len(sent_refs)
    side = lax.rem(lax.axis_index("region") // 2, size)
    for i in range(size):
        part = pl.ds(pl.multiple_of((side ^ i) * rows, 16), rows)
        total = keep_ref[part, :] + got_ref[part, :]
        if i == 0:
            own_ref[...] = total
        else:
            sent_refs[i - 1][...] = total.astype(BF)


def split(keep, got, size):
    rows, channels = keep.shape[0] // size, keep.shape[1]
    return call(
        split_body,
        [jax.ShapeDtypeStruct((rows, channels), F32)]
        + [jax.ShapeDtypeStruct((rows, channels), BF)] * (size - 1),
        [keep, got],
    )


def unpack_body(place_ref, rows_ref, out_ref):
    regions, cap_rows, channels = rows_ref.shape
    points = out_ref.shape[0]
    total = regions * cap_rows
    place = jnp.transpose(place_ref[...])[:, 0:1].astype(jnp.int32)
    block = jnp.broadcast_to((place >> 7).astype(F32), (points, LANES)).astype(BF)
    within = jnp.broadcast_to((place & (LANES - 1)).astype(F32), (points, LANES)).astype(BF)
    lane = iota((points, LANES), 1, F32).astype(BF)
    one = jnp.where(lane == within, jnp.ones_like(lane), jnp.zeros_like(lane))
    rows = rows_ref[...].reshape(total, channels)
    chunk = 256
    for start in range(0, points, chunk):
        keep = slice(start, start + chunk)
        picks = [
            jnp.where(block[keep] == jnp.asarray(q, BF), one[keep], jnp.zeros_like(one[keep]))
            for q in range(total // LANES)
        ]
        picker = jnp.concatenate(picks, axis=1)
        out_ref[keep, :] = jnp.dot(picker, rows, preferred_element_type=F32).astype(BF)


def unpack(place, rows, points):
    regions, cap_rows, channels = rows.shape
    return call(
        unpack_body,
        [jax.ShapeDtypeStruct((points, channels), BF)],
        [place, rows],
        flops=2 * regions * cap_rows * points * channels,
    )[0]


def from_sides(near, away):
    count = lax.axis_size("region")
    pairs = [(i, i + 1) for i in range(1, count - 1, 2)]
    return swapped(near, 1), lax.ppermute(away, "region", pairs + [(j, i) for i, j in pairs])


def swapped(array, bit):
    count = lax.axis_size("region")
    return lax.ppermute(array, "region", [(i, i ^ bit) for i in range(count)])


def in_order(pieces, side):
    return jnp.concatenate(
        [lax.select_n(side ^ q, *pieces) for q in range(len(pieces))], axis=0
    )


def reduce_group(term, bit, size):
    side = (lax.axis_index("region") // bit) % size
    rows = term.shape[0] // size
    parts = [lax.dynamic_slice_in_dim(term, (side ^ i) * rows, rows) for i in range(size)]
    return sum_group(parts[0], [part.astype(BF) for part in parts[1:]], bit)


def exchange_group(term, bit, size, beside):
    side = (lax.axis_index("region") // bit) % size
    term, beside = lax.optimization_barrier((term.astype(BF), beside))
    terms = gather_group(term, bit, size)
    total = lax.select_n(side, *terms).astype(F32)
    for q in range(1, size):
        total = total + lax.select_n(side ^ q, *terms).astype(F32)
    return total.astype(BF), beside


def sum_group(total, sent, bit):
    for i, part in enumerate(sent):
        total = total + swapped(part, bit * (i + 1)).astype(F32)
    return total


def gather_group(term, bit, size):
    return [term] + [swapped(term, bit * i) for i in range(1, size)]


def groups_of(count):
    found, bit = [], 2
    while bit < count:
        size = min(4, count // bit)
        found.append((bit, size))
        bit *= size
    return found


def last_body(size, places, *refs):
    out_far, wide_ref, sems = refs[-3:]
    rows = refs[0].shape[0]
    core = this_core()
    side = lax.rem(lax.axis_index("region") // 2, size)
    copies = []
    for n, (other, i) in enumerate(places):
        wide_ref[n] = refs[n][...].astype(F32)
        half = 1 - core if other else core
        at = pl.multiple_of((half * size + (side ^ i)) * rows, 16)
        copies += start_all([(wide_ref.at[n], out_far.at[pl.ds(at, rows)])], sems.at[n : n + 1])
    for copy in copies:
        copy.wait()


def last_step(size, places, pieces, out=None):
    count, (rows, channels) = len(pieces), pieces[0].shape
    again = out is not None
    return pl.pallas_call(
        functools.partial(last_body, size, places),
        out_shape=jax.ShapeDtypeStruct((2 * size * rows, channels), F32),
        in_specs=[VMEM] * count + [FAR] * again,
        out_specs=FAR,
        scratch_shapes=[
            pltpu.VMEM((count, rows, channels), F32),
            pltpu.SemaphoreType.DMA((count,)),
        ],
        input_output_aliases={count: 0} if again else {},
        compiler_params=pltpu.CompilerParams(vmem_limit_bytes=16 * MIB),
        cost_estimate=pl.CostEstimate(
            flops=0, bytes_accessed=6 * count * rows * channels, transcendentals=0
        ),
    )(*pieces, *([out] if again else []))


def exchange(array):
    return lax.all_to_all(array, "region", split_axis=0, concat_axis=0, tiled=True)


def local(point_feats, point_owner, point_slot, adjacency, kernel, cotangent):
    regions = lax.axis_size("region")
    points, channels = point_feats.shape
    tiles, vox = cotangent.shape[0], cotangent.shape[1]
    capacity = (5 * points + 2 * regions - 1) // (2 * regions)
    cap_rows = up_to(capacity, 16)
    msg, place = pack(
        point_owner.reshape(1, points), point_slot.reshape(1, points), point_feats, regions, cap_rows
    )
    received = exchange(msg)
    cot, cot_near, cot_away = to_dense(adjacency, cotangent)
    near, away = from_sides(cot_near, cot_away)
    mirrored = jnp.transpose(kernel[::-1], (0, 2, 1)).reshape(KOFF * channels, channels)
    grad = inner_gradient(cot, mirrored)
    edge_grad = edge_gradient(cot, near, away, mirrored)
    scaling = 1.0 / math.sqrt(tiles * regions * vox)
    turned, feats_near, feats_away, back = voxels(adjacency, received, grad, edge_grad, cap_rows)
    returned = exchange(back)
    keep, send = weight_terms(turned, near, away, cot, scaling)
    groups = groups_of(regions)
    bit, size = groups[0]
    term, *sent = split(keep, swapped(send, 1), size)
    weights = kernel.reshape(KOFF * channels, channels)
    turned, feats_near, feats_away, *sent = lax.optimization_barrier(
        (turned, feats_near, feats_away, *sent)
    )
    feats_near, feats_away = from_sides(feats_near, feats_away)
    inner = inner_forward(turned, weights)
    got = [swapped(part, bit * (i + 1)) for i, part in enumerate(sent)]
    got, returned, inner, feats_near, feats_away = lax.optimization_barrier(
        (got, returned, inner, feats_near, feats_away)
    )
    for part in got:
        term = term + part.astype(F32)
    for bit, size in groups[1:-1]:
        term = reduce_group(term, bit, size)
    bit, size = groups[-1]
    term, (returned, feats_near, feats_away) = exchange_group(
        term, bit, size, (returned, feats_near, feats_away)
    )
    grad_points = unpack(place, returned, points)
    out_tiles = edge_forward(adjacency, turned, feats_near, feats_away, weights, inner, tiles)
    for bit, size in groups[-2:0:-1]:
        side = (lax.axis_index("region") // bit) % size
        term = in_order(gather_group(term, bit, size), side)
    term, grad_points, out_tiles = lax.optimization_barrier((term, grad_points, out_tiles))
    bit, size = groups[0]
    own = gather_group(term, bit, size)
    others = [swapped(piece, 1) for piece in own]
    first = [(False, i) for i in range(size)] + [(True, 0)]
    summed = last_step(size, first, own + others[:1])
    summed = last_step(size, [(True, i) for i in range(1, size)], others[1:], summed)
    grad_weight = summed.reshape(KOFF, channels, channels)
    return out_tiles, grad_points, grad_weight


def solution(mesh):
    placed = (
        P(("groups", "region"), None),
        P(("groups", "region"), None),
        P(("groups", "region")),
        P(("groups", "region"), None),
        P(),
        P(("groups", "region"), None, None),
    )
    return jax.shard_map(
        local,
        mesh=mesh,
        in_specs=placed,
        out_specs=(
            P(("groups", "region"), None, None),
            P(("groups", "region"), None),
            P("groups", None, None),
        ),
        check_vma=False,
    )
```
